32 devices in a mesh: groups: 2 (over y), dp: 4 (over z), mp: 2 (over x), sub: 2 (over core).
Axes of the slice: x: 2, y: 2, z: 4, core: 2. Of those that a mesh axis runs over, the one named last changes fastest.
Arguments:
- hidden: bfloat16 [4096, 14336], P(('groups', 'dp', 'sub'), 'mp'), parts along dimension 0, may hold values from -6 to 6
- out_grad: bfloat16 [4096, 4096], P(('groups', 'dp', 'sub'), 'mp'), parts along dimension 0, may hold values from -80 to 80
- lengths: int32 [64], P(('groups', 'dp', 'sub')), parts along dimension 0, may hold values from 16 to 64
- proj_in: bfloat16 [14336, 32], P('mp'), may hold values from -0.005859375 to 0.005859375
- proj_out: bfloat16 [4096, 32], P('mp'), may hold values from -0.09375 to 0.09375
- test_proj: bfloat16 [2048, 1024], P(('mp', 'sub')), may hold values from -6 to 6
Outputs:
- covariance: float32 [2048, 1024], P(('groups', 'dp', 'sub')), parts along dimension 0
- scores: float32 [64, 2048], P(('groups', 'dp', 'sub'), 'mp'), parts along dimension 0
The draws below stay inside these ranges and needn't reach their ends.
There are 2 independent parts, one for each index of `groups`. The reference program is written for one: setup_inputs(seed, part) draws one part's arguments, and reference() takes and returns one part's arrays. A program takes and returns all parts, laid end to end along the dimension named above; an argument that names none is the same for every part. Nothing has to cross between parts.
All inputs are finite; a program needn't handle non-finite values.
Results may differ from the reference program's by a relative error of at most 0.004.
Values may be sent and summed in bfloat16 or wider, within the bound.
No kernel may reach another device: no remote copies, remote signals or barrier semaphores. Data moves between devices by JAX's collectives and lax.ppermute only.
A program may use at most 64 MiB of HBM per device.

```python
import jax
import jax.numpy as jnp
from jax import lax

D = 4096
FF = 14336
K_IN = 32
K_OUT = 32
SEQ = 64
PROJ = 1024
EXAMPLES = 32
TOKENS = 2048
TESTS = 2048


def draw_out_grad(key, part):
    key = jax.random.fold_in(key, 11)
    first, second = jax.random.split(key, 2)
    ramp = 3.0 ** (jnp.arange(EXAMPLES, dtype=jnp.float32) / max(EXAMPLES - 1, 1))
    base = jnp.clip(jax.random.normal(first, (EXAMPLES * SEQ, D), jnp.float32), -6.0, 6.0)
    spread = jnp.exp(jax.random.uniform(second, (EXAMPLES,), jnp.float32, -1.15, 1.15))
    factor = jnp.repeat(spread * ramp, SEQ, total_repeat_length=EXAMPLES * SEQ)
    return (base * factor[:, None]).astype(jnp.bfloat16)


def draw_lengths(key, part):
    key = jax.random.fold_in(key, 23)
    drawn = jax.random.randint(key, (EXAMPLES,), SEQ // 4, SEQ + 1, dtype=jnp.int32)
    return drawn.at[0].set(SEQ).at[1].set(SEQ // 4)


def shard_levels(rng, dims, cuts, least, high):
    def one(dim, parts):
        draws = jax.random.uniform(jax.random.fold_in(jax.random.fold_in(rng, 6), dim), (parts,), jnp.float32, least / len(cuts), high / len(cuts))
        return jnp.repeat(jnp.exp(draws), dims[dim] // parts).reshape((-1,) + (1,) * (len(dims) - dim - 1))

    gain = one(*cuts[0])
    for cut in cuts[1:]:
        gain = gain * one(*cut)
    return gain


def normal_values(stream_key, shape, deviation, limit, cuts=(), kind=jnp.bfloat16):
    entries = deviation * jax.random.normal(stream_key, shape, jnp.float32)
    if cuts:
        entries = entries * shard_levels(stream_key, shape, cuts, -0.22, 0.18)
    return jnp.clip(entries, -limit, limit).astype(kind)


def setup_inputs(seed: int = 0, part: int = 0) -> dict:
    streams_of = jax.random.split(jax.random.key(seed), 7)
    part_splits = jax.random.split(jax.random.fold_in(streams_of[6], part), 7)
    return {
        "hidden": normal_values(part_splits[0], (TOKENS, FF), 1.0, 6.0, ((0, 8), (1, 2))),
        "out_grad": draw_out_grad(jax.random.fold_in(jax.random.fold_in(streams_of[6], part), 71), part),
        "lengths": draw_lengths(jax.random.fold_in(jax.random.fold_in(streams_of[6], part), 71), part),
        "proj_in": normal_values(streams_of[3], (FF, K_IN), (FF * SEQ) ** -0.5, 0.005859375, ((0, 2),)),
        "proj_out": normal_values(streams_of[4], (D, K_OUT), D ** -0.5, 0.09375, ((0, 2),)),
        "test_proj": normal_values(streams_of[5], (TESTS, PROJ), 1.0, 6.0, ((0, 4),)),
    }


def reference(hidden, out_grad, lengths, proj_in, proj_out, test_proj):
    slots = jnp.arange(EXAMPLES * SEQ, dtype=jnp.int32) % SEQ
    limits = jnp.repeat(lengths, SEQ, total_repeat_length=EXAMPLES * SEQ)
    mask = (slots < limits).astype(jnp.float32)
    act_proj = jnp.dot(hidden, proj_in, preferred_element_type=jnp.float32) * mask[:, None]
    grad_proj = jnp.dot(out_grad, proj_out, preferred_element_type=jnp.float32)
    grads = jnp.einsum('eti,etj->eij', act_proj.reshape(EXAMPLES, SEQ, K_IN), grad_proj.reshape(EXAMPLES, SEQ, K_OUT), precision=lax.Precision.HIGHEST)
    grads = grads.reshape(EXAMPLES, K_IN * K_OUT).astype(jnp.bfloat16)
    covariance = jnp.dot(grads.T, grads, preferred_element_type=jnp.float32) / EXAMPLES
    wide = grads.astype(jnp.float32)
    total = jnp.sum(wide * wide)
    scores = jnp.dot(grads, test_proj.T, preferred_element_type=jnp.float32) * lax.rsqrt(total / EXAMPLES + 1e-06)
    return (covariance, scores)
```

```python
import jax
import jax.numpy as jnp
from jax import lax
from jax.sharding import PartitionSpec as P

SEQ = 64


def gather_all(block, axes):
    n = lax.axis_size(axes)
    if n > 8:
        return lax.all_gather(block, axes)
    me = lax.axis_index(axes)
    got = [block]
    for step in range(1, n):
        got.append(lax.ppermute(block, axes, [(i, (i + step) % n) for i in range(n)]))
    stacked = jnp.stack(got)
    order = (me - jnp.arange(n)) % n
    return jnp.take(stacked, order, axis=0, mode="clip")


def sum_over(part, axis):
    n = lax.axis_size(axis)
    if n == 2:
        return part + lax.ppermute(part, axis, [(0, 1), (1, 0)])
    return lax.psum(part, axis)


def per_device(hidden, out_grad, lengths, proj_in, proj_out, test_proj):
    rows = hidden.shape[0]
    count = lengths.shape[0]
    width_in = proj_in.shape[1]
    width_out = proj_out.shape[1]
    flat = width_in * width_out
    sharers = lax.axis_size(("dp", "sub"))
    examples_all = count * sharers
    n_sub = lax.axis_size("sub")
    mask = (jnp.arange(SEQ, dtype=jnp.int32)[None, :] < lengths[:, None]).astype(jnp.float32)

    if n_sub == 2:
        other = lax.ppermute(test_proj, "sub", [(0, 1), (1, 0)])
    part_in = jnp.dot(hidden, proj_in, preferred_element_type=jnp.float32)
    part_out = jnp.dot(out_grad, proj_out, preferred_element_type=jnp.float32)
    both = sum_over(jnp.concatenate([part_in, part_out], axis=1), "mp")
    both = both.reshape(count, SEQ, width_in + width_out)
    act_proj = both[:, :, :width_in] * mask[:, :, None]
    grad_proj = both[:, :, width_in:]
    grads = jnp.einsum("eti,etj->eij", act_proj, grad_proj, precision=lax.Precision.HIGHEST)
    grads = grads.reshape(count, flat).astype(jnp.bfloat16)

    every = gather_all(grads, ("dp", "sub")).reshape(examples_all, flat)
    own_rows = flat // sharers
    mine = lax.dynamic_slice_in_dim(every, lax.axis_index(("dp", "sub")) * own_rows, own_rows, axis=1)
    covariance = jnp.einsum("ek,el->kl", mine, every, preferred_element_type=jnp.float32) / examples_all
    wide = every.astype(jnp.float32)
    total = jnp.sum(wide * wide)
    factor = lax.rsqrt(total / examples_all + 1e-06)
    if n_sub == 2:
        near = jnp.einsum("ep,qp->eq", grads, test_proj, preferred_element_type=jnp.float32)
        far = jnp.einsum("ep,qp->eq", grads, other, preferred_element_type=jnp.float32)
        first = lax.axis_index("sub") == 0
        scores = jnp.concatenate([jnp.where(first, near, far), jnp.where(first, far, near)], axis=1)
    else:
        tests = lax.all_gather(test_proj, "sub", axis=0, tiled=True)
        scores = jnp.einsum("ep,qp->eq", grads, tests, preferred_element_type=jnp.float32)
    return (covariance, scores * factor)


def solution(mesh):
    in_specs = (
        P(("groups", "dp", "sub"), "mp"),
        P(("groups", "dp", "sub"), "mp"),
        P(("groups", "dp", "sub")),
        P("mp", None),
        P("mp", None),
        P(("mp", "sub"), None),
    )
    out_specs = (P(("groups", "dp", "sub"), None), P(("groups", "dp", "sub"), "mp"))
    return jax.shard_map(
        per_device, mesh=mesh, in_specs=in_specs, out_specs=out_specs, check_vma=False
    )
```

```python
import jax
import jax.numpy as jnp
from jax import lax
from jax.sharding import PartitionSpec as P

SEQ = 64


def gather_all(block, axes):
    n = lax.axis_size(axes)
    if n > 8:
        return lax.all_gather(block, axes)
    return lax.all_to_all(jnp.broadcast_to(block, (n, *block.shape)), axes, 0, 0)


def sum_over(part, axis):
    n = lax.axis_size(axis)
    if n == 2:
        return part + lax.ppermute(part, axis, [(0, 1), (1, 0)])
    return lax.psum(part, axis)


def per_device(hidden, out_grad, lengths, proj_in, proj_out, test_proj):
    rows = hidden.shape[0]
    count = lengths.shape[0]
    width_in = proj_in.shape[1]
    width_out = proj_out.shape[1]
    flat = width_in * width_out
    sharers = lax.axis_size(("dp", "sub"))
    examples_all = count * sharers
    n_sub = lax.axis_size("sub")
    mask = (jnp.arange(SEQ, dtype=jnp.int32)[None, :] < lengths[:, None]).astype(jnp.float32)

    if n_sub == 2:
        other = lax.ppermute(test_proj, "sub", [(0, 1), (1, 0)])
    part_in = jnp.dot(hidden, proj_in, preferred_element_type=jnp.float32)
    part_out = jnp.dot(out_grad, proj_out, preferred_element_type=jnp.float32)
    both = sum_over(jnp.concatenate([part_in, part_out], axis=1), "mp")
    both = both.reshape(count, SEQ, width_in + width_out)
    act_proj = both[:, :, :width_in] * mask[:, :, None]
    grad_proj = both[:, :, width_in:]
    grads = jnp.einsum("eti,etj->eij", act_proj, grad_proj, precision=lax.Precision.HIGHEST)
    grads = grads.reshape(count, flat).astype(jnp.bfloat16)

    every = gather_all(grads, ("dp", "sub")).reshape(examples_all, flat)
    own_rows = flat // sharers
    mine = lax.dynamic_slice_in_dim(every, lax.axis_index(("dp", "sub")) * own_rows, own_rows, axis=1)
    covariance = jnp.einsum("ek,el->kl", mine, every, preferred_element_type=jnp.float32) / examples_all
    wide = every.astype(jnp.float32)
    total = jnp.sum(wide * wide)
    factor = lax.rsqrt(total / examples_all + 1e-06)
    if n_sub == 2:
        near = jnp.einsum("ep,qp->eq", grads, test_proj, preferred_element_type=jnp.float32)
        far = jnp.einsum("ep,qp->eq", grads, other, preferred_element_type=jnp.float32)
        first = lax.axis_index("sub") == 0
        scores = jnp.concatenate([jnp.where(first, near, far), jnp.where(first, far, near)], axis=1)
    else:
        tests = lax.all_gather(test_proj, "sub", axis=0, tiled=True)
        scores = jnp.einsum("ep,qp->eq", grads, tests, preferred_element_type=jnp.float32)
    return (covariance, scores * factor)


def solution(mesh):
    in_specs = (
        P(("groups", "dp", "sub"), "mp"),
        P(("groups", "dp", "sub"), "mp"),
        P(("groups", "dp", "sub")),
        P("mp", None),
        P("mp", None),
        P(("mp", "sub"), None),
    )
    out_specs = (P(("groups", "dp", "sub"), None), P(("groups", "dp", "sub"), "mp"))
    return jax.shard_map(
        per_device, mesh=mesh, in_specs=in_specs, out_specs=out_specs, check_vma=False
    )
```

```python
import functools

import jax
import jax.numpy as jnp
from jax import lax
from jax.experimental import pallas as pl
from jax.experimental.pallas import tpu as pltpu
from jax.sharding import PartitionSpec as P

SEQ = 64
CHUNK = 1024
CONTRACT_LAST = (((1,), (1,)), ((), ()))
CONTRACT_FIRST = (((0,), (0,)), ((), ()))


def chunks_of(width):
    return [(at, min(CHUNK, width - at)) for at in range(0, width, CHUNK)]


def project_kernel(hidden, out_grad, proj_in, proj_out, out, hid, og, pin, pout, sems):
    jobs = []
    for src, src_w, dst, dst_w in ((out_grad, proj_out, og, pout), (hidden, proj_in, hid, pin)):
        for at, size in chunks_of(src.shape[1]):
            jobs.append((src.at[:, pl.ds(at, size)], dst.at[:, pl.ds(at, size)],
                         src_w.at[:, pl.ds(at, size)], dst_w.at[:, pl.ds(at, size)]))
    copies = []
    for n, (src, dst, src_w, dst_w) in enumerate(jobs):
        pair = (pltpu.make_async_copy(src_w, dst_w, sems.at[1, n]), pltpu.make_async_copy(src, dst, sems.at[0, n]))
        for copy in pair:
            copy.start()
        copies.append(pair)
    first = len(chunks_of(out_grad.shape[1]))
    sums = [None, None]
    for n, (_, dst, _, dst_w) in enumerate(jobs):
        for copy in copies[n]:
            copy.wait()
        part = lax.dot_general(dst[...], dst_w[...], CONTRACT_LAST, preferred_element_type=jnp.float32)
        which = 0 if n >= first else 1
        sums[which] = part if sums[which] is None else sums[which] + part
    out[...] = jnp.concatenate(sums, axis=1).T


def project(hidden, out_grad, proj_in, proj_out):
    rows, width = hidden.shape
    narrow = out_grad.shape[1]
    k_in, k_out = proj_in.shape[1], proj_out.shape[1]
    jobs = len(chunks_of(width)) + len(chunks_of(narrow))
    return pl.pallas_call(
        project_kernel,
        out_shape=jax.ShapeDtypeStruct((k_in + k_out, rows), jnp.float32),
        in_specs=[pl.BlockSpec(memory_space=pl.ANY)] * 4,
        out_specs=pl.BlockSpec(memory_space=pltpu.VMEM),
        scratch_shapes=[
            pltpu.VMEM((rows, width), jnp.bfloat16),
            pltpu.VMEM((rows, narrow), jnp.bfloat16),
            pltpu.VMEM((k_in, width), jnp.bfloat16),
            pltpu.VMEM((k_out, narrow), jnp.bfloat16),
            pltpu.SemaphoreType.DMA((2, jobs)),
        ],
        compiler_params=pltpu.CompilerParams(vmem_limit_bytes=24 << 20),
    )(hidden, out_grad, proj_in.T, proj_out.T)


def grads_kernel(k_in, lengths, *refs):
    *pieces, out = refs
    both = pieces[0][...]
    for piece in pieces[1:]:
        both = both + piece[...]
    count = lengths.shape[0]
    rows = both.shape[1]
    slot = lax.broadcasted_iota(jnp.int32, (1, rows), 1)
    limit = jnp.full((1, rows), 0, jnp.int32)
    for e in range(count):
        limit = jnp.where((slot >= e * SEQ) & (slot < (e + 1) * SEQ), e * SEQ + lengths[e], limit)
    act = jnp.where(slot < limit, both[:k_in], 0.0)
    grad = both[k_in:]
    row = lax.broadcasted_iota(jnp.int32, (16, rows), 0)
    col = lax.broadcasted_iota(jnp.int32, (16, rows), 1)
    pick = jnp.where((col >= row * SEQ) & (col < (row + 1) * SEQ), 1.0, 0.0).astype(jnp.bfloat16)
    per = 8
    k_out = grad.shape[0]
    for at in range(0, k_in, per):
        rest = jnp.concatenate([act[i:i + 1] * grad for i in range(at, at + per)], axis=0)
        total = None
        for _ in range(3):
            high = rest.astype(jnp.bfloat16)
            rest = rest - high.astype(jnp.float32)
            part = lax.dot_general(pick, high, CONTRACT_LAST, preferred_element_type=jnp.float32)
            total = part if total is None else total + part
        out[:, at * k_out:(at + per) * k_out] = total[:count].astype(jnp.bfloat16)


def example_grads(lengths, pieces, k_in, k_out):
    return pl.pallas_call(
        functools.partial(grads_kernel, k_in),
        out_shape=jax.ShapeDtypeStruct((lengths.shape[0], k_in * k_out), jnp.bfloat16),
        in_specs=[pl.BlockSpec(memory_space=pltpu.SMEM)] + [pl.BlockSpec(memory_space=pltpu.VMEM)] * len(pieces),
        out_specs=pl.BlockSpec(memory_space=pltpu.VMEM),
    )(lengths, *pieces)


def finish_kernel(examples, n_pieces, n_raw, place, *refs):
    pieces, mine = refs[:n_pieces], refs[n_pieces:2 * n_pieces]
    raw = refs[2 * n_pieces:2 * n_pieces + n_raw]
    cov, scores = refs[2 * n_pieces + n_raw:]
    every = jnp.concatenate([p[...] for p in pieces], axis=0)
    own = jnp.concatenate([p[...] for p in mine], axis=0)
    wide = every.astype(jnp.float32)
    factor = lax.rsqrt(jnp.sum(wide * wide) / examples + 1e-06)
    if n_raw == 2:
        near, far = raw[0][...], raw[1][...]
        first = place[0] == 0
        half = near.shape[1]
        scores[:, :half] = jnp.where(first, near, far) * factor
        scores[:, half:] = jnp.where(first, far, near) * factor
    else:
        scores[...] = raw[0][...] * factor
    cov[...] = lax.dot_general(own, every, CONTRACT_FIRST, preferred_element_type=jnp.float32) * (1.0 / examples)


def finish(place, examples, pieces, mine, raw):
    flat = pieces[0].shape[1]
    vmem = pl.BlockSpec(memory_space=pltpu.VMEM)
    return pl.pallas_call(
        functools.partial(finish_kernel, examples, len(pieces), len(raw)),
        out_shape=(
            jax.ShapeDtypeStruct((mine[0].shape[1], flat), jnp.float32),
            jax.ShapeDtypeStruct((raw[0].shape[0], sum(r.shape[1] for r in raw)), jnp.float32),
        ),
        in_specs=[pl.BlockSpec(memory_space=pltpu.SMEM)] + [vmem] * (2 * len(pieces) + len(raw)),
        out_specs=(vmem, vmem),
    )(place, *pieces, *mine, *raw)


def per_device(hidden, out_grad, lengths, proj_in, proj_out, test_proj):
    k_in, k_out = proj_in.shape[1], proj_out.shape[1]
    flat = k_in * k_out
    group = ("dp", "sub")
    sharers = lax.axis_size(group)
    examples = lengths.shape[0] * sharers
    n_sub = lax.axis_size("sub")

    both = project(hidden, out_grad, proj_in, proj_out)
    if lax.axis_size("mp") == 2:
        pieces = [both, lax.ppermute(both, "mp", [(0, 1), (1, 0)])]
    else:
        pieces = [lax.psum(both, "mp")]
    grads = example_grads(lengths, pieces, k_in, k_out)

    if n_sub == 2:
        other = lax.ppermute(test_proj, "sub", [(0, 1), (1, 0)])
        tests = [test_proj, other]
    else:
        tests = [lax.all_gather(test_proj, "sub", axis=0, tiled=True)]
    raw = [jnp.einsum("ep,qp->eq", grads, t, preferred_element_type=jnp.float32) for t in tests]

    if sharers in (2, 4, 8):
        held = grads
        step = sharers // 2
        while True:
            came = lax.ppermute(held, group, [(i, i ^ step) for i in range(sharers)])
            if step == 1:
                break
            held = jnp.concatenate([held, came], axis=0)
            step //= 2
        gathered = [held, came]
    else:
        gathered = [lax.all_gather(grads, group, axis=0, tiled=True)]
    own_rows = flat // sharers
    at = lax.axis_index(group) * own_rows
    mine = [lax.dynamic_slice_in_dim(g, at, own_rows, axis=1) for g in gathered]
    place = lax.axis_index("sub").astype(jnp.int32).reshape(1)
    return finish(place, examples, gathered, mine, raw)


def solution(mesh):
    in_specs = (
        P(("groups", "dp", "sub"), "mp"),
        P(("groups", "dp", "sub"), "mp"),
        P(("groups", "dp", "sub")),
        P("mp", None),
        P("mp", None),
        P(("mp", "sub"), None),
    )
    out_specs = (P(("groups", "dp", "sub"), None), P(("groups", "dp", "sub"), "mp"))
    return jax.shard_map(
        per_device, mesh=mesh, in_specs=in_specs, out_specs=out_specs, check_vma=False
    )
```

```python
import functools

import jax
import jax.numpy as jnp
from jax import lax
from jax.experimental import pallas as pl
from jax.experimental.pallas import tpu as pltpu
from jax.sharding import PartitionSpec as P

SEQ = 64
CHUNK = 1024
CONTRACT_LAST = (((1,), (1,)), ((), ()))
CONTRACT_FIRST = (((0,), (0,)), ((), ()))


def chunks_of(width):
    return [(at, min(CHUNK, width - at)) for at in range(0, width, CHUNK)]


def project_kernel(hidden, out_grad, proj_in, proj_out, out, hid, og, pin, pout, sems):
    jobs = []
    for src, src_w, dst, dst_w in ((out_grad, proj_out, og, pout), (hidden, proj_in, hid, pin)):
        for at, size in chunks_of(src.shape[1]):
            jobs.append((src.at[:, pl.ds(at, size)], dst.at[:, pl.ds(at, size)],
                         src_w.at[:, pl.ds(at, size)], dst_w.at[:, pl.ds(at, size)]))
    copies = []
    for n, (src, dst, src_w, dst_w) in enumerate(jobs):
        pair = (pltpu.make_async_copy(src_w, dst_w, sems.at[1, n]), pltpu.make_async_copy(src, dst, sems.at[0, n]))
        for copy in pair:
            copy.start()
        copies.append(pair)
    first = len(chunks_of(out_grad.shape[1]))
    sums = [None, None]
    for n, (_, dst, _, dst_w) in enumerate(jobs):
        for copy in copies[n]:
            copy.wait()
        part = lax.dot_general(dst[...], dst_w[...], CONTRACT_LAST, preferred_element_type=jnp.float32)
        which = 0 if n >= first else 1
        sums[which] = part if sums[which] is None else sums[which] + part
    out[...] = jnp.concatenate(sums, axis=1).T


def project(hidden, out_grad, proj_in, proj_out):
    rows, width = hidden.shape
    narrow = out_grad.shape[1]
    k_in, k_out = proj_in.shape[1], proj_out.shape[1]
    jobs = len(chunks_of(width)) + len(chunks_of(narrow))
    return pl.pallas_call(
        project_kernel,
        out_shape=jax.ShapeDtypeStruct((k_in + k_out, rows), jnp.float32),
        in_specs=[pl.BlockSpec(memory_space=pltpu.HBM)] * 4,
        out_specs=pl.BlockSpec(memory_space=pltpu.VMEM),
        scratch_shapes=[
            pltpu.VMEM((rows, width), jnp.bfloat16),
            pltpu.VMEM((rows, narrow), jnp.bfloat16),
            pltpu.VMEM((k_in, width), jnp.bfloat16),
            pltpu.VMEM((k_out, narrow), jnp.bfloat16),
            pltpu.SemaphoreType.DMA((2, jobs)),
        ],
        compiler_params=pltpu.CompilerParams(vmem_limit_bytes=24 << 20),
    )(*(pltpu.with_memory_space_constraint(x, pltpu.HBM) for x in (hidden, out_grad, proj_in.T, proj_out.T)))


def grads_kernel(k_in, mask, *refs):
    *pieces, out = refs
    both = pieces[0][...]
    for piece in pieces[1:]:
        both = both + piece[...]
    rows = both.shape[1]
    act = both[:k_in] * mask[...]
    grad = both[k_in:]
    row = lax.broadcasted_iota(jnp.int32, (16, rows), 0)
    col = lax.broadcasted_iota(jnp.int32, (16, rows), 1)
    pick = jnp.where((col >= row * SEQ) & (col < (row + 1) * SEQ), 1.0, 0.0).astype(jnp.bfloat16)
    per = 8
    k_out = grad.shape[0]
    for at in range(0, k_in, per):
        rest = jnp.concatenate([act[i:i + 1] * grad for i in range(at, at + per)], axis=0)
        total = None
        for _ in range(3):
            high = rest.astype(jnp.bfloat16)
            rest = rest - high.astype(jnp.float32)
            part = lax.dot_general(pick, high, CONTRACT_LAST, preferred_element_type=jnp.float32)
            total = part if total is None else total + part
        out[:, at * k_out:(at + per) * k_out] = total[:out.shape[0]].astype(jnp.bfloat16)


def example_grads(mask, pieces, k_in, k_out):
    vmem = pl.BlockSpec(memory_space=pltpu.VMEM)
    return pl.pallas_call(
        functools.partial(grads_kernel, k_in),
        out_shape=jax.ShapeDtypeStruct((mask.shape[1] // SEQ, k_in * k_out), jnp.bfloat16),
        in_specs=[vmem] * (1 + len(pieces)),
        out_specs=vmem,
        compiler_params=pltpu.CompilerParams(vmem_limit_bytes=6 << 20),
    )(mask, *pieces)


def finish_kernel(examples, n_pieces, n_raw, *refs):
    pieces, raw = refs[:n_pieces], refs[n_pieces:n_pieces + n_raw]
    cov, scores = refs[n_pieces + n_raw:]
    own_rows = cov.shape[0]
    place = lax.axis_index(("dp", "sub"))
    every = jnp.concatenate([p[...] for p in pieces], axis=0)
    if own_rows % 128 == 0:
        at = pl.multiple_of(place * own_rows, own_rows)
        own = jnp.concatenate([p[:, pl.ds(at, own_rows)] for p in pieces], axis=0)
    else:
        at = pl.multiple_of((place * own_rows) // 128 * 128, 128)
        wider = jnp.concatenate([p[:, pl.ds(at, 128)] for p in pieces], axis=0)
        own = pltpu.roll(wider.astype(jnp.float32), at - place * own_rows + 128, 1)[:, :own_rows].astype(jnp.bfloat16)
    wide = every.astype(jnp.float32)
    factor = lax.rsqrt(jnp.sum(wide * wide) / examples + 1e-06)
    if n_raw == 2:
        near, far = raw[0][...], raw[1][...]
        first = lax.axis_index("sub") == 0
        half = near.shape[1]
        scores[:, :half] = jnp.where(first, near, far) * factor
        scores[:, half:] = jnp.where(first, far, near) * factor
    else:
        scores[...] = raw[0][...] * factor
    cov[...] = lax.dot_general(own, every, CONTRACT_FIRST, preferred_element_type=jnp.float32) * (1.0 / examples)


def finish(examples, own_rows, pieces, raw):
    flat = pieces[0].shape[1]
    vmem = pl.BlockSpec(memory_space=pltpu.VMEM)
    return pl.pallas_call(
        functools.partial(finish_kernel, examples, len(pieces), len(raw)),
        out_shape=(
            jax.ShapeDtypeStruct((own_rows, flat), jnp.float32),
            jax.ShapeDtypeStruct((raw[0].shape[0], sum(r.shape[1] for r in raw)), jnp.float32),
        ),
        in_specs=[vmem] * (len(pieces) + len(raw)),
        out_specs=(vmem, vmem),
        compiler_params=pltpu.CompilerParams(vmem_limit_bytes=8 << 20),
    )(*pieces, *raw)


def per_device(hidden, out_grad, lengths, proj_in, proj_out, test_proj):
    k_in, k_out = proj_in.shape[1], proj_out.shape[1]
    flat = k_in * k_out
    rows = hidden.shape[0]
    group = ("dp", "sub")
    sharers = lax.axis_size(group)
    examples = lengths.shape[0] * sharers
    n_sub = lax.axis_size("sub")

    both = project(hidden, out_grad, proj_in, proj_out)
    if lax.axis_size("mp") == 2:
        pieces = [both, lax.ppermute(both, "mp", [(0, 1), (1, 0)])]
    else:
        pieces = [lax.psum(both, "mp")]
    lengths, test_proj, _ = lax.optimization_barrier((lengths, test_proj, both))
    slots = jnp.arange(SEQ, dtype=jnp.int32)
    mask = (slots[None, :] < lengths[:, None]).astype(jnp.float32).reshape(1, rows)
    grads = example_grads(mask, pieces, k_in, k_out)

    if n_sub == 2:
        other = lax.ppermute(test_proj, "sub", [(0, 1), (1, 0)])
        tests = [test_proj, other]
    else:
        tests = [lax.all_gather(test_proj, "sub", axis=0, tiled=True)]
    raw = [jnp.einsum("ep,qp->eq", grads, t, preferred_element_type=jnp.float32) for t in tests]

    if sharers in (2, 4, 8):
        held = grads
        step = sharers // 2
        while True:
            came = lax.ppermute(held, group, [(i, i ^ step) for i in range(sharers)])
            if step == 1:
                break
            held = jnp.concatenate([held, came], axis=0)
            step //= 2
        gathered = [held, came]
    else:
        gathered = [lax.all_gather(grads, group, axis=0, tiled=True)]
    return finish(examples, flat // sharers, gathered, raw)


def solution(mesh):
    in_specs = (
        P(("groups", "dp", "sub"), "mp"),
        P(("groups", "dp", "sub"), "mp"),
        P(("groups", "dp", "sub")),
        P("mp", None),
        P("mp", None),
        P(("mp", "sub"), None),
    )
    out_specs = (P(("groups", "dp", "sub"), None), P(("groups", "dp", "sub"), "mp"))
    return jax.shard_map(
        per_device, mesh=mesh, in_specs=in_specs, out_specs=out_specs, check_vma=False
    )
```

```python
import functools

import jax
import jax.numpy as jnp
from jax import lax
from jax.experimental import pallas as pl
from jax.experimental.pallas import tpu as pltpu
from jax.sharding import PartitionSpec as P

SEQ = 64
CHUNK = 1024
CONTRACT_LAST = (((1,), (1,)), ((), ()))
CONTRACT_FIRST = (((0,), (0,)), ((), ()))


def chunks_of(width):
    return [(at, min(CHUNK, width - at)) for at in range(0, width, CHUNK)]


def project_kernel(hidden, out_grad, proj_in, proj_out, out, hid, og, pin, pout, sems):
    jobs = []
    for src, src_w, dst, dst_w in ((out_grad, proj_out, og, pout), (hidden, proj_in, hid, pin)):
        for at, size in chunks_of(src.shape[1]):
            jobs.append((src.at[:, pl.ds(at, size)], dst.at[:, pl.ds(at, size)],
                         src_w.at[:, pl.ds(at, size)], dst_w.at[:, pl.ds(at, size)]))
    copies = []
    for n, (src, dst, src_w, dst_w) in enumerate(jobs):
        pair = (pltpu.make_async_copy(src_w, dst_w, sems.at[1, n]), pltpu.make_async_copy(src, dst, sems.at[0, n]))
        for copy in pair:
            copy.start()
        copies.append(pair)
    first = len(chunks_of(out_grad.shape[1]))
    sums = [None, None]
    for n, (_, dst, _, dst_w) in enumerate(jobs):
        for copy in copies[n]:
            copy.wait()
        part = lax.dot_general(dst_w[...], dst[...], CONTRACT_LAST, preferred_element_type=jnp.float32)
        which = 0 if n >= first else 1
        sums[which] = part if sums[which] is None else sums[which] + part
    k_in = pin.shape[0]
    out[:k_in] = sums[0]
    out[k_in:] = sums[1]


def project(hidden, out_grad, proj_in, proj_out):
    rows, width = hidden.shape
    narrow = out_grad.shape[1]
    k_in, k_out = proj_in.shape[1], proj_out.shape[1]
    jobs = len(chunks_of(width)) + len(chunks_of(narrow))
    return pl.pallas_call(
        project_kernel,
        out_shape=jax.ShapeDtypeStruct((k_in + k_out, rows), jnp.float32),
        in_specs=[pl.BlockSpec(memory_space=pltpu.HBM)] * 4,
        out_specs=pl.BlockSpec(memory_space=pltpu.VMEM),
        scratch_shapes=[
            pltpu.VMEM((rows, width), jnp.bfloat16),
            pltpu.VMEM((rows, narrow), jnp.bfloat16),
            pltpu.VMEM((k_in, width), jnp.bfloat16),
            pltpu.VMEM((k_out, narrow), jnp.bfloat16),
            pltpu.SemaphoreType.DMA((2, jobs)),
        ],
        compiler_params=pltpu.CompilerParams(vmem_limit_bytes=24 << 20),
        cost_estimate=pl.CostEstimate(
            flops=2 * rows * (width * k_in + narrow * k_out),
            bytes_accessed=2 * rows * (width + narrow) + 2 * (width * k_in + narrow * k_out),
            transcendentals=0,
        ),
    )(*(pltpu.with_memory_space_constraint(x, pltpu.HBM) for x in (hidden, out_grad, proj_in.T, proj_out.T)))


def grads_kernel(k_in, mask, *refs):
    *pieces, out = refs
    both = pieces[0][...]
    for piece in pieces[1:]:
        both = both + piece[...]
    rows = both.shape[1]
    act = both[:k_in] * mask[...]
    grad = both[k_in:]
    row = lax.broadcasted_iota(jnp.int32, (16, rows), 0)
    col = lax.broadcasted_iota(jnp.int32, (16, rows), 1)
    pick = jnp.where((col >= row * SEQ) & (col < (row + 1) * SEQ), 1.0, 0.0).astype(jnp.bfloat16)
    per = 8
    k_out = grad.shape[0]
    for at in range(0, k_in, per):
        rest = jnp.concatenate([act[i:i + 1] * grad for i in range(at, at + per)], axis=0)
        total = None
        for _ in range(3):
            high = rest.astype(jnp.bfloat16)
            rest = rest - high.astype(jnp.float32)
            part = lax.dot_general(pick, high, CONTRACT_LAST, preferred_element_type=jnp.float32)
            total = part if total is None else total + part
        out[:, at * k_out:(at + per) * k_out] = total[:out.shape[0]].astype(jnp.bfloat16)


def example_grads(mask, pieces, k_in, k_out):
    vmem = pl.BlockSpec(memory_space=pltpu.VMEM)
    return pl.pallas_call(
        functools.partial(grads_kernel, k_in),
        out_shape=jax.ShapeDtypeStruct((mask.shape[1] // SEQ, k_in * k_out), jnp.bfloat16),
        in_specs=[vmem] * (1 + len(pieces)),
        out_specs=vmem,
        compiler_params=pltpu.CompilerParams(vmem_limit_bytes=6 << 20),
        cost_estimate=pl.CostEstimate(flops=1 << 33, bytes_accessed=0, transcendentals=0),
    )(mask, *pieces)


def finish_kernel(examples, n_pieces, n_raw, *refs):
    pieces, raw = refs[:n_pieces], refs[n_pieces:n_pieces + n_raw]
    cov, scores = refs[n_pieces + n_raw:]
    own_rows = cov.shape[0]
    place = lax.axis_index(("dp", "sub"))
    every = jnp.concatenate([p[...] for p in pieces], axis=0)
    if own_rows % 128 == 0:
        at = pl.multiple_of(place * own_rows, own_rows)
        own = jnp.concatenate([p[:, pl.ds(at, own_rows)] for p in pieces], axis=0)
    else:
        at = pl.multiple_of((place * own_rows) // 128 * 128, 128)
        wider = jnp.concatenate([p[:, pl.ds(at, 128)] for p in pieces], axis=0)
        own = pltpu.roll(wider.astype(jnp.float32), at - place * own_rows + 128, 1)[:, :own_rows].astype(jnp.bfloat16)
    wide = every.astype(jnp.float32)
    factor = lax.rsqrt(jnp.sum(wide * wide) / examples + 1e-06)
    if n_raw == 2:
        near, far = raw[0][...], raw[1][...]
        first = lax.axis_index("sub") == 0
        half = near.shape[1]
        scores[:, :half] = jnp.where(first, near, far) * factor
        scores[:, half:] = jnp.where(first, far, near) * factor
    else:
        scores[...] = raw[0][...] * factor
    cov[...] = lax.dot_general(own, every, CONTRACT_FIRST, preferred_element_type=jnp.float32) * (1.0 / examples)


def finish(examples, own_rows, pieces, raw):
    flat = pieces[0].shape[1]
    vmem = pl.BlockSpec(memory_space=pltpu.VMEM)
    return pl.pallas_call(
        functools.partial(finish_kernel, examples, len(pieces), len(raw)),
        out_shape=(
            jax.ShapeDtypeStruct((own_rows, flat), jnp.float32),
            jax.ShapeDtypeStruct((raw[0].shape[0], sum(r.shape[1] for r in raw)), jnp.float32),
        ),
        in_specs=[vmem] * (len(pieces) + len(raw)),
        out_specs=(vmem, vmem),
        compiler_params=pltpu.CompilerParams(vmem_limit_bytes=8 << 20),
    )(*pieces, *raw)


def per_device(hidden, out_grad, lengths, proj_in, proj_out, test_proj):
    k_in, k_out = proj_in.shape[1], proj_out.shape[1]
    flat = k_in * k_out
    rows = hidden.shape[0]
    group = ("dp", "sub")
    sharers = lax.axis_size(group)
    examples = lengths.shape[0] * sharers
    n_sub = lax.axis_size("sub")

    both = project(hidden, out_grad, proj_in, proj_out)
    if lax.axis_size("mp") == 2:
        pieces = [both, lax.ppermute(both, "mp", [(0, 1), (1, 0)])]
    else:
        pieces = [lax.psum(both, "mp")]
    lengths, _ = lax.optimization_barrier((lengths, both))
    slots = jnp.arange(SEQ, dtype=jnp.int32)
    mask = (slots[None, :] < lengths[:, None]).astype(jnp.float32).reshape(1, rows)
    grads = example_grads(mask, pieces, k_in, k_out)

    if n_sub == 2:
        other = lax.ppermute(test_proj, "sub", [(0, 1), (1, 0)])
        tests = [test_proj, other]
    else:
        tests = [lax.all_gather(test_proj, "sub", axis=0, tiled=True)]
    raw = [jnp.einsum("ep,qp->eq", grads, t, preferred_element_type=jnp.float32) for t in tests]

    if sharers in (2, 4, 8):
        held = grads
        step = sharers // 2
        while True:
            came = lax.ppermute(held, group, [(i, i ^ step) for i in range(sharers)])
            if step == 1:
                break
            held = jnp.concatenate([held, came], axis=0)
            step //= 2
        gathered = [held, came]
    else:
        gathered = [lax.all_gather(grads, group, axis=0, tiled=True)]
    return finish(examples, flat // sharers, gathered, raw)


def solution(mesh):
    in_specs = (
        P(("groups", "dp", "sub"), "mp"),
        P(("groups", "dp", "sub"), "mp"),
        P(("groups", "dp", "sub")),
        P("mp", None),
        P("mp", None),
        P(("mp", "sub"), None),
    )
    out_specs = (P(("groups", "dp", "sub"), None), P(("groups", "dp", "sub"), "mp"))
    return jax.shard_map(
        per_device, mesh=mesh, in_specs=in_specs, out_specs=out_specs, check_vma=False
    )
```

```python
import functools

import jax
import jax.numpy as jnp
from jax import lax
from jax.experimental import pallas as pl
from jax.experimental.pallas import tpu as pltpu
from jax.sharding import PartitionSpec as P

SEQ = 64
ROWS = 64
CONTRACT_LAST = (((1,), (1,)), ((), ()))
CONTRACT_FIRST = (((0,), (0,)), ((), ()))


def project_kernel(hidden, out_grad, proj_in, proj_out, out, hid, og, pin, pout, sems):
    rows = hidden.shape[0]
    k_in = pin.shape[0]
    parts = [pl.ds(at, ROWS) for at in range(0, rows, ROWS)]
    copies = [
        pltpu.make_async_copy(proj_out, pout, sems.at[0]),
        pltpu.make_async_copy(out_grad, og, sems.at[1]),
        pltpu.make_async_copy(proj_in, pin, sems.at[2]),
    ]
    copies += [pltpu.make_async_copy(hidden.at[part], hid.at[part], sems.at[3 + n]) for n, part in enumerate(parts)]
    for copy in copies:
        copy.start()
    for copy in copies[:2]:
        copy.wait()
    out[k_in:] = lax.dot_general(pout[...], og[...], CONTRACT_LAST, preferred_element_type=jnp.float32)
    copies[2].wait()
    sums = []
    for part, copy in zip(parts, copies[3:]):
        copy.wait()
        sums.append(lax.dot_general(pin[...], hid[part], CONTRACT_LAST, preferred_element_type=jnp.float32))
    out[:k_in] = jnp.concatenate(sums, axis=1)


def project(hidden, out_grad, proj_in, proj_out):
    rows, width = hidden.shape
    narrow = out_grad.shape[1]
    k_in, k_out = proj_in.shape[1], proj_out.shape[1]
    return pl.pallas_call(
        project_kernel,
        out_shape=jax.ShapeDtypeStruct((k_in + k_out, rows), jnp.float32),
        in_specs=[pl.BlockSpec(memory_space=pltpu.HBM)] * 4,
        out_specs=pl.BlockSpec(memory_space=pltpu.VMEM),
        scratch_shapes=[
            pltpu.VMEM((rows, width), jnp.bfloat16),
            pltpu.VMEM((rows, narrow), jnp.bfloat16),
            pltpu.VMEM((k_in, width), jnp.bfloat16),
            pltpu.VMEM((k_out, narrow), jnp.bfloat16),
            pltpu.SemaphoreType.DMA((3 + rows // ROWS,)),
        ],
        compiler_params=pltpu.CompilerParams(vmem_limit_bytes=24 << 20),
        cost_estimate=pl.CostEstimate(
            flops=2 * rows * (width * k_in + narrow * k_out),
            bytes_accessed=2 * rows * (width + narrow) + 2 * (width * k_in + narrow * k_out),
            transcendentals=0,
        ),
    )(*(pltpu.with_memory_space_constraint(x, pltpu.HBM) for x in (hidden, out_grad, proj_in.T, proj_out.T)))


def grads_kernel(k_in, mask, *refs):
    *pieces, out = refs
    both = pieces[0][...]
    for piece in pieces[1:]:
        both = both + piece[...]
    rows = both.shape[1]
    act = both[:k_in] * mask[...]
    grad = both[k_in:]
    row = lax.broadcasted_iota(jnp.int32, (16, rows), 0)
    col = lax.broadcasted_iota(jnp.int32, (16, rows), 1)
    pick = jnp.where((col >= row * SEQ) & (col < (row + 1) * SEQ), 1.0, 0.0).astype(jnp.bfloat16)
    per = 8
    k_out = grad.shape[0]
    for at in range(0, k_in, per):
        rest = jnp.concatenate([act[i:i + 1] * grad for i in range(at, at + per)], axis=0)
        total = None
        for _ in range(3):
            high = rest.astype(jnp.bfloat16)
            rest = rest - high.astype(jnp.float32)
            part = lax.dot_general(pick, high, CONTRACT_LAST, preferred_element_type=jnp.float32)
            total = part if total is None else total + part
        out[:, at * k_out:(at + per) * k_out] = total[:out.shape[0]].astype(jnp.bfloat16)


def example_grads(mask, pieces, k_in, k_out):
    vmem = pl.BlockSpec(memory_space=pltpu.VMEM)
    return pl.pallas_call(
        functools.partial(grads_kernel, k_in),
        out_shape=jax.ShapeDtypeStruct((mask.shape[1] // SEQ, k_in * k_out), jnp.bfloat16),
        in_specs=[vmem] * (1 + len(pieces)),
        out_specs=vmem,
        compiler_params=pltpu.CompilerParams(vmem_limit_bytes=6 << 20),
        cost_estimate=pl.CostEstimate(flops=1 << 33, bytes_accessed=0, transcendentals=0),
    )(mask, *pieces)


def finish_kernel(examples, n_pieces, n_raw, *refs):
    pieces, raw = refs[:n_pieces], refs[n_pieces:n_pieces + n_raw]
    cov, scores = refs[n_pieces + n_raw:]
    own_rows = cov.shape[0]
    place = lax.axis_index(("dp", "sub"))
    every = jnp.concatenate([p[...] for p in pieces], axis=0)
    if own_rows % 128 == 0:
        at = pl.multiple_of(place * own_rows, own_rows)
        own = jnp.concatenate([p[:, pl.ds(at, own_rows)] for p in pieces], axis=0)
    else:
        at = pl.multiple_of((place * own_rows) // 128 * 128, 128)
        wider = jnp.concatenate([p[:, pl.ds(at, 128)] for p in pieces], axis=0)
        own = pltpu.roll(wider.astype(jnp.float32), at - place * own_rows + 128, 1)[:, :own_rows].astype(jnp.bfloat16)
    wide = every.astype(jnp.float32)
    factor = lax.rsqrt(jnp.sum(wide * wide) / examples + 1e-06)
    if n_raw == 2:
        near, far = raw[0][...], raw[1][...]
        first = lax.axis_index("sub") == 0
        half = near.shape[1]
        scores[:, :half] = jnp.where(first, near, far) * factor
        scores[:, half:] = jnp.where(first, far, near) * factor
    else:
        scores[...] = raw[0][...] * factor
    cov[...] = lax.dot_general(own, every, CONTRACT_FIRST, preferred_element_type=jnp.float32) * (1.0 / examples)


def finish(examples, own_rows, pieces, raw):
    flat = pieces[0].shape[1]
    vmem = pl.BlockSpec(memory_space=pltpu.VMEM)
    return pl.pallas_call(
        functools.partial(finish_kernel, examples, len(pieces), len(raw)),
        out_shape=(
            jax.ShapeDtypeStruct((own_rows, flat), jnp.float32),
            jax.ShapeDtypeStruct((raw[0].shape[0], sum(r.shape[1] for r in raw)), jnp.float32),
        ),
        in_specs=[vmem] * (len(pieces) + len(raw)),
        out_specs=(vmem, vmem),
        compiler_params=pltpu.CompilerParams(vmem_limit_bytes=8 << 20),
    )(*pieces, *raw)


def per_device(hidden, out_grad, lengths, proj_in, proj_out, test_proj):
    k_in, k_out = proj_in.shape[1], proj_out.shape[1]
    flat = k_in * k_out
    rows = hidden.shape[0]
    group = ("dp", "sub")
    sharers = lax.axis_size(group)
    examples = lengths.shape[0] * sharers
    n_sub = lax.axis_size("sub")

    both = project(hidden, out_grad, proj_in, proj_out)
    if lax.axis_size("mp") == 2:
        pieces = [both, lax.ppermute(both, "mp", [(0, 1), (1, 0)])]
    else:
        pieces = [lax.psum(both, "mp")]
    lengths, _ = lax.optimization_barrier((lengths, both))
    slots = jnp.arange(SEQ, dtype=jnp.int32)
    mask = (slots[None, :] < lengths[:, None]).astype(jnp.float32).reshape(1, rows)
    grads = example_grads(mask, pieces, k_in, k_out)

    if n_sub == 2 and sharers == 8:
        swap = [(i, i ^ 1) for i in range(sharers)]
        came = lax.ppermute(grads, group, swap)
        held = jnp.concatenate([grads, came], axis=0)
        gathered = [held]
        for step in (2, 4, 6):
            gathered.append(lax.ppermute(held, group, [(i, i ^ step) for i in range(sharers)]))
        near = jnp.einsum("ep,qp->eq", grads, test_proj, preferred_element_type=jnp.float32)
        for_other = jnp.einsum("ep,qp->eq", came, test_proj, preferred_element_type=jnp.float32)
        raw = [near, lax.ppermute(for_other, group, swap)]
    else:
        tests = lax.all_gather(test_proj, "sub", axis=0, tiled=True)
        raw = [jnp.einsum("ep,qp->eq", grads, tests, preferred_element_type=jnp.float32)]
        gathered = [lax.all_gather(grads, group, axis=0, tiled=True)]
    return finish(examples, flat // sharers, gathered, raw)


def solution(mesh):
    in_specs = (
        P(("groups", "dp", "sub"), "mp"),
        P(("groups", "dp", "sub"), "mp"),
        P(("groups", "dp", "sub")),
        P("mp", None),
        P("mp", None),
        P(("mp", "sub"), None),
    )
    out_specs = (P(("groups", "dp", "sub"), None), P(("groups", "dp", "sub"), "mp"))
    return jax.shard_map(
        per_device, mesh=mesh, in_specs=in_specs, out_specs=out_specs, check_vma=False
    )
```

```python
import functools

import jax
import jax.numpy as jnp
from jax import lax
from jax.experimental import pallas as pl
from jax.experimental.pallas import tpu as pltpu
from jax.sharding import PartitionSpec as P

SEQ = 64
CHUNK = 1024
DEPTH = 256
CONTRACT_LAST = (((1,), (1,)), ((), ()))
CONTRACT_FIRST = (((0,), (0,)), ((), ()))


def chunks_of(width):
    return [(at, min(CHUNK, width - at)) for at in range(0, width, CHUNK)]


def tree_sum(terms):
    while len(terms) > 1:
        terms = [a + b for a, b in zip(terms[::2], terms[1::2])] + terms[len(terms) // 2 * 2:]
    return terms[0]


def project_kernel(scales, hidden, out_grad, proj_in, proj_out, out, hid, og, pin, pout, sems):
    jobs = []
    for which, (src, src_w, dst, dst_w) in enumerate(((out_grad, proj_out, og, pout), (hidden, proj_in, hid, pin))):
        weights = pltpu.make_async_copy(src_w, dst_w, sems.at[0, which])
        weights.start()
        for at, size in chunks_of(src.shape[1]):
            part = pl.ds(at, size)
            copy = pltpu.make_async_copy(src.at[:, part], dst.at[:, part], sems.at[1, len(jobs)])
            copy.start()
            jobs.append((which, weights if at == 0 else None, copy, dst, dst_w, at, size))
    sums = [[], []]
    for which, weights, copy, dst, dst_w, at, size in jobs:
        if weights is not None:
            weights.wait()
        copy.wait()
        sums[which].append(tree_sum([
            lax.dot_general(dst_w[:, at + k:at + k + DEPTH], dst[:, at + k:at + k + DEPTH], CONTRACT_LAST,
                            preferred_element_type=jnp.float32)
            for k in range(0, size, DEPTH)
        ]))
    k_in = pin.shape[0]
    out[:k_in] = tree_sum(sums[1]) * scales[0]
    out[k_in:] = tree_sum(sums[0]) * scales[1]


def project(hidden, out_grad, proj_in, proj_out, scales):
    rows, width = hidden.shape
    narrow = out_grad.shape[1]
    k_in, k_out = proj_in.shape[1], proj_out.shape[1]
    return pl.pallas_call(
        functools.partial(project_kernel, scales),
        out_shape=jax.ShapeDtypeStruct((k_in + k_out, rows), jnp.float32),
        in_specs=[pl.BlockSpec(memory_space=pltpu.HBM)] * 4,
        out_specs=pl.BlockSpec(memory_space=pltpu.VMEM),
        scratch_shapes=[
            pltpu.VMEM((rows, width), jnp.bfloat16),
            pltpu.VMEM((rows, narrow), jnp.bfloat16),
            pltpu.VMEM((k_in, width), jnp.bfloat16),
            pltpu.VMEM((k_out, narrow), jnp.bfloat16),
            pltpu.SemaphoreType.DMA((2, len(chunks_of(width)) + len(chunks_of(narrow)))),
        ],
        compiler_params=pltpu.CompilerParams(vmem_limit_bytes=24 << 20),
        cost_estimate=pl.CostEstimate(
            flops=2 * rows * (width * k_in + narrow * k_out),
            bytes_accessed=2 * rows * (width + narrow) + 2 * (width * k_in + narrow * k_out),
            transcendentals=0,
        ),
    )(*(pltpu.with_memory_space_constraint(x, pltpu.HBM) for x in (hidden, out_grad, proj_in.T, proj_out.T)))


def grads_kernel(k_in, scales, mask, *refs):
    *pieces, out = refs
    both = pieces[0][...]
    for piece in pieces[1:]:
        both = both + piece[...]
    rows = both.shape[1]
    act = both[:k_in] * (mask[...] * (1.0 / scales[0]))
    grad = both[k_in:] * (1.0 / scales[1])
    row = lax.broadcasted_iota(jnp.int32, (16, rows), 0)
    col = lax.broadcasted_iota(jnp.int32, (16, rows), 1)
    pick = jnp.where((col >= row * SEQ) & (col < (row + 1) * SEQ), 1.0, 0.0).astype(jnp.bfloat16)
    per = 8
    k_out = grad.shape[0]
    for at in range(0, k_in, per):
        rest = jnp.concatenate([act[i:i + 1] * grad for i in range(at, at + per)], axis=0)
        total = None
        for _ in range(3):
            high = rest.astype(jnp.bfloat16)
            rest = rest - high.astype(jnp.float32)
            part = lax.dot_general(pick, high, CONTRACT_LAST, preferred_element_type=jnp.float32)
            total = part if total is None else total + part
        out[:, at * k_out:(at + per) * k_out] = total[:out.shape[0]].astype(jnp.bfloat16)


def example_grads(mask, pieces, k_in, k_out, scales):
    vmem = pl.BlockSpec(memory_space=pltpu.VMEM)
    return pl.pallas_call(
        functools.partial(grads_kernel, k_in, scales),
        out_shape=jax.ShapeDtypeStruct((mask.shape[1] // SEQ, k_in * k_out), jnp.bfloat16),
        in_specs=[vmem] * (1 + len(pieces)),
        out_specs=vmem,
        compiler_params=pltpu.CompilerParams(vmem_limit_bytes=6 << 20),
        cost_estimate=pl.CostEstimate(flops=1 << 33, bytes_accessed=0, transcendentals=0),
    )(mask, *pieces)


def finish_kernel(examples, n_pieces, n_raw, *refs):
    pieces, raw = refs[:n_pieces], refs[n_pieces:n_pieces + n_raw]
    cov, scores = refs[n_pieces + n_raw:]
    own_rows = cov.shape[0]
    place = lax.axis_index(("dp", "sub"))
    every = jnp.concatenate([p[...] for p in pieces], axis=0)
    if own_rows % 128 == 0:
        at = pl.multiple_of(place * own_rows, own_rows)
        own = jnp.concatenate([p[:, pl.ds(at, own_rows)] for p in pieces], axis=0)
    else:
        at = pl.multiple_of((place * own_rows) // 128 * 128, 128)
        wider = jnp.concatenate([p[:, pl.ds(at, 128)] for p in pieces], axis=0)
        own = pltpu.roll(wider.astype(jnp.float32), at - place * own_rows + 128, 1)[:, :own_rows].astype(jnp.bfloat16)
    wide = every.astype(jnp.float32)
    factor = lax.rsqrt(jnp.sum(wide * wide) / examples + 1e-06)
    if n_raw == 2:
        near, far = raw[0][...], raw[1][...]
        first = lax.axis_index("sub") == 0
        half = near.shape[1]
        scores[:, :half] = jnp.where(first, near, far) * factor
        scores[:, half:] = jnp.where(first, far, near) * factor
    else:
        scores[...] = raw[0][...] * factor
    cov[...] = lax.dot_general(own, every, CONTRACT_FIRST, preferred_element_type=jnp.float32) * (1.0 / examples)


def finish(examples, own_rows, pieces, raw):
    flat = pieces[0].shape[1]
    vmem = pl.BlockSpec(memory_space=pltpu.VMEM)
    return pl.pallas_call(
        functools.partial(finish_kernel, examples, len(pieces), len(raw)),
        out_shape=(
            jax.ShapeDtypeStruct((own_rows, flat), jnp.float32),
            jax.ShapeDtypeStruct((raw[0].shape[0], sum(r.shape[1] for r in raw)), jnp.float32),
        ),
        in_specs=[vmem] * (len(pieces) + len(raw)),
        out_specs=(vmem, vmem),
        compiler_params=pltpu.CompilerParams(vmem_limit_bytes=8 << 20),
    )(*pieces, *raw)


def per_device(hidden, out_grad, lengths, proj_in, proj_out, test_proj):
    k_in, k_out = proj_in.shape[1], proj_out.shape[1]
    flat = k_in * k_out
    rows = hidden.shape[0]
    group = ("dp", "sub")
    sharers = lax.axis_size(group)
    examples = lengths.shape[0] * sharers
    n_sub = lax.axis_size("sub")

    paired = lax.axis_size("mp") == 2
    scales = (128.0, 4.0) if paired else (1.0, 1.0)
    both = project(hidden, out_grad, proj_in, proj_out, scales)
    if paired:
        sent = lax.optimization_barrier(both.astype(jnp.float16))
        came = lax.ppermute(sent, "mp", [(0, 1), (1, 0)])
        pieces = [sent.astype(jnp.float32), came.astype(jnp.float32)]
    else:
        pieces = [lax.psum(both, "mp")]
    lengths, _ = lax.optimization_barrier((lengths, both))
    slots = jnp.arange(SEQ, dtype=jnp.int32)
    mask = (slots[None, :] < lengths[:, None]).astype(jnp.float32).reshape(1, rows)
    grads = example_grads(mask, pieces, k_in, k_out, scales)

    if n_sub == 2 and sharers == 8:
        swap = [(i, i ^ 1) for i in range(sharers)]
        came = lax.ppermute(grads, group, swap)
        held = jnp.concatenate([grads, came], axis=0)
        gathered = [held]
        for step in (2, 4, 6):
            gathered.append(lax.ppermute(held, group, [(i, i ^ step) for i in range(sharers)]))
        near = jnp.einsum("ep,qp->eq", grads, test_proj, preferred_element_type=jnp.float32)
        for_other = jnp.einsum("ep,qp->eq", came, test_proj, preferred_element_type=jnp.float32)
        raw = [near, lax.ppermute(for_other, group, swap)]
    else:
        tests = lax.all_gather(test_proj, "sub", axis=0, tiled=True)
        raw = [jnp.einsum("ep,qp->eq", grads, tests, preferred_element_type=jnp.float32)]
        gathered = [lax.all_gather(grads, group, axis=0, tiled=True)]
    return finish(examples, flat // sharers, gathered, raw)


def solution(mesh):
    in_specs = (
        P(("groups", "dp", "sub"), "mp"),
        P(("groups", "dp", "sub"), "mp"),
        P(("groups", "dp", "sub")),
        P("mp", None),
        P("mp", None),
        P(("mp", "sub"), None),
    )
    out_specs = (P(("groups", "dp", "sub"), None), P(("groups", "dp", "sub"), "mp"))
    return jax.shard_map(
        per_device, mesh=mesh, in_specs=in_specs, out_specs=out_specs, check_vma=False
    )
```

```python
import functools

import jax
import jax.numpy as jnp
from jax import lax
from jax.experimental import pallas as pl
from jax.experimental.pallas import tpu as pltpu
from jax.sharding import PartitionSpec as P

SEQ = 64
CHUNK = 1024
DEPTH = 256
SENDS = (
    [(3, 0)],
    [(1, 0), (2, 1)],
    [(0, 1), (2, 0)],
    [(0, 2), (2, 3)],
    [(1, 2), (3, 1), (0, 3)],
    [(3, 2), (1, 3)],
)
CONTRACT_LAST = (((1,), (1,)), ((), ()))
CONTRACT_FIRST = (((0,), (0,)), ((), ()))


def chunks_of(width):
    return [(at, min(CHUNK, width - at)) for at in range(0, width, CHUNK)]


def tree_sum(terms):
    while len(terms) > 1:
        terms = [a + b for a, b in zip(terms[::2], terms[1::2])] + terms[len(terms) // 2 * 2:]
    return terms[0]


def split_dot(weights, data, at, size):
    lanes = [slice(at + k, at + k + DEPTH) for k in range(0, size, DEPTH)]
    left = jnp.concatenate([weights[:, lane] for lane in lanes], axis=0)
    right = jnp.concatenate([data[:, lane] for lane in lanes], axis=0)
    both = lax.dot_general(left, right, CONTRACT_LAST, preferred_element_type=jnp.float32)
    m, n = weights.shape[0], data.shape[0]
    return tree_sum([both[i * m:(i + 1) * m, i * n:(i + 1) * n] for i in range(len(lanes))])


def project_kernel(scales, hidden, out_grad, proj_in, proj_out, out, hid, og, pin, pout, sems):
    jobs = []
    for which, (src, src_w, dst, dst_w) in enumerate(((out_grad, proj_out, og, pout), (hidden, proj_in, hid, pin))):
        weights = pltpu.make_async_copy(src_w, dst_w, sems.at[0, which])
        weights.start()
        for at, size in chunks_of(src.shape[1]):
            part = pl.ds(at, size)
            copy = pltpu.make_async_copy(src.at[:, part], dst.at[:, part], sems.at[1, len(jobs)])
            copy.start()
            jobs.append((which, weights if at == 0 else None, copy, dst, dst_w, at, size))
    sums = [[], []]
    for which, weights, copy, dst, dst_w, at, size in jobs:
        if weights is not None:
            weights.wait()
        copy.wait()
        sums[which].append(split_dot(dst_w, dst, at, size))
    k_in = pin.shape[0]
    out[:k_in] = tree_sum(sums[1]) * scales[0]
    out[k_in:] = tree_sum(sums[0]) * scales[1]


def project(hidden, out_grad, proj_in, proj_out, scales):
    rows, width = hidden.shape
    narrow = out_grad.shape[1]
    k_in, k_out = proj_in.shape[1], proj_out.shape[1]
    return pl.pallas_call(
        functools.partial(project_kernel, scales),
        out_shape=jax.ShapeDtypeStruct((k_in + k_out, rows), jnp.float32),
        in_specs=[pl.BlockSpec(memory_space=pltpu.HBM)] * 4,
        out_specs=pl.BlockSpec(memory_space=pltpu.VMEM),
        scratch_shapes=[
            pltpu.VMEM((rows, width), jnp.bfloat16),
            pltpu.VMEM((rows, narrow), jnp.bfloat16),
            pltpu.VMEM((k_in, width), jnp.bfloat16),
            pltpu.VMEM((k_out, narrow), jnp.bfloat16),
            pltpu.SemaphoreType.DMA((2, len(chunks_of(width)) + len(chunks_of(narrow)))),
        ],
        compiler_params=pltpu.CompilerParams(vmem_limit_bytes=24 << 20),
        cost_estimate=pl.CostEstimate(
            flops=2 * rows * (width * k_in + narrow * k_out),
            bytes_accessed=2 * rows * (width + narrow) + 2 * (width * k_in + narrow * k_out),
            transcendentals=0,
        ),
    )(*(pltpu.with_memory_space_constraint(x, pltpu.HBM) for x in (hidden, out_grad, proj_in.T, proj_out.T)))


def grads_kernel(k_in, scales, mask, *refs):
    *pieces, out = refs
    both = pieces[0][...]
    for piece in pieces[1:]:
        both = both + piece[...]
    rows = both.shape[1]
    act = both[:k_in] * (mask[...] * (1.0 / scales[0]))
    grad = both[k_in:] * (1.0 / scales[1])
    row = lax.broadcasted_iota(jnp.int32, (16, rows), 0)
    col = lax.broadcasted_iota(jnp.int32, (16, rows), 1)
    pick = jnp.where((col >= row * SEQ) & (col < (row + 1) * SEQ), 1.0, 0.0).astype(jnp.bfloat16)
    per = 8
    k_out = grad.shape[0]
    for at in range(0, k_in, per):
        rest = jnp.concatenate([act[i:i + 1] * grad for i in range(at, at + per)], axis=0)
        total = None
        for _ in range(3):
            high = rest.astype(jnp.bfloat16)
            rest = rest - high.astype(jnp.float32)
            part = lax.dot_general(pick, high, CONTRACT_LAST, preferred_element_type=jnp.float32)
            total = part if total is None else total + part
        out[:, at * k_out:(at + per) * k_out] = total[:out.shape[0]].astype(jnp.bfloat16)


def example_grads(mask, pieces, k_in, k_out, scales):
    vmem = pl.BlockSpec(memory_space=pltpu.VMEM)
    return pl.pallas_call(
        functools.partial(grads_kernel, k_in, scales),
        out_shape=jax.ShapeDtypeStruct((mask.shape[1] // SEQ, k_in * k_out), jnp.bfloat16),
        in_specs=[vmem] * (1 + len(pieces)),
        out_specs=vmem,
        compiler_params=pltpu.CompilerParams(vmem_limit_bytes=6 << 20),
        cost_estimate=pl.CostEstimate(flops=1 << 33, bytes_accessed=0, transcendentals=0),
    )(mask, *pieces)


def finish_kernel(examples, n_pieces, n_raw, *refs):
    pieces, raw = refs[:n_pieces], refs[n_pieces:n_pieces + n_raw]
    cov, scores = refs[n_pieces + n_raw:]
    own_rows = cov.shape[0]
    place = lax.axis_index(("dp", "sub"))
    every = jnp.concatenate([p[...] for p in pieces], axis=0)
    if own_rows % 128 == 0:
        at = pl.multiple_of(place * own_rows, own_rows)
        own = jnp.concatenate([p[:, pl.ds(at, own_rows)] for p in pieces], axis=0)
    else:
        at = pl.multiple_of((place * own_rows) // 128 * 128, 128)
        wider = jnp.concatenate([p[:, pl.ds(at, 128)] for p in pieces], axis=0)
        own = pltpu.roll(wider.astype(jnp.float32), at - place * own_rows + 128, 1)[:, :own_rows].astype(jnp.bfloat16)
    wide = every.astype(jnp.float32)
    factor = lax.rsqrt(jnp.sum(wide * wide) / examples + 1e-06)
    if n_raw == 2:
        near, far = raw[0][...], raw[1][...]
        first = lax.axis_index("sub") == 0
        half = near.shape[1]
        scores[:, :half] = jnp.where(first, near, far) * factor
        scores[:, half:] = jnp.where(first, far, near) * factor
    else:
        scores[...] = raw[0][...] * factor
    cov[...] = lax.dot_general(own, every, CONTRACT_FIRST, preferred_element_type=jnp.float32) * (1.0 / examples)


def finish(examples, own_rows, pieces, raw):
    flat = pieces[0].shape[1]
    vmem = pl.BlockSpec(memory_space=pltpu.VMEM)
    return pl.pallas_call(
        functools.partial(finish_kernel, examples, len(pieces), len(raw)),
        out_shape=(
            jax.ShapeDtypeStruct((own_rows, flat), jnp.float32),
            jax.ShapeDtypeStruct((raw[0].shape[0], sum(r.shape[1] for r in raw)), jnp.float32),
        ),
        in_specs=[vmem] * (len(pieces) + len(raw)),
        out_specs=(vmem, vmem),
        compiler_params=pltpu.CompilerParams(vmem_limit_bytes=8 << 20),
    )(*pieces, *raw)


def per_device(hidden, out_grad, lengths, proj_in, proj_out, test_proj):
    k_in, k_out = proj_in.shape[1], proj_out.shape[1]
    flat = k_in * k_out
    rows = hidden.shape[0]
    group = ("dp", "sub")
    sharers = lax.axis_size(group)
    examples = lengths.shape[0] * sharers
    n_sub = lax.axis_size("sub")

    paired = lax.axis_size("mp") == 2
    scales = (128.0, 4.0) if paired else (1.0, 1.0)
    both = project(hidden, out_grad, proj_in, proj_out, scales)
    if paired:
        sent = lax.optimization_barrier(both.astype(jnp.float16))
        came = lax.ppermute(sent, "mp", [(0, 1), (1, 0)])
        pieces = [sent.astype(jnp.float32), came.astype(jnp.float32)]
    else:
        pieces = [lax.psum(both, "mp")]
    lengths, _ = lax.optimization_barrier((lengths, both))
    slots = jnp.arange(SEQ, dtype=jnp.int32)
    mask = (slots[None, :] < lengths[:, None]).astype(jnp.float32).reshape(1, rows)
    grads = example_grads(mask, pieces, k_in, k_out, scales)

    if n_sub == 2 and lax.axis_size("dp") == 4:
        swap = [(i, i ^ 1) for i in range(sharers)]
        came = lax.ppermute(grads, group, swap)
        held = jnp.concatenate([grads, came], axis=0)
        gathered = [held]
        for pairs in reversed(SENDS):
            gathered.append(lax.ppermute(held, "dp", pairs))
        near = jnp.einsum("ep,qp->eq", grads, test_proj, preferred_element_type=jnp.float32)
        for_other = jnp.einsum("ep,qp->eq", came, test_proj, preferred_element_type=jnp.float32)
        raw = [near, lax.ppermute(for_other, group, swap)]
    else:
        tests = lax.all_gather(test_proj, "sub", axis=0, tiled=True)
        raw = [jnp.einsum("ep,qp->eq", grads, tests, preferred_element_type=jnp.float32)]
        gathered = [lax.all_gather(grads, group, axis=0, tiled=True)]
    return finish(examples, flat // sharers, gathered, raw)


def solution(mesh):
    in_specs = (
        P(("groups", "dp", "sub"), "mp"),
        P(("groups", "dp", "sub"), "mp"),
        P(("groups", "dp", "sub")),
        P("mp", None),
        P("mp", None),
        P(("mp", "sub"), None),
    )
    out_specs = (P(("groups", "dp", "sub"), None), P(("groups", "dp", "sub"), "mp"))
    return jax.shard_map(
        per_device, mesh=mesh, in_specs=in_specs, out_specs=out_specs, check_vma=False
    )
```

```python
import functools

import jax
import jax.numpy as jnp
from jax import lax
from jax.experimental import pallas as pl
from jax.experimental.pallas import tpu as pltpu
from jax.sharding import PartitionSpec as P

SEQ = 64
DEPTH = 256
SENDS = ((6, 3, 7, 4, 0, 5, 2, 1), (0, 5, 2, 1, 6, 3, 4, 7))
CONTRACT_LAST = (((1,), (1,)), ((), ()))
CONTRACT_FIRST = (((0,), (0,)), ((), ()))


def chunk_of(width):
    return next(size for size in (1024, 512, 256, 128) if width % size == 0)


def tree_sum(terms):
    while len(terms) > 1:
        terms = [a + b for a, b in zip(terms[::2], terms[1::2])] + terms[len(terms) // 2 * 2:]
    return terms[0]


def project_kernel(scales, hidden, out_grad, proj_in, proj_out, out, hid, og, pin, pout, sems):
    k_in = pin.shape[0]
    sides = ((out_grad, proj_out, og, pout), (hidden, proj_in, hid, pin))

    def part_copy(which, n):
        src, _, dst, _ = sides[which]
        size = chunk_of(src.shape[1])
        lanes = pl.ds(n * size if isinstance(n, int) else pl.multiple_of(n * size, size), size)
        return pltpu.make_async_copy(src.at[:, lanes], dst.at[:, lanes], sems.at[which, 1 + n])

    def weight_copy(which):
        return pltpu.make_async_copy(sides[which][1], sides[which][3], sems.at[which, 0])

    counts = [side[0].shape[1] // chunk_of(side[0].shape[1]) for side in sides]
    for which in (0, 1):
        weight_copy(which).start()
        for n in range(counts[which]):
            part_copy(which, n).start()
    for which in (0, 1):
        _, _, dst, dst_w = sides[which]
        size = chunk_of(dst.shape[1])
        depth = min(size, DEPTH)
        weight_copy(which).wait()

        def step(n, total):
            part_copy(which, n).wait()
            terms = []
            for k in range(0, size, depth):
                lanes = pl.ds(pl.multiple_of(n * size + k, depth), depth)
                terms.append(lax.dot_general(dst_w[:, lanes], dst[:, lanes], CONTRACT_LAST,
                                             preferred_element_type=jnp.float32))
            return total + tree_sum(terms)

        zero = jnp.zeros((dst_w.shape[0], dst.shape[0]), jnp.float32)
        total = lax.fori_loop(0, counts[which], step, zero)
        if which == 0:
            out[k_in:] = total * scales[1]
        else:
            out[:k_in] = total * scales[0]


def project(hidden, out_grad, proj_in, proj_out, scales):
    rows, width = hidden.shape
    narrow = out_grad.shape[1]
    k_in, k_out = proj_in.shape[1], proj_out.shape[1]
    return pl.pallas_call(
        functools.partial(project_kernel, scales),
        out_shape=jax.ShapeDtypeStruct((k_in + k_out, rows), jnp.float32),
        in_specs=[pl.BlockSpec(memory_space=pltpu.HBM)] * 4,
        out_specs=pl.BlockSpec(memory_space=pltpu.VMEM),
        scratch_shapes=[
            pltpu.VMEM((rows, width), jnp.bfloat16),
            pltpu.VMEM((rows, narrow), jnp.bfloat16),
            pltpu.VMEM((k_in, width), jnp.bfloat16),
            pltpu.VMEM((k_out, narrow), jnp.bfloat16),
            pltpu.SemaphoreType.DMA((2, 1 + max(width // chunk_of(width), narrow // chunk_of(narrow)))),
        ],
        compiler_params=pltpu.CompilerParams(vmem_limit_bytes=24 << 20),
        cost_estimate=pl.CostEstimate(
            flops=2 * rows * (width * k_in + narrow * k_out),
            bytes_accessed=2 * rows * (width + narrow) + 2 * (width * k_in + narrow * k_out),
            transcendentals=0,
        ),
    )(*(pltpu.with_memory_space_constraint(x, pltpu.HBM) for x in (hidden, out_grad, proj_in.T, proj_out.T)))


def grads_kernel(k_in, scales, mask, *refs):
    *pieces, out = refs
    both = pieces[0][...]
    for piece in pieces[1:]:
        both = both + piece[...]
    rows = both.shape[1]
    act = both[:k_in] * (mask[...] * (1.0 / scales[0]))
    grad = both[k_in:] * (1.0 / scales[1])
    row = lax.broadcasted_iota(jnp.int32, (16, rows), 0)
    col = lax.broadcasted_iota(jnp.int32, (16, rows), 1)
    pick = jnp.where((col >= row * SEQ) & (col < (row + 1) * SEQ), 1.0, 0.0).astype(jnp.bfloat16)
    per = 8
    k_out = grad.shape[0]
    for at in range(0, k_in, per):
        rest = jnp.concatenate([act[i:i + 1] * grad for i in range(at, at + per)], axis=0)
        total = None
        for _ in range(3):
            high = rest.astype(jnp.bfloat16)
            rest = rest - high.astype(jnp.float32)
            part = lax.dot_general(pick, high, CONTRACT_LAST, preferred_element_type=jnp.float32)
            total = part if total is None else total + part
        out[:, at * k_out:(at + per) * k_out] = total[:out.shape[0]].astype(jnp.bfloat16)


def example_grads(mask, pieces, k_in, k_out, scales):
    vmem = pl.BlockSpec(memory_space=pltpu.VMEM)
    return pl.pallas_call(
        functools.partial(grads_kernel, k_in, scales),
        out_shape=jax.ShapeDtypeStruct((mask.shape[1] // SEQ, k_in * k_out), jnp.bfloat16),
        in_specs=[vmem] * (1 + len(pieces)),
        out_specs=vmem,
        compiler_params=pltpu.CompilerParams(vmem_limit_bytes=6 << 20),
        cost_estimate=pl.CostEstimate(flops=1 << 33, bytes_accessed=0, transcendentals=0),
    )(mask, *pieces)


def finish_kernel(examples, n_pieces, n_raw, *refs):
    pieces, raw = refs[:n_pieces], refs[n_pieces:n_pieces + n_raw]
    cov, scores = refs[n_pieces + n_raw:]
    own_rows = cov.shape[0]
    place = lax.axis_index(("dp", "sub"))
    every = jnp.concatenate([p[...] for p in pieces], axis=0)
    if own_rows % 128 == 0:
        at = pl.multiple_of(place * own_rows, own_rows)
        own = jnp.concatenate([p[:, pl.ds(at, own_rows)] for p in pieces], axis=0)
    else:
        at = pl.multiple_of((place * own_rows) // 128 * 128, 128)
        wider = jnp.concatenate([p[:, pl.ds(at, 128)] for p in pieces], axis=0)
        own = pltpu.roll(wider.astype(jnp.float32), at - place * own_rows + 128, 1)[:, :own_rows].astype(jnp.bfloat16)
    wide = every.astype(jnp.float32)
    factor = lax.rsqrt(jnp.sum(wide * wide) / examples + 1e-06)
    if n_raw == 2:
        near, far = raw[0][...], raw[1][...]
        first = lax.axis_index("sub") == 0
        half = near.shape[1]
        scores[:, :half] = jnp.where(first, near, far) * factor
        scores[:, half:] = jnp.where(first, far, near) * factor
    else:
        scores[...] = raw[0][...] * factor
    cov[...] = lax.dot_general(own, every, CONTRACT_FIRST, preferred_element_type=jnp.float32) * (1.0 / examples)


def finish(examples, own_rows, pieces, raw):
    flat = pieces[0].shape[1]
    vmem = pl.BlockSpec(memory_space=pltpu.VMEM)
    return pl.pallas_call(
        functools.partial(finish_kernel, examples, len(pieces), len(raw)),
        out_shape=(
            jax.ShapeDtypeStruct((own_rows, flat), jnp.float32),
            jax.ShapeDtypeStruct((raw[0].shape[0], sum(r.shape[1] for r in raw)), jnp.float32),
        ),
        in_specs=[vmem] * (len(pieces) + len(raw)),
        out_specs=(vmem, vmem),
        compiler_params=pltpu.CompilerParams(vmem_limit_bytes=8 << 20),
    )(*pieces, *raw)


def per_device(hidden, out_grad, lengths, proj_in, proj_out, test_proj):
    k_in, k_out = proj_in.shape[1], proj_out.shape[1]
    flat = k_in * k_out
    rows = hidden.shape[0]
    group = ("dp", "sub")
    sharers = lax.axis_size(group)
    examples = lengths.shape[0] * sharers
    n_sub = lax.axis_size("sub")

    paired = lax.axis_size("mp") == 2
    scales = (128.0, 4.0) if paired else (1.0, 1.0)
    both = project(hidden, out_grad, proj_in, proj_out, scales)
    if paired:
        sent = lax.optimization_barrier(both.astype(jnp.float16))
        came = lax.ppermute(sent, "mp", [(0, 1), (1, 0)])
        pieces = [sent.astype(jnp.float32), came.astype(jnp.float32)]
    else:
        pieces = [lax.psum(both, "mp")]
    lengths, _ = lax.optimization_barrier((lengths, both))
    slots = jnp.arange(SEQ, dtype=jnp.int32)
    mask = (slots[None, :] < lengths[:, None]).astype(jnp.float32).reshape(1, rows)
    grads = example_grads(mask, pieces, k_in, k_out, scales)

    if n_sub == 2 and lax.axis_size("dp") == 4:
        swap = [(i, i ^ 1) for i in range(sharers)]
        came = lax.ppermute(grads, group, swap)
        held = jnp.concatenate([grads, came], axis=0)
        place = lax.axis_index(group)
        fetched = []
        for targets in reversed(SENDS):
            block = lax.ppermute(held, group, list(enumerate(targets)))
            kept = sum(1 << i for i, target in enumerate(targets) if i != target)
            fetched.append(jnp.where(((kept >> place) & 1) == 1, block, 0))
        fetched = jnp.concatenate(fetched, axis=0)
        gathered = [held, fetched, lax.ppermute(fetched, group, swap)]
        near = jnp.einsum("ep,qp->eq", grads, test_proj, preferred_element_type=jnp.float32)
        for_other = jnp.einsum("ep,qp->eq", came, test_proj, preferred_element_type=jnp.float32)
        raw = [near, lax.ppermute(for_other, group, swap)]
    else:
        tests = lax.all_gather(test_proj, "sub", axis=0, tiled=True)
        raw = [jnp.einsum("ep,qp->eq", grads, tests, preferred_element_type=jnp.float32)]
        gathered = [lax.all_gather(grads, group, axis=0, tiled=True)]
    return finish(examples, flat // sharers, gathered, raw)


def solution(mesh):
    in_specs = (
        P(("groups", "dp", "sub"), "mp"),
        P(("groups", "dp", "sub"), "mp"),
        P(("groups", "dp", "sub")),
        P("mp", None),
        P("mp", None),
        P(("mp", "sub"), None),
    )
    out_specs = (P(("groups", "dp", "sub"), None), P(("groups", "dp", "sub"), "mp"))
    return jax.shard_map(
        per_device, mesh=mesh, in_specs=in_specs, out_specs=out_specs, check_vma=False
    )
```

```python
import functools

import jax
import jax.numpy as jnp
from jax import lax
from jax.experimental import pallas as pl
from jax.experimental.pallas import tpu as pltpu
from jax.sharding import PartitionSpec as P

SEQ = 64
DEPTH = 256
SENDS = ((7, 2, 3, 5, 0, 4, 1, 6), (5, 0, 7, 1, 3, 6, 2, 4))
CONTRACT_LAST = (((1,), (1,)), ((), ()))
CONTRACT_FIRST = (((0,), (0,)), ((), ()))


def chunk_of(width):
    return next(size for size in (1024, 512, 256, 128) if width % size == 0)


def tree_sum(terms):
    while len(terms) > 1:
        terms = [a + b for a, b in zip(terms[::2], terms[1::2])] + terms[len(terms) // 2 * 2:]
    return terms[0]


def project_kernel(scales, hidden, out_grad, proj_in, proj_out, out, hid, og, pin, pout, sems):
    k_in = pin.shape[0]
    sides = ((out_grad, proj_out, og, pout), (hidden, proj_in, hid, pin))

    def part_copy(which, n):
        src, _, dst, _ = sides[which]
        size = chunk_of(src.shape[1])
        lanes = pl.ds(n * size if isinstance(n, int) else pl.multiple_of(n * size, size), size)
        return pltpu.make_async_copy(src.at[:, lanes], dst.at[:, lanes], sems.at[which, 1 + n])

    def weight_copy(which):
        return pltpu.make_async_copy(sides[which][1], sides[which][3], sems.at[which, 0])

    counts = [side[0].shape[1] // chunk_of(side[0].shape[1]) for side in sides]
    for which in (0, 1):
        weight_copy(which).start()
        for n in range(counts[which]):
            part_copy(which, n).start()
    for which in (0, 1):
        _, _, dst, dst_w = sides[which]
        size = chunk_of(dst.shape[1])
        depth = min(size, DEPTH)
        weight_copy(which).wait()

        def step(n, total):
            part_copy(which, n).wait()
            terms = []
            for k in range(0, size, depth):
                lanes = pl.ds(pl.multiple_of(n * size + k, depth), depth)
                terms.append(lax.dot_general(dst_w[:, lanes], dst[:, lanes], CONTRACT_LAST,
                                             preferred_element_type=jnp.float32))
            return total + tree_sum(terms)

        zero = jnp.zeros((dst_w.shape[0], dst.shape[0]), jnp.float32)
        total = lax.fori_loop(0, counts[which], step, zero)
        if which == 0:
            out[k_in:] = total * scales[1]
        else:
            out[:k_in] = total * scales[0]


def project(hidden, out_grad, proj_in, proj_out, scales):
    rows, width = hidden.shape
    narrow = out_grad.shape[1]
    k_in, k_out = proj_in.shape[1], proj_out.shape[1]
    return pl.pallas_call(
        functools.partial(project_kernel, scales),
        out_shape=jax.ShapeDtypeStruct((k_in + k_out, rows), jnp.float32),
        in_specs=[pl.BlockSpec(memory_space=pltpu.HBM)] * 4,
        out_specs=pl.BlockSpec(memory_space=pltpu.VMEM),
        scratch_shapes=[
            pltpu.VMEM((rows, width), jnp.bfloat16),
            pltpu.VMEM((rows, narrow), jnp.bfloat16),
            pltpu.VMEM((k_in, width), jnp.bfloat16),
            pltpu.VMEM((k_out, narrow), jnp.bfloat16),
            pltpu.SemaphoreType.DMA((2, 1 + max(width // chunk_of(width), narrow // chunk_of(narrow)))),
        ],
        compiler_params=pltpu.CompilerParams(vmem_limit_bytes=24 << 20),
        cost_estimate=pl.CostEstimate(
            flops=2 * rows * (width * k_in + narrow * k_out),
            bytes_accessed=2 * rows * (width + narrow) + 2 * (width * k_in + narrow * k_out),
            transcendentals=0,
        ),
    )(*(pltpu.with_memory_space_constraint(x, pltpu.HBM) for x in (hidden, out_grad, proj_in.T, proj_out.T)))


def grads_kernel(k_in, scales, mask, *refs):
    *pieces, out = refs
    both = pieces[0][...]
    for piece in pieces[1:]:
        both = both + piece[...]
    rows = both.shape[1]
    act = both[:k_in] * (mask[...] * (1.0 / scales[0]))
    grad = both[k_in:] * (1.0 / scales[1])
    row = lax.broadcasted_iota(jnp.int32, (16, rows), 0)
    col = lax.broadcasted_iota(jnp.int32, (16, rows), 1)
    pick = jnp.where((col >= row * SEQ) & (col < (row + 1) * SEQ), 1.0, 0.0).astype(jnp.bfloat16)
    per = 8
    k_out = grad.shape[0]
    for at in range(0, k_in, per):
        rest = jnp.concatenate([act[i:i + 1] * grad for i in range(at, at + per)], axis=0)
        total = None
        for _ in range(3):
            high = rest.astype(jnp.bfloat16)
            rest = rest - high.astype(jnp.float32)
            part = lax.dot_general(pick, high, CONTRACT_LAST, preferred_element_type=jnp.float32)
            total = part if total is None else total + part
        out[:, at * k_out:(at + per) * k_out] = total[:out.shape[0]].astype(jnp.bfloat16)


def example_grads(mask, pieces, k_in, k_out, scales):
    vmem = pl.BlockSpec(memory_space=pltpu.VMEM)
    return pl.pallas_call(
        functools.partial(grads_kernel, k_in, scales),
        out_shape=jax.ShapeDtypeStruct((mask.shape[1] // SEQ, k_in * k_out), jnp.bfloat16),
        in_specs=[vmem] * (1 + len(pieces)),
        out_specs=vmem,
        compiler_params=pltpu.CompilerParams(vmem_limit_bytes=6 << 20),
        cost_estimate=pl.CostEstimate(flops=1 << 33, bytes_accessed=0, transcendentals=0),
    )(mask, *pieces)


def finish_kernel(examples, n_pieces, n_raw, *refs):
    pieces, raw = refs[:n_pieces], refs[n_pieces:n_pieces + n_raw]
    cov, scores = refs[n_pieces + n_raw:]
    own_rows = cov.shape[0]
    place = lax.axis_index(("dp", "sub"))
    every = jnp.concatenate([p[...] for p in pieces], axis=0)
    if own_rows % 128 == 0:
        at = pl.multiple_of(place * own_rows, own_rows)
        own = jnp.concatenate([p[:, pl.ds(at, own_rows)] for p in pieces], axis=0)
    else:
        at = pl.multiple_of((place * own_rows) // 128 * 128, 128)
        wider = jnp.concatenate([p[:, pl.ds(at, 128)] for p in pieces], axis=0)
        own = pltpu.roll(wider.astype(jnp.float32), at - place * own_rows + 128, 1)[:, :own_rows].astype(jnp.bfloat16)
    wide = every.astype(jnp.float32)
    factor = lax.rsqrt(jnp.sum(wide * wide) / examples + 1e-06)
    if n_raw == 2:
        near, far = raw[0][...], raw[1][...]
        first = lax.axis_index("sub") == 0
        half = near.shape[1]
        scores[:, :half] = jnp.where(first, near, far) * factor
        scores[:, half:] = jnp.where(first, far, near) * factor
    else:
        scores[...] = raw[0][...] * factor
    cov[...] = lax.dot_general(own, every, CONTRACT_FIRST, preferred_element_type=jnp.float32) * (1.0 / examples)


def finish(examples, own_rows, pieces, raw):
    flat = pieces[0].shape[1]
    vmem = pl.BlockSpec(memory_space=pltpu.VMEM)
    return pl.pallas_call(
        functools.partial(finish_kernel, examples, len(pieces), len(raw)),
        out_shape=(
            jax.ShapeDtypeStruct((own_rows, flat), jnp.float32),
            jax.ShapeDtypeStruct((raw[0].shape[0], sum(r.shape[1] for r in raw)), jnp.float32),
        ),
        in_specs=[vmem] * (len(pieces) + len(raw)),
        out_specs=(vmem, vmem),
        compiler_params=pltpu.CompilerParams(vmem_limit_bytes=8 << 20),
    )(*pieces, *raw)


def first_arrivals(sends):
    seen = [{chip} for chip in range(len(sends[0]) // 2)]
    flags = []
    for targets in sends:
        bits = 0
        for node, target in enumerate(targets):
            if node // 2 not in seen[target // 2]:
                seen[target // 2].add(node // 2)
                bits |= 1 << target
        flags.append(bits)
    assert all(len(chips) == len(seen) for chips in seen)
    return flags


def per_device(hidden, out_grad, lengths, proj_in, proj_out, test_proj):
    k_in, k_out = proj_in.shape[1], proj_out.shape[1]
    flat = k_in * k_out
    rows = hidden.shape[0]
    group = ("dp", "sub")
    sharers = lax.axis_size(group)
    examples = lengths.shape[0] * sharers
    n_sub = lax.axis_size("sub")

    paired = lax.axis_size("mp") == 2
    scales = (128.0, 4.0) if paired else (1.0, 1.0)
    both = project(hidden, out_grad, proj_in, proj_out, scales)
    if paired:
        sent = lax.optimization_barrier(both.astype(jnp.float16))
        came = lax.ppermute(sent, "mp", [(0, 1), (1, 0)])
        pieces = [sent.astype(jnp.float32), came.astype(jnp.float32)]
    else:
        pieces = [lax.psum(both, "mp")]
    lengths, _ = lax.optimization_barrier((lengths, both))
    slots = jnp.arange(SEQ, dtype=jnp.int32)
    mask = (slots[None, :] < lengths[:, None]).astype(jnp.float32).reshape(1, rows)
    grads = example_grads(mask, pieces, k_in, k_out, scales)

    if n_sub == 2 and lax.axis_size("dp") == 4:
        swap = [(i, i ^ 1) for i in range(sharers)]
        came = lax.ppermute(grads, group, swap)
        held = jnp.concatenate([grads, came], axis=0)
        place = lax.axis_index(group)
        blocks = [lax.ppermute(held, group, list(enumerate(targets))) for targets in reversed(SENDS)][::-1]
        fetched = [jnp.where(((kept >> place) & 1) == 1, b, 0) for b, kept in zip(blocks, first_arrivals(SENDS))]
        fetched = jnp.concatenate(fetched, axis=0)
        gathered = [held, fetched, lax.ppermute(fetched, group, swap)]
        near = jnp.einsum("ep,qp->eq", grads, test_proj, preferred_element_type=jnp.float32)
        for_other = jnp.einsum("ep,qp->eq", came, test_proj, preferred_element_type=jnp.float32)
        raw = [near, lax.ppermute(for_other, group, swap)]
    else:
        tests = lax.all_gather(test_proj, "sub", axis=0, tiled=True)
        raw = [jnp.einsum("ep,qp->eq", grads, tests, preferred_element_type=jnp.float32)]
        gathered = [lax.all_gather(grads, group, axis=0, tiled=True)]
    return finish(examples, flat // sharers, gathered, raw)


def solution(mesh):
    in_specs = (
        P(("groups", "dp", "sub"), "mp"),
        P(("groups", "dp", "sub"), "mp"),
        P(("groups", "dp", "sub")),
        P("mp", None),
        P("mp", None),
        P(("mp", "sub"), None),
    )
    out_specs = (P(("groups", "dp", "sub"), None), P(("groups", "dp", "sub"), "mp"))
    return jax.shard_map(
        per_device, mesh=mesh, in_specs=in_specs, out_specs=out_specs, check_vma=False
    )
```

```python
import functools

import jax
import jax.numpy as jnp
from jax import lax
from jax.experimental import pallas as pl
from jax.experimental.pallas import tpu as pltpu
from jax.sharding import PartitionSpec as P

SEQ = 64
DEPTH = 256
SENDS = ((7, 2, 3, 5, 0, 4, 1, 6), (5, 0, 7, 1, 3, 6, 2, 4))
CONTRACT_LAST = (((1,), (1,)), ((), ()))
CONTRACT_FIRST = (((0,), (0,)), ((), ()))


def chunk_of(width):
    return next(size for size in (1024, 512, 256, 128) if width % size == 0)


def tree_sum(terms):
    while len(terms) > 1:
        terms = [a + b for a, b in zip(terms[::2], terms[1::2])] + terms[len(terms) // 2 * 2:]
    return terms[0]


def project_kernel(scales, hidden, out_grad, proj_in, proj_out, out, hid, og, pin, pout, sems):
    k_in = pin.shape[0]
    sides = ((out_grad, proj_out, og, pout), (hidden, proj_in, hid, pin))

    def part_copy(which, n):
        src, _, dst, _ = sides[which]
        size = chunk_of(src.shape[1])
        lanes = pl.ds(n * size if isinstance(n, int) else pl.multiple_of(n * size, size), size)
        return pltpu.make_async_copy(src.at[:, lanes], dst.at[:, lanes], sems.at[which, 1 + n])

    def weight_copy(which):
        return pltpu.make_async_copy(sides[which][1], sides[which][3], sems.at[which, 0])

    counts = [side[0].shape[1] // chunk_of(side[0].shape[1]) for side in sides]
    for which in (0, 1):
        weight_copy(which).start()
        for n in range(counts[which]):
            part_copy(which, n).start()
    for which in (0, 1):
        _, _, dst, dst_w = sides[which]
        size = chunk_of(dst.shape[1])
        depth = min(size, DEPTH)
        weight_copy(which).wait()

        def step(n, total):
            part_copy(which, n).wait()
            terms = []
            for k in range(0, size, depth):
                lanes = pl.ds(pl.multiple_of(n * size + k, depth), depth)
                terms.append(lax.dot_general(dst_w[:, lanes], dst[:, lanes], CONTRACT_LAST,
                                             preferred_element_type=jnp.float32))
            return total + tree_sum(terms)

        zero = jnp.zeros((dst_w.shape[0], dst.shape[0]), jnp.float32)
        total = lax.fori_loop(0, counts[which], step, zero)
        if which == 0:
            out[k_in:] = total * scales[1]
        else:
            out[:k_in] = total * scales[0]


def project(hidden, out_grad, proj_in, proj_out, scales):
    rows, width = hidden.shape
    narrow = out_grad.shape[1]
    k_in, k_out = proj_in.shape[1], proj_out.shape[1]
    return pl.pallas_call(
        functools.partial(project_kernel, scales),
        out_shape=jax.ShapeDtypeStruct((k_in + k_out, rows), jnp.float32),
        in_specs=[pl.BlockSpec(memory_space=pltpu.HBM)] * 4,
        out_specs=pl.BlockSpec(memory_space=pltpu.VMEM),
        scratch_shapes=[
            pltpu.VMEM((rows, width), jnp.bfloat16),
            pltpu.VMEM((rows, narrow), jnp.bfloat16),
            pltpu.VMEM((k_in, width), jnp.bfloat16),
            pltpu.VMEM((k_out, narrow), jnp.bfloat16),
            pltpu.SemaphoreType.DMA((2, 1 + max(width // chunk_of(width), narrow // chunk_of(narrow)))),
        ],
        compiler_params=pltpu.CompilerParams(vmem_limit_bytes=24 << 20),
        cost_estimate=pl.CostEstimate(
            flops=2 * rows * (width * k_in + narrow * k_out),
            bytes_accessed=2 * rows * (width + narrow) + 2 * (width * k_in + narrow * k_out),
            transcendentals=0,
        ),
    )(*(pltpu.with_memory_space_constraint(x, pltpu.HBM) for x in (hidden, out_grad, proj_in.T, proj_out.T)))


def grads_kernel(k_in, scales, mask, *refs):
    *pieces, out = refs
    both = pieces[0][...]
    for piece in pieces[1:]:
        both = both + piece[...]
    rows = both.shape[1]
    act = both[:k_in] * (mask[...] * (1.0 / scales[0]))
    grad = both[k_in:] * (1.0 / scales[1])
    row = lax.broadcasted_iota(jnp.int32, (16, rows), 0)
    col = lax.broadcasted_iota(jnp.int32, (16, rows), 1)
    pick = jnp.where((col >= row * SEQ) & (col < (row + 1) * SEQ), 1.0, 0.0).astype(jnp.bfloat16)
    per = 8
    k_out = grad.shape[0]
    for at in range(0, k_in, per):
        rest = jnp.concatenate([act[i:i + 1] * grad for i in range(at, at + per)], axis=0)
        total = None
        for _ in range(3):
            high = rest.astype(jnp.bfloat16)
            rest = rest - high.astype(jnp.float32)
            part = lax.dot_general(pick, high, CONTRACT_LAST, preferred_element_type=jnp.float32)
            total = part if total is None else total + part
        out[:, at * k_out:(at + per) * k_out] = total[:out.shape[0]].astype(jnp.bfloat16)


def example_grads(mask, pieces, k_in, k_out, scales):
    vmem = pl.BlockSpec(memory_space=pltpu.VMEM)
    return pl.pallas_call(
        functools.partial(grads_kernel, k_in, scales),
        out_shape=jax.ShapeDtypeStruct((mask.shape[1] // SEQ, k_in * k_out), jnp.bfloat16),
        in_specs=[vmem] * (1 + len(pieces)),
        out_specs=vmem,
        compiler_params=pltpu.CompilerParams(vmem_limit_bytes=6 << 20),
        cost_estimate=pl.CostEstimate(flops=1 << 33, bytes_accessed=0, transcendentals=0),
    )(mask, *pieces)


def finish_kernel(examples, n_pieces, n_raw, *refs):
    pieces, raw = refs[:n_pieces], refs[n_pieces:n_pieces + n_raw]
    cov, scores = refs[n_pieces + n_raw:]
    own_rows = cov.shape[0]
    place = lax.axis_index(("dp", "sub"))
    every = jnp.concatenate([p[...] for p in pieces], axis=0)
    if own_rows % 128 == 0:
        at = pl.multiple_of(place * own_rows, own_rows)
        own = jnp.concatenate([p[:, pl.ds(at, own_rows)] for p in pieces], axis=0)
    else:
        at = pl.multiple_of((place * own_rows) // 128 * 128, 128)
        wider = jnp.concatenate([p[:, pl.ds(at, 128)] for p in pieces], axis=0)
        own = pltpu.roll(wider.astype(jnp.float32), at - place * own_rows + 128, 1)[:, :own_rows].astype(jnp.bfloat16)
    wide = every.astype(jnp.float32)
    factor = lax.rsqrt(jnp.sum(wide * wide) / examples + 1e-06)
    if n_raw == 2:
        near, far = raw[0][...], raw[1][...]
        first = lax.axis_index("sub") == 0
        half = near.shape[1]
        scores[:, :half] = jnp.where(first, near, far) * factor
        scores[:, half:] = jnp.where(first, far, near) * factor
    else:
        scores[...] = raw[0][...] * factor
    cov[...] = lax.dot_general(own, every, CONTRACT_FIRST, preferred_element_type=jnp.float32) * (1.0 / examples)


def finish(examples, own_rows, pieces, raw):
    flat = pieces[0].shape[1]
    vmem = pl.BlockSpec(memory_space=pltpu.VMEM)
    return pl.pallas_call(
        functools.partial(finish_kernel, examples, len(pieces), len(raw)),
        out_shape=(
            jax.ShapeDtypeStruct((own_rows, flat), jnp.float32),
            jax.ShapeDtypeStruct((raw[0].shape[0], sum(r.shape[1] for r in raw)), jnp.float32),
        ),
        in_specs=[vmem] * (len(pieces) + len(raw)),
        out_specs=(vmem, vmem),
        compiler_params=pltpu.CompilerParams(vmem_limit_bytes=8 << 20),
    )(*pieces, *raw)


def first_arrivals(sends):
    seen = [{chip} for chip in range(len(sends[0]) // 2)]
    flags = []
    for targets in sends:
        bits = 0
        for node, target in enumerate(targets):
            if node // 2 not in seen[target // 2]:
                seen[target // 2].add(node // 2)
                bits |= 1 << target
        flags.append(bits)
    assert all(len(chips) == len(seen) for chips in seen)
    return flags


def per_device(hidden, out_grad, lengths, proj_in, proj_out, test_proj):
    k_in, k_out = proj_in.shape[1], proj_out.shape[1]
    flat = k_in * k_out
    rows = hidden.shape[0]
    group = ("dp", "sub")
    sharers = lax.axis_size(group)
    examples = lengths.shape[0] * sharers
    n_sub = lax.axis_size("sub")

    paired = lax.axis_size("mp") == 2
    scales = (128.0, 4.0) if paired else (1.0, 1.0)
    both = project(hidden, out_grad, proj_in, proj_out, scales)
    if paired:
        sent = lax.optimization_barrier(both.astype(jnp.float16))
        came = lax.ppermute(sent, "mp", [(0, 1), (1, 0)])
        pieces = [sent.astype(jnp.float32), came.astype(jnp.float32)]
    else:
        pieces = [lax.psum(both, "mp")]
    lengths, _ = lax.optimization_barrier((lengths, both))
    slots = jnp.arange(SEQ, dtype=jnp.int32)
    mask = (slots[None, :] < lengths[:, None]).astype(jnp.float32).reshape(1, rows)
    grads = example_grads(mask, pieces, k_in, k_out, scales)

    if n_sub == 2 and lax.axis_size("dp") == 4:
        swap = [(i, i ^ 1) for i in range(sharers)]
        came = lax.ppermute(grads, group, swap)
        held = jnp.concatenate([grads, came], axis=0)
        place = lax.axis_index(group)
        fetched = []
        for targets, kept in reversed(list(zip(SENDS, first_arrivals(SENDS)))):
            block = lax.ppermute(held, group, list(enumerate(targets)))
            fetched.append(jnp.where(((kept >> place) & 1) == 1, block, 0))
        fetched = jnp.concatenate(fetched, axis=0)
        gathered = [held, fetched, lax.ppermute(fetched, group, swap)]
        near = jnp.einsum("ep,qp->eq", grads, test_proj, preferred_element_type=jnp.float32)
        for_other = jnp.einsum("ep,qp->eq", came, test_proj, preferred_element_type=jnp.float32)
        raw = [near, lax.ppermute(for_other, group, swap)]
    else:
        tests = lax.all_gather(test_proj, "sub", axis=0, tiled=True)
        raw = [jnp.einsum("ep,qp->eq", grads, tests, preferred_element_type=jnp.float32)]
        gathered = [lax.all_gather(grads, group, axis=0, tiled=True)]
    return finish(examples, flat // sharers, gathered, raw)


def solution(mesh):
    in_specs = (
        P(("groups", "dp", "sub"), "mp"),
        P(("groups", "dp", "sub"), "mp"),
        P(("groups", "dp", "sub")),
        P("mp", None),
        P("mp", None),
        P(("mp", "sub"), None),
    )
    out_specs = (P(("groups", "dp", "sub"), None), P(("groups", "dp", "sub"), "mp"))
    return jax.shard_map(
        per_device, mesh=mesh, in_specs=in_specs, out_specs=out_specs, check_vma=False
    )
```

```python
import functools

import jax
import jax.numpy as jnp
from jax import lax
from jax.experimental import pallas as pl
from jax.experimental.pallas import tpu as pltpu
from jax.sharding import PartitionSpec as P

SEQ = 64
DEPTH = 256
SENDS = ((7, 2, 3, 5, 0, 4, 1, 6), (5, 0, 7, 1, 3, 6, 2, 4))
CONTRACT_LAST = (((1,), (1,)), ((), ()))
CONTRACT_FIRST = (((0,), (0,)), ((), ()))


def project_kernel(scales, size, hidden, out_grad, proj_in, proj_out, out, data, weights, sums, sems):
    narrow, width = out_grad.shape[1], hidden.shape[1]
    before = narrow // size
    first_weights = pltpu.make_async_copy(proj_out, weights.at[:, pl.ds(0, narrow)], sems.at[0])
    other_weights = pltpu.make_async_copy(proj_in, weights.at[:, pl.ds(narrow, width)], sems.at[1])
    first_weights.start()
    for n in range(before + width // size):
        src, at = (out_grad, n * size) if n < before else (hidden, n * size - narrow)
        pltpu.make_async_copy(src.at[:, pl.ds(at, size)], data.at[:, pl.ds(n * size, size)], sems.at[2 + n]).start()
        if n == 0:
            other_weights.start()
    sums[...] = jnp.zeros_like(sums)
    first_weights.wait()

    def step(n, carry):
        @pl.when(n == before)
        def _():
            other_weights.wait()

        lanes = pl.ds(pl.multiple_of(n * size, size), size)
        pltpu.make_async_copy(hidden.at[:, pl.ds(0, size)], data.at[:, lanes], sems.at[2 + n]).wait()
        which = (n < before).astype(jnp.int32)
        sums[which] += lax.dot_general(data[:, lanes], weights[:, lanes], CONTRACT_LAST,
                                       preferred_element_type=jnp.float32)
        return carry

    lax.fori_loop(0, before + width // size, step, 0)
    k_in = proj_in.shape[0]
    out[:k_in] = sums[0].T * scales[0]
    out[k_in:] = sums[1].T * scales[1]


def project(hidden, out_grad, proj_in, proj_out, scales):
    rows, width = hidden.shape
    narrow = out_grad.shape[1]
    k_in, k_out = proj_in.shape[1], proj_out.shape[1]
    size = next(size for size in (1024, 512, 256, 128) if width % size == 0 and narrow % size == 0)
    return pl.pallas_call(
        functools.partial(project_kernel, scales, size),
        out_shape=jax.ShapeDtypeStruct((k_in + k_out, rows), jnp.float32),
        in_specs=[pl.BlockSpec(memory_space=pltpu.HBM)] * 4,
        out_specs=pl.BlockSpec(memory_space=pltpu.VMEM),
        scratch_shapes=[
            pltpu.VMEM((rows, narrow + width), jnp.bfloat16),
            pltpu.VMEM((k_in, narrow + width), jnp.bfloat16),
            pltpu.VMEM((2, rows, k_in), jnp.float32),
            pltpu.SemaphoreType.DMA((2 + (narrow + width) // size,)),
        ],
        compiler_params=pltpu.CompilerParams(vmem_limit_bytes=24 << 20),
        cost_estimate=pl.CostEstimate(
            flops=2 * rows * (width * k_in + narrow * k_out),
            bytes_accessed=2 * rows * (width + narrow) + 2 * (width * k_in + narrow * k_out),
            transcendentals=0,
        ),
    )(*(pltpu.with_memory_space_constraint(x, pltpu.HBM) for x in (hidden, out_grad, proj_in.T, proj_out.T)))


def grads_kernel(k_in, scales, mask, *refs):
    *pieces, out = refs
    both = pieces[0][...]
    for piece in pieces[1:]:
        both = both + piece[...]
    rows = both.shape[1]
    act = both[:k_in] * (mask[...] * (1.0 / scales[0]))
    grad = both[k_in:] * (1.0 / scales[1])
    row = lax.broadcasted_iota(jnp.int32, (16, rows), 0)
    col = lax.broadcasted_iota(jnp.int32, (16, rows), 1)
    pick = jnp.where((col >= row * SEQ) & (col < (row + 1) * SEQ), 1.0, 0.0).astype(jnp.bfloat16)
    per = 8
    k_out = grad.shape[0]
    for at in range(0, k_in, per):
        rest = jnp.concatenate([act[i:i + 1] * grad for i in range(at, at + per)], axis=0)
        total = None
        for _ in range(2):
            high = rest.astype(jnp.bfloat16)
            rest = rest - high.astype(jnp.float32)
            part = lax.dot_general(pick, high, CONTRACT_LAST, preferred_element_type=jnp.float32)
            total = part if total is None else total + part
        out[:, at * k_out:(at + per) * k_out] = total[:out.shape[0]].astype(jnp.bfloat16)


def example_grads(mask, pieces, k_in, k_out, scales):
    vmem = pl.BlockSpec(memory_space=pltpu.VMEM)
    return pl.pallas_call(
        functools.partial(grads_kernel, k_in, scales),
        out_shape=jax.ShapeDtypeStruct((mask.shape[1] // SEQ, k_in * k_out), jnp.bfloat16),
        in_specs=[vmem] * (1 + len(pieces)),
        out_specs=vmem,
        compiler_params=pltpu.CompilerParams(vmem_limit_bytes=6 << 20),
        cost_estimate=pl.CostEstimate(flops=1 << 33, bytes_accessed=0, transcendentals=0),
    )(mask, *pieces)


def finish_kernel(examples, n_pieces, n_raw, *refs):
    pieces, raw = refs[:n_pieces], refs[n_pieces:n_pieces + n_raw]
    cov, scores, block, row, sems = refs[n_pieces + n_raw:]
    own_rows, flat = cov.shape
    place = lax.axis_index(("dp", "sub"))
    every = jnp.concatenate([p[...] for p in pieces], axis=0)
    if own_rows % 128 == 0:
        at = pl.multiple_of(place * own_rows, own_rows)
        own = jnp.concatenate([p[:, pl.ds(at, own_rows)] for p in pieces], axis=0)
    else:
        at = pl.multiple_of((place * own_rows) // 128 * 128, 128)
        wider = jnp.concatenate([p[:, pl.ds(at, 128)] for p in pieces], axis=0)
        own = pltpu.roll(wider.astype(jnp.float32), at - place * own_rows + 128, 1)[:, :own_rows].astype(jnp.bfloat16)
    copies = []
    for n, at in enumerate(range(0, flat, flat // 4)):
        lanes = pl.ds(at, flat // 4)
        block[:, lanes] = lax.dot_general(own, every[:, at:at + flat // 4], CONTRACT_FIRST,
                                          preferred_element_type=jnp.float32) * (1.0 / examples)
        copies.append(pltpu.make_async_copy(block.at[:, lanes], cov.at[:, lanes], sems.at[n]))
        copies[-1].start()
    wide = every.astype(jnp.float32)
    factor = lax.rsqrt(jnp.sum(wide * wide) / examples + 1e-06)
    if n_raw == 2:
        near, far = raw[0][...], raw[1][...]
        first = lax.axis_index("sub") == 0
        half = near.shape[1]
        row[:, :half] = jnp.where(first, near, far) * factor
        row[:, half:] = jnp.where(first, far, near) * factor
    else:
        row[...] = raw[0][...] * factor
    copies.append(pltpu.make_async_copy(row, scores, sems.at[4]))
    copies[-1].start()
    for copy in copies:
        copy.wait()


def finish(examples, own_rows, pieces, raw):
    flat = pieces[0].shape[1]
    vmem = pl.BlockSpec(memory_space=pltpu.VMEM)
    hbm = pl.BlockSpec(memory_space=pltpu.HBM)
    cov = (own_rows, flat)
    scores = (raw[0].shape[0], sum(r.shape[1] for r in raw))
    return pl.pallas_call(
        functools.partial(finish_kernel, examples, len(pieces), len(raw)),
        out_shape=(jax.ShapeDtypeStruct(cov, jnp.float32), jax.ShapeDtypeStruct(scores, jnp.float32)),
        in_specs=[vmem] * (len(pieces) + len(raw)),
        out_specs=(hbm, hbm),
        scratch_shapes=[pltpu.VMEM(cov, jnp.float32), pltpu.VMEM(scores, jnp.float32), pltpu.SemaphoreType.DMA((5,))],
        compiler_params=pltpu.CompilerParams(vmem_limit_bytes=8 << 20),
    )(*pieces, *raw)


def first_arrivals(sends):
    seen = [{chip} for chip in range(len(sends[0]) // 2)]
    flags = []
    for targets in sends:
        bits = 0
        for node, target in enumerate(targets):
            if node // 2 not in seen[target // 2]:
                seen[target // 2].add(node // 2)
                bits |= 1 << target
        flags.append(bits)
    assert all(len(chips) == len(seen) for chips in seen)
    return flags


def per_device(hidden, out_grad, lengths, proj_in, proj_out, test_proj):
    k_in, k_out = proj_in.shape[1], proj_out.shape[1]
    flat = k_in * k_out
    rows = hidden.shape[0]
    group = ("dp", "sub")
    sharers = lax.axis_size(group)
    examples = lengths.shape[0] * sharers
    n_sub = lax.axis_size("sub")

    paired = lax.axis_size("mp") == 2
    scales = (128.0, 4.0) if paired else (1.0, 1.0)
    both = project(hidden, out_grad, proj_in, proj_out, scales)
    if paired:
        sent = lax.optimization_barrier(both.astype(jnp.float16))
        came = lax.ppermute(sent, "mp", [(0, 1), (1, 0)])
        pieces = [sent.astype(jnp.float32), came.astype(jnp.float32)]
    else:
        pieces = [lax.psum(both, "mp")]
    lengths, _ = lax.optimization_barrier((lengths, both))
    slots = jnp.arange(SEQ, dtype=jnp.int32)
    mask = (slots[None, :] < lengths[:, None]).astype(jnp.float32).reshape(1, rows)
    grads = example_grads(mask, pieces, k_in, k_out, scales)

    if n_sub == 2 and lax.axis_size("dp") == 4:
        swap = [(i, i ^ 1) for i in range(sharers)]
        came = lax.ppermute(grads, group, swap)
        held = jnp.concatenate([grads, came], axis=0)
        place = lax.axis_index(group)
        fetched = []
        for targets, kept in reversed(list(zip(SENDS, first_arrivals(SENDS)))):
            block = lax.ppermute(held, group, list(enumerate(targets)))
            fetched.append(jnp.where(((kept >> place) & 1) == 1, block, 0))
        fetched = jnp.concatenate(fetched, axis=0)
        gathered = [held, fetched, lax.ppermute(fetched, group, swap)]
        near = jnp.einsum("ep,qp->eq", grads, test_proj, preferred_element_type=jnp.float32)
        for_other = jnp.einsum("ep,qp->eq", came, test_proj, preferred_element_type=jnp.float32)
        raw = [near, lax.ppermute(for_other, group, swap)]
    else:
        tests = lax.all_gather(test_proj, "sub", axis=0, tiled=True)
        raw = [jnp.einsum("ep,qp->eq", grads, tests, preferred_element_type=jnp.float32)]
        gathered = [lax.all_gather(grads, group, axis=0, tiled=True)]
    return finish(examples, flat // sharers, gathered, raw)


def solution(mesh):
    in_specs = (
        P(("groups", "dp", "sub"), "mp"),
        P(("groups", "dp", "sub"), "mp"),
        P(("groups", "dp", "sub")),
        P("mp", None),
        P("mp", None),
        P(("mp", "sub"), None),
    )
    out_specs = (P(("groups", "dp", "sub"), None), P(("groups", "dp", "sub"), "mp"))
    return jax.shard_map(
        per_device, mesh=mesh, in_specs=in_specs, out_specs=out_specs, check_vma=False
    )
```

```python
import functools

import jax
import jax.numpy as jnp
from jax import lax
from jax.experimental import pallas as pl
from jax.experimental.pallas import tpu as pltpu
from jax.sharding import PartitionSpec as P

SEQ = 64
DEPTH = 256
SENDS = ((7, 2, 3, 5, 0, 4, 1, 6), (5, 0, 7, 1, 3, 6, 2, 4))
CONTRACT_LAST = (((1,), (1,)), ((), ()))
CONTRACT_FIRST = (((0,), (0,)), ((), ()))


def project_kernel(scales, size, hidden, out_grad, proj_in, proj_out, out, data, weights, sums, sems):
    rows, width = hidden.shape
    narrow = out_grad.shape[1]
    half = rows // 2
    wide_lanes, narrow_lanes = pl.ds(0, width), pl.ds(width, narrow)
    copies = [
        pltpu.make_async_copy(proj_in, weights.at[:, wide_lanes], sems.at[0]),
        pltpu.make_async_copy(hidden.at[pl.ds(0, half)], data.at[pl.ds(0, half), wide_lanes], sems.at[1]),
        pltpu.make_async_copy(hidden.at[pl.ds(half, half)], data.at[pl.ds(half, half), wide_lanes], sems.at[2]),
        pltpu.make_async_copy(proj_out, weights.at[:, narrow_lanes], sems.at[3]),
        pltpu.make_async_copy(out_grad, data.at[:, narrow_lanes], sems.at[4]),
    ]
    for copy in copies:
        copy.start()
    sums[...] = jnp.zeros_like(sums)
    many, few = width // size, narrow // size
    copies[0].wait()

    def step(n, carry):
        for first, needed in ((0, copies[1:2]), (many, copies[2:3]), (2 * many, copies[3:])):
            @pl.when(n == first)
            def _():
                for copy in needed:
                    copy.wait()

        late = n >= 2 * many
        n = n - jnp.where(late, 2 * many, 0)
        lower = n >= jnp.where(late, few, many)
        chunk = n - jnp.where(lower, jnp.where(late, few, many), 0) + jnp.where(late, many, 0)
        lanes = pl.ds(pl.multiple_of(chunk * size, size), size)
        part = pl.ds(pl.multiple_of(jnp.where(lower, half, 0), half), half)
        which = late.astype(jnp.int32)
        sums[which, part] += lax.dot_general(data[part, lanes], weights[:, lanes], CONTRACT_LAST,
                                             preferred_element_type=jnp.float32)
        return carry

    lax.fori_loop(0, 2 * (many + few), step, 0)
    k_in = proj_in.shape[0]
    out[:k_in] = sums[0].T * scales[0]
    out[k_in:] = sums[1].T * scales[1]


def project(hidden, out_grad, proj_in, proj_out, scales):
    rows, width = hidden.shape
    narrow = out_grad.shape[1]
    k_in, k_out = proj_in.shape[1], proj_out.shape[1]
    size = next(size for size in (1024, 512, 256, 128) if width % size == 0 and narrow % size == 0)
    return pl.pallas_call(
        functools.partial(project_kernel, scales, size),
        out_shape=jax.ShapeDtypeStruct((k_in + k_out, rows), jnp.float32),
        in_specs=[pl.BlockSpec(memory_space=pltpu.HBM)] * 4,
        out_specs=pl.BlockSpec(memory_space=pltpu.VMEM),
        scratch_shapes=[
            pltpu.VMEM((rows, narrow + width), jnp.bfloat16),
            pltpu.VMEM((k_in, narrow + width), jnp.bfloat16),
            pltpu.VMEM((2, rows, k_in), jnp.float32),
            pltpu.SemaphoreType.DMA((5,)),
        ],
        compiler_params=pltpu.CompilerParams(vmem_limit_bytes=24 << 20),
        cost_estimate=pl.CostEstimate(
            flops=2 * rows * (width * k_in + narrow * k_out),
            bytes_accessed=2 * rows * (width + narrow) + 2 * (width * k_in + narrow * k_out),
            transcendentals=0,
        ),
    )(*(pltpu.with_memory_space_constraint(x, pltpu.HBM) for x in (hidden, out_grad, proj_in.T, proj_out.T)))


def grads_kernel(k_in, scales, mask, *refs):
    *pieces, out = refs
    both = pieces[0][...]
    for piece in pieces[1:]:
        both = both + piece[...]
    rows = both.shape[1]
    act = both[:k_in] * (mask[...] * (1.0 / scales[0]))
    grad = both[k_in:] * (1.0 / scales[1])
    row = lax.broadcasted_iota(jnp.int32, (16, rows), 0)
    col = lax.broadcasted_iota(jnp.int32, (16, rows), 1)
    pick = jnp.where((col >= row * SEQ) & (col < (row + 1) * SEQ), 1.0, 0.0).astype(jnp.bfloat16)
    per = 8
    k_out = grad.shape[0]
    for at in range(0, k_in, per):
        rest = jnp.concatenate([act[i:i + 1] * grad for i in range(at, at + per)], axis=0)
        total = None
        for _ in range(2):
            high = rest.astype(jnp.bfloat16)
            rest = rest - high.astype(jnp.float32)
            part = lax.dot_general(pick, high, CONTRACT_LAST, preferred_element_type=jnp.float32)
            total = part if total is None else total + part
        out[:, at * k_out:(at + per) * k_out] = total[:out.shape[0]].astype(jnp.bfloat16)


def example_grads(mask, pieces, k_in, k_out, scales):
    vmem = pl.BlockSpec(memory_space=pltpu.VMEM)
    return pl.pallas_call(
        functools.partial(grads_kernel, k_in, scales),
        out_shape=jax.ShapeDtypeStruct((mask.shape[1] // SEQ, k_in * k_out), jnp.bfloat16),
        in_specs=[vmem] * (1 + len(pieces)),
        out_specs=vmem,
        compiler_params=pltpu.CompilerParams(vmem_limit_bytes=6 << 20),
        cost_estimate=pl.CostEstimate(flops=1 << 33, bytes_accessed=0, transcendentals=0),
    )(mask, *pieces)


def finish_kernel(examples, n_pieces, n_raw, *refs):
    pieces, raw = refs[:n_pieces], refs[n_pieces:n_pieces + n_raw]
    cov, scores, block, row, sems = refs[n_pieces + n_raw:]
    own_rows, flat = cov.shape
    place = lax.axis_index(("dp", "sub"))
    every = jnp.concatenate([p[...] for p in pieces], axis=0)
    if own_rows % 128 == 0:
        at = pl.multiple_of(place * own_rows, own_rows)
        own = jnp.concatenate([p[:, pl.ds(at, own_rows)] for p in pieces], axis=0)
    else:
        at = pl.multiple_of((place * own_rows) // 128 * 128, 128)
        wider = jnp.concatenate([p[:, pl.ds(at, 128)] for p in pieces], axis=0)
        own = pltpu.roll(wider.astype(jnp.float32), at - place * own_rows + 128, 1)[:, :own_rows].astype(jnp.bfloat16)
    copies = []
    for n, at in enumerate(range(0, flat, flat // 4)):
        lanes = pl.ds(at, flat // 4)
        block[:, lanes] = lax.dot_general(own, every[:, at:at + flat // 4], CONTRACT_FIRST,
                                          preferred_element_type=jnp.float32) * (1.0 / examples)
        copies.append(pltpu.make_async_copy(block.at[:, lanes], cov.at[:, lanes], sems.at[n]))
        copies[-1].start()
    wide = every.astype(jnp.float32)
    factor = lax.rsqrt(jnp.sum(wide * wide) / examples + 1e-06)
    if n_raw == 2:
        near, far = raw[0][...], raw[1][...]
        first = lax.axis_index("sub") == 0
        half = near.shape[1]
        row[:, :half] = jnp.where(first, near, far) * factor
        row[:, half:] = jnp.where(first, far, near) * factor
    else:
        row[...] = raw[0][...] * factor
    copies.append(pltpu.make_async_copy(row, scores, sems.at[4]))
    copies[-1].start()
    for copy in copies:
        copy.wait()


def finish(examples, own_rows, pieces, raw):
    flat = pieces[0].shape[1]
    vmem = pl.BlockSpec(memory_space=pltpu.VMEM)
    hbm = pl.BlockSpec(memory_space=pltpu.HBM)
    cov = (own_rows, flat)
    scores = (raw[0].shape[0], sum(r.shape[1] for r in raw))
    return pl.pallas_call(
        functools.partial(finish_kernel, examples, len(pieces), len(raw)),
        out_shape=(jax.ShapeDtypeStruct(cov, jnp.float32), jax.ShapeDtypeStruct(scores, jnp.float32)),
        in_specs=[vmem] * (len(pieces) + len(raw)),
        out_specs=(hbm, hbm),
        scratch_shapes=[pltpu.VMEM(cov, jnp.float32), pltpu.VMEM(scores, jnp.float32), pltpu.SemaphoreType.DMA((5,))],
        compiler_params=pltpu.CompilerParams(vmem_limit_bytes=8 << 20),
    )(*pieces, *raw)


def first_arrivals(sends):
    seen = [{chip} for chip in range(len(sends[0]) // 2)]
    flags = []
    for targets in sends:
        bits = 0
        for node, target in enumerate(targets):
            if node // 2 not in seen[target // 2]:
                seen[target // 2].add(node // 2)
                bits |= 1 << target
        flags.append(bits)
    assert all(len(chips) == len(seen) for chips in seen)
    return flags


def per_device(hidden, out_grad, lengths, proj_in, proj_out, test_proj):
    k_in, k_out = proj_in.shape[1], proj_out.shape[1]
    flat = k_in * k_out
    rows = hidden.shape[0]
    group = ("dp", "sub")
    sharers = lax.axis_size(group)
    examples = lengths.shape[0] * sharers
    n_sub = lax.axis_size("sub")

    paired = lax.axis_size("mp") == 2
    scales = (128.0, 4.0) if paired else (1.0, 1.0)
    both = project(hidden, out_grad, proj_in, proj_out, scales)
    if paired:
        sent = lax.optimization_barrier(both.astype(jnp.float16))
        came = lax.ppermute(sent, "mp", [(0, 1), (1, 0)])
        pieces = [sent.astype(jnp.float32), came.astype(jnp.float32)]
    else:
        pieces = [lax.psum(both, "mp")]
    lengths, _ = lax.optimization_barrier((lengths, both))
    slots = jnp.arange(SEQ, dtype=jnp.int32)
    mask = (slots[None, :] < lengths[:, None]).astype(jnp.float32).reshape(1, rows)
    grads = example_grads(mask, pieces, k_in, k_out, scales)

    if n_sub == 2 and lax.axis_size("dp") == 4:
        swap = [(i, i ^ 1) for i in range(sharers)]
        came = lax.ppermute(grads, group, swap)
        held = jnp.concatenate([grads, came], axis=0)
        place = lax.axis_index(group)
        fetched = []
        for targets, kept in reversed(list(zip(SENDS, first_arrivals(SENDS)))):
            block = lax.ppermute(held, group, list(enumerate(targets)))
            fetched.append(jnp.where(((kept >> place) & 1) == 1, block, 0))
        fetched = jnp.concatenate(fetched, axis=0)
        gathered = [held, fetched, lax.ppermute(fetched, group, swap)]
        near = jnp.einsum("ep,qp->eq", grads, test_proj, preferred_element_type=jnp.float32)
        for_other = jnp.einsum("ep,qp->eq", came, test_proj, preferred_element_type=jnp.float32)
        raw = [near, lax.ppermute(for_other, group, swap)]
    else:
        tests = lax.all_gather(test_proj, "sub", axis=0, tiled=True)
        raw = [jnp.einsum("ep,qp->eq", grads, tests, preferred_element_type=jnp.float32)]
        gathered = [lax.all_gather(grads, group, axis=0, tiled=True)]
    return finish(examples, flat // sharers, gathered, raw)


def solution(mesh):
    in_specs = (
        P(("groups", "dp", "sub"), "mp"),
        P(("groups", "dp", "sub"), "mp"),
        P(("groups", "dp", "sub")),
        P("mp", None),
        P("mp", None),
        P(("mp", "sub"), None),
    )
    out_specs = (P(("groups", "dp", "sub"), None), P(("groups", "dp", "sub"), "mp"))
    return jax.shard_map(
        per_device, mesh=mesh, in_specs=in_specs, out_specs=out_specs, check_vma=False
    )
```

```python
import functools

import jax
import jax.numpy as jnp
from jax import lax
from jax.experimental import pallas as pl
from jax.experimental.pallas import tpu as pltpu
from jax.sharding import PartitionSpec as P

SEQ = 64
DEPTH = 256
SENDS = ((7, 2, 3, 5, 0, 4, 1, 6), (5, 0, 7, 1, 3, 6, 2, 4))
CONTRACT_LAST = (((1,), (1,)), ((), ()))
CONTRACT_FIRST = (((0,), (0,)), ((), ()))


def chunk_of(width):
    return width if width <= 2048 else next(size for size in (1792, 2048, 1024, 512, 256, 128) if width % size == 0)


def tree_sum(terms):
    while len(terms) > 1:
        terms = [a + b for a, b in zip(terms[::2], terms[1::2])] + terms[len(terms) // 2 * 2:]
    return terms[0]


def project_kernel(scales, hidden, out_grad, proj_in, proj_out, out, hid, og, pin, pout, sems):
    k_in = pin.shape[0]
    sides = ((out_grad, proj_out, og, pout), (hidden, proj_in, hid, pin))

    def part_copy(which, n):
        src, _, dst, _ = sides[which]
        size = chunk_of(src.shape[1])
        lanes = pl.ds(n * size if isinstance(n, int) else pl.multiple_of(n * size, size), size)
        return pltpu.make_async_copy(src.at[:, lanes], dst.at[:, lanes], sems.at[which, 1 + n])

    def weight_copy(which):
        return pltpu.make_async_copy(sides[which][1], sides[which][3], sems.at[which, 0])

    counts = [side[0].shape[1] // chunk_of(side[0].shape[1]) for side in sides]
    for which in (0, 1):
        weight_copy(which).start()
        for n in range(counts[which]):
            part_copy(which, n).start()
    for which in (0, 1):
        _, _, dst, dst_w = sides[which]
        size = chunk_of(dst.shape[1])
        depth = min(size, DEPTH)
        weight_copy(which).wait()

        def step(n, total):
            part_copy(which, n).wait()
            terms = []
            for k in range(0, size, depth):
                lanes = pl.ds(pl.multiple_of(n * size + k, depth), depth)
                terms.append(lax.dot_general(dst_w[:, lanes], dst[:, lanes], CONTRACT_LAST,
                                             preferred_element_type=jnp.float32))
            return total + tree_sum(terms)

        zero = jnp.zeros((dst_w.shape[0], dst.shape[0]), jnp.float32)
        total = lax.fori_loop(0, counts[which], step, zero)
        if which == 0:
            out[k_in:] = total * scales[1]
        else:
            out[:k_in] = total * scales[0]


def project(hidden, out_grad, proj_in, proj_out, scales):
    rows, width = hidden.shape
    narrow = out_grad.shape[1]
    k_in, k_out = proj_in.shape[1], proj_out.shape[1]
    return pl.pallas_call(
        functools.partial(project_kernel, scales),
        out_shape=jax.ShapeDtypeStruct((k_in + k_out, rows), jnp.float32),
        in_specs=[pl.BlockSpec(memory_space=pltpu.HBM)] * 4,
        out_specs=pl.BlockSpec(memory_space=pltpu.VMEM),
        scratch_shapes=[
            pltpu.VMEM((rows, width), jnp.bfloat16),
            pltpu.VMEM((rows, narrow), jnp.bfloat16),
            pltpu.VMEM((k_in, width), jnp.bfloat16),
            pltpu.VMEM((k_out, narrow), jnp.bfloat16),
            pltpu.SemaphoreType.DMA((2, 1 + max(width // chunk_of(width), narrow // chunk_of(narrow)))),
        ],
        compiler_params=pltpu.CompilerParams(vmem_limit_bytes=24 << 20),
        cost_estimate=pl.CostEstimate(
            flops=2 * rows * (width * k_in + narrow * k_out),
            bytes_accessed=2 * rows * (width + narrow) + 2 * (width * k_in + narrow * k_out),
            transcendentals=0,
        ),
    )(*(pltpu.with_memory_space_constraint(x, pltpu.HBM) for x in (hidden, out_grad, proj_in.T, proj_out.T)))


def grads_kernel(k_in, scales, mask, *refs):
    *pieces, out = refs
    both = pieces[0][...]
    for piece in pieces[1:]:
        both = both + piece[...]
    rows = both.shape[1]
    act = both[:k_in] * (mask[...] * (1.0 / scales[0]))
    grad = both[k_in:] * (1.0 / scales[1])
    row = lax.broadcasted_iota(jnp.int32, (16, rows), 0)
    col = lax.broadcasted_iota(jnp.int32, (16, rows), 1)
    pick = jnp.where((col >= row * SEQ) & (col < (row + 1) * SEQ), 1.0, 0.0).astype(jnp.bfloat16)
    per = 8
    k_out = grad.shape[0]
    for at in range(0, k_in, per):
        rest = jnp.concatenate([act[i:i + 1] * grad for i in range(at, at + per)], axis=0)
        total = None
        for _ in range(2):
            high = rest.astype(jnp.bfloat16)
            rest = rest - high.astype(jnp.float32)
            part = lax.dot_general(pick, high, CONTRACT_LAST, preferred_element_type=jnp.float32)
            total = part if total is None else total + part
        out[:, at * k_out:(at + per) * k_out] = total[:out.shape[0]].astype(jnp.bfloat16)


def example_grads(mask, pieces, k_in, k_out, scales):
    vmem = pl.BlockSpec(memory_space=pltpu.VMEM)
    return pl.pallas_call(
        functools.partial(grads_kernel, k_in, scales),
        out_shape=jax.ShapeDtypeStruct((mask.shape[1] // SEQ, k_in * k_out), jnp.bfloat16),
        in_specs=[vmem] * (1 + len(pieces)),
        out_specs=vmem,
        compiler_params=pltpu.CompilerParams(vmem_limit_bytes=6 << 20),
        cost_estimate=pl.CostEstimate(flops=1 << 33, bytes_accessed=0, transcendentals=0),
    )(mask, *pieces)


def finish_kernel(examples, n_pieces, n_raw, *refs):
    pieces, raw = refs[:n_pieces], refs[n_pieces:n_pieces + n_raw]
    cov, scores, block, row, sems = refs[n_pieces + n_raw:]
    own_rows, flat = cov.shape
    place = lax.axis_index(("dp", "sub"))
    every = jnp.concatenate([p[...] for p in pieces], axis=0)
    if own_rows % 128 == 0:
        at = pl.multiple_of(place * own_rows, own_rows)
        own = jnp.concatenate([p[:, pl.ds(at, own_rows)] for p in pieces], axis=0)
    else:
        at = pl.multiple_of((place * own_rows) // 128 * 128, 128)
        wider = jnp.concatenate([p[:, pl.ds(at, 128)] for p in pieces], axis=0)
        own = pltpu.roll(wider.astype(jnp.float32), at - place * own_rows + 128, 1)[:, :own_rows].astype(jnp.bfloat16)
    copies = []
    for n, at in enumerate(range(0, flat, flat // 4)):
        lanes = pl.ds(at, flat // 4)
        block[:, lanes] = lax.dot_general(own, every[:, at:at + flat // 4], CONTRACT_FIRST,
                                          preferred_element_type=jnp.float32) * (1.0 / examples)
        copies.append(pltpu.make_async_copy(block.at[:, lanes], cov.at[:, lanes], sems.at[n]))
        copies[-1].start()
    wide = every.astype(jnp.float32)
    factor = lax.rsqrt(jnp.sum(wide * wide) / examples + 1e-06)
    if n_raw == 2:
        near, far = raw[0][...], raw[1][...]
        first = lax.axis_index("sub") == 0
        half = near.shape[1]
        row[:, :half] = jnp.where(first, near, far) * factor
        row[:, half:] = jnp.where(first, far, near) * factor
    else:
        row[...] = raw[0][...] * factor
    copies.append(pltpu.make_async_copy(row, scores, sems.at[4]))
    copies[-1].start()
    for copy in copies:
        copy.wait()


def finish(examples, own_rows, pieces, raw):
    flat = pieces[0].shape[1]
    vmem = pl.BlockSpec(memory_space=pltpu.VMEM)
    hbm = pl.BlockSpec(memory_space=pltpu.HBM)
    cov = (own_rows, flat)
    scores = (raw[0].shape[0], sum(r.shape[1] for r in raw))
    return pl.pallas_call(
        functools.partial(finish_kernel, examples, len(pieces), len(raw)),
        out_shape=(jax.ShapeDtypeStruct(cov, jnp.float32), jax.ShapeDtypeStruct(scores, jnp.float32)),
        in_specs=[vmem] * (len(pieces) + len(raw)),
        out_specs=(hbm, hbm),
        scratch_shapes=[pltpu.VMEM(cov, jnp.float32), pltpu.VMEM(scores, jnp.float32), pltpu.SemaphoreType.DMA((5,))],
        compiler_params=pltpu.CompilerParams(vmem_limit_bytes=8 << 20),
    )(*pieces, *raw)


def first_arrivals(sends):
    seen = [{chip} for chip in range(len(sends[0]) // 2)]
    flags = []
    for targets in sends:
        bits = 0
        for node, target in enumerate(targets):
            if node // 2 not in seen[target // 2]:
                seen[target // 2].add(node // 2)
                bits |= 1 << target
        flags.append(bits)
    assert all(len(chips) == len(seen) for chips in seen)
    return flags


def per_device(hidden, out_grad, lengths, proj_in, proj_out, test_proj):
    k_in, k_out = proj_in.shape[1], proj_out.shape[1]
    flat = k_in * k_out
    rows = hidden.shape[0]
    group = ("dp", "sub")
    sharers = lax.axis_size(group)
    examples = lengths.shape[0] * sharers
    n_sub = lax.axis_size("sub")

    paired = lax.axis_size("mp") == 2
    scales = (128.0, 4.0) if paired else (1.0, 1.0)
    both = project(hidden, out_grad, proj_in, proj_out, scales)
    if paired:
        sent = lax.optimization_barrier(both.astype(jnp.float16))
        came = lax.ppermute(sent, "mp", [(0, 1), (1, 0)])
        pieces = [sent.astype(jnp.float32), came.astype(jnp.float32)]
    else:
        pieces = [lax.psum(both, "mp")]
    lengths, _ = lax.optimization_barrier((lengths, both))
    slots = jnp.arange(SEQ, dtype=jnp.int32)
    mask = (slots[None, :] < lengths[:, None]).astype(jnp.float32).reshape(1, rows)
    grads = example_grads(mask, pieces, k_in, k_out, scales)

    if n_sub == 2 and lax.axis_size("dp") == 4:
        swap = [(i, i ^ 1) for i in range(sharers)]
        came = lax.ppermute(grads, group, swap)
        held = jnp.concatenate([grads, came], axis=0)
        place = lax.axis_index(group)
        fetched = []
        for targets, kept in reversed(list(zip(SENDS, first_arrivals(SENDS)))):
            block = lax.ppermute(held, group, list(enumerate(targets)))
            fetched.append(jnp.where(((kept >> place) & 1) == 1, block, 0))
        fetched = jnp.concatenate(fetched, axis=0)
        gathered = [held, fetched, lax.ppermute(fetched, group, swap)]
        near = jnp.einsum("ep,qp->eq", grads, test_proj, preferred_element_type=jnp.float32)
        for_other = jnp.einsum("ep,qp->eq", came, test_proj, preferred_element_type=jnp.float32)
        raw = [near, lax.ppermute(for_other, group, swap)]
    else:
        tests = lax.all_gather(test_proj, "sub", axis=0, tiled=True)
        raw = [jnp.einsum("ep,qp->eq", grads, tests, preferred_element_type=jnp.float32)]
        gathered = [lax.all_gather(grads, group, axis=0, tiled=True)]
    return finish(examples, flat // sharers, gathered, raw)


def solution(mesh):
    in_specs = (
        P(("groups", "dp", "sub"), "mp"),
        P(("groups", "dp", "sub"), "mp"),
        P(("groups", "dp", "sub")),
        P("mp", None),
        P("mp", None),
        P(("mp", "sub"), None),
    )
    out_specs = (P(("groups", "dp", "sub"), None), P(("groups", "dp", "sub"), "mp"))
    return jax.shard_map(
        per_device, mesh=mesh, in_specs=in_specs, out_specs=out_specs, check_vma=False
    )
```

```python
import functools

import jax
import jax.numpy as jnp
from jax import lax
from jax.experimental import pallas as pl
from jax.experimental.pallas import tpu as pltpu
from jax.sharding import PartitionSpec as P

SEQ = 64
DEPTH = 256
SWAPPED_SEND = (2, 5, 4, 7, 6, 0, 3, 1)
DIRECT_SEND = (7, 6, 1, 0, 2, 3, 5, 4)
CONTRACT_LAST = (((1,), (1,)), ((), ()))
CONTRACT_FIRST = (((0,), (0,)), ((), ()))


def chunk_of(width):
    return width if width <= 2048 else next(size for size in (1792, 2048, 1024, 512, 256, 128) if width % size == 0)


def tree_sum(terms):
    while len(terms) > 1:
        terms = [a + b for a, b in zip(terms[::2], terms[1::2])] + terms[len(terms) // 2 * 2:]
    return terms[0]


def project_kernel(scales, hidden, out_grad, proj_in, proj_out, out, hid, og, pin, pout, sems):
    k_in = pin.shape[0]
    sides = ((out_grad, proj_out, og, pout), (hidden, proj_in, hid, pin))

    def part_copy(which, n):
        src, _, dst, _ = sides[which]
        size = chunk_of(src.shape[1])
        lanes = pl.ds(n * size if isinstance(n, int) else pl.multiple_of(n * size, size), size)
        return pltpu.make_async_copy(src.at[:, lanes], dst.at[:, lanes], sems.at[which, 1 + n])

    def weight_copy(which):
        return pltpu.make_async_copy(sides[which][1], sides[which][3], sems.at[which, 0])

    counts = [side[0].shape[1] // chunk_of(side[0].shape[1]) for side in sides]
    for which in (0, 1):
        weight_copy(which).start()
        for n in range(counts[which]):
            part_copy(which, n).start()
    for which in (0, 1):
        _, _, dst, dst_w = sides[which]
        size = chunk_of(dst.shape[1])
        depth = min(size, DEPTH)
        weight_copy(which).wait()

        def step(n, total):
            part_copy(which, n).wait()
            terms = []
            for k in range(0, size, depth):
                lanes = pl.ds(pl.multiple_of(n * size + k, depth), depth)
                terms.append(lax.dot_general(dst_w[:, lanes], dst[:, lanes], CONTRACT_LAST,
                                             preferred_element_type=jnp.float32))
            return total + tree_sum(terms)

        zero = jnp.zeros((dst_w.shape[0], dst.shape[0]), jnp.float32)
        total = lax.fori_loop(0, counts[which], step, zero)
        if which == 0:
            out[k_in:] = total * scales[1]
        else:
            out[:k_in] = total * scales[0]


def project(hidden, out_grad, proj_in, proj_out, scales):
    rows, width = hidden.shape
    narrow = out_grad.shape[1]
    k_in, k_out = proj_in.shape[1], proj_out.shape[1]
    return pl.pallas_call(
        functools.partial(project_kernel, scales),
        out_shape=jax.ShapeDtypeStruct((k_in + k_out, rows), jnp.float32),
        in_specs=[pl.BlockSpec(memory_space=pltpu.HBM)] * 4,
        out_specs=pl.BlockSpec(memory_space=pltpu.VMEM),
        scratch_shapes=[
            pltpu.VMEM((rows, width), jnp.bfloat16),
            pltpu.VMEM((rows, narrow), jnp.bfloat16),
            pltpu.VMEM((k_in, width), jnp.bfloat16),
            pltpu.VMEM((k_out, narrow), jnp.bfloat16),
            pltpu.SemaphoreType.DMA((2, 1 + max(width // chunk_of(width), narrow // chunk_of(narrow)))),
        ],
        compiler_params=pltpu.CompilerParams(vmem_limit_bytes=24 << 20),
        cost_estimate=pl.CostEstimate(
            flops=2 * rows * (width * k_in + narrow * k_out),
            bytes_accessed=2 * rows * (width + narrow) + 2 * (width * k_in + narrow * k_out),
            transcendentals=0,
        ),
    )(*(pltpu.with_memory_space_constraint(x, pltpu.HBM) for x in (hidden, out_grad, proj_in.T, proj_out.T)))


def grads_kernel(k_in, scales, mask, *refs):
    *pieces, out = refs
    both = pieces[0][...]
    for piece in pieces[1:]:
        both = both + piece[...]
    rows = both.shape[1]
    act = both[:k_in] * (mask[...] * (1.0 / scales[0]))
    grad = both[k_in:] * (1.0 / scales[1])
    row = lax.broadcasted_iota(jnp.int32, (16, rows), 0)
    col = lax.broadcasted_iota(jnp.int32, (16, rows), 1)
    pick = jnp.where((col >= row * SEQ) & (col < (row + 1) * SEQ), 1.0, 0.0).astype(jnp.bfloat16)
    per = 8
    k_out = grad.shape[0]
    for at in range(0, k_in, per):
        rest = jnp.concatenate([act[i:i + 1] * grad for i in range(at, at + per)], axis=0)
        total = None
        for _ in range(2):
            high = rest.astype(jnp.bfloat16)
            rest = rest - high.astype(jnp.float32)
            part = lax.dot_general(pick, high, CONTRACT_LAST, preferred_element_type=jnp.float32)
            total = part if total is None else total + part
        out[:, at * k_out:(at + per) * k_out] = total[:out.shape[0]].astype(jnp.bfloat16)


def example_grads(mask, pieces, k_in, k_out, scales):
    vmem = pl.BlockSpec(memory_space=pltpu.VMEM)
    return pl.pallas_call(
        functools.partial(grads_kernel, k_in, scales),
        out_shape=jax.ShapeDtypeStruct((mask.shape[1] // SEQ, k_in * k_out), jnp.bfloat16),
        in_specs=[vmem] * (1 + len(pieces)),
        out_specs=vmem,
        compiler_params=pltpu.CompilerParams(vmem_limit_bytes=6 << 20),
        cost_estimate=pl.CostEstimate(flops=1 << 33, bytes_accessed=0, transcendentals=0),
    )(mask, *pieces)


def finish_kernel(examples, n_pieces, n_raw, *refs):
    pieces, raw = refs[:n_pieces], refs[n_pieces:n_pieces + n_raw]
    cov, scores, block, row, sems = refs[n_pieces + n_raw:]
    own_rows, flat = cov.shape
    place = lax.axis_index(("dp", "sub"))
    every = jnp.concatenate([p[...] for p in pieces], axis=0)
    if own_rows % 128 == 0:
        at = pl.multiple_of(place * own_rows, own_rows)
        own = jnp.concatenate([p[:, pl.ds(at, own_rows)] for p in pieces], axis=0)
    else:
        at = pl.multiple_of((place * own_rows) // 128 * 128, 128)
        wider = jnp.concatenate([p[:, pl.ds(at, 128)] for p in pieces], axis=0)
        own = pltpu.roll(wider.astype(jnp.float32), at - place * own_rows + 128, 1)[:, :own_rows].astype(jnp.bfloat16)
    copies = []
    for n, at in enumerate(range(0, flat, flat // 4)):
        lanes = pl.ds(at, flat // 4)
        block[:, lanes] = lax.dot_general(own, every[:, at:at + flat // 4], CONTRACT_FIRST,
                                          preferred_element_type=jnp.float32) * (1.0 / examples)
        copies.append(pltpu.make_async_copy(block.at[:, lanes], cov.at[:, lanes], sems.at[n]))
        copies[-1].start()
    wide = every.astype(jnp.float32)
    factor = lax.rsqrt(jnp.sum(wide * wide) / examples + 1e-06)
    if n_raw == 2:
        near, far = raw[0][...], raw[1][...]
        first = lax.axis_index("sub") == 0
        half = near.shape[1]
        row[:, :half] = jnp.where(first, near, far) * factor
        row[:, half:] = jnp.where(first, far, near) * factor
    else:
        row[...] = raw[0][...] * factor
    copies.append(pltpu.make_async_copy(row, scores, sems.at[4]))
    copies[-1].start()
    for copy in copies:
        copy.wait()


def finish(examples, own_rows, pieces, raw):
    flat = pieces[0].shape[1]
    vmem = pl.BlockSpec(memory_space=pltpu.VMEM)
    hbm = pl.BlockSpec(memory_space=pltpu.HBM)
    cov = (own_rows, flat)
    scores = (raw[0].shape[0], sum(r.shape[1] for r in raw))
    return pl.pallas_call(
        functools.partial(finish_kernel, examples, len(pieces), len(raw)),
        out_shape=(jax.ShapeDtypeStruct(cov, jnp.float32), jax.ShapeDtypeStruct(scores, jnp.float32)),
        in_specs=[vmem] * (len(pieces) + len(raw)),
        out_specs=(hbm, hbm),
        scratch_shapes=[pltpu.VMEM(cov, jnp.float32), pltpu.VMEM(scores, jnp.float32), pltpu.SemaphoreType.DMA((5,))],
        compiler_params=pltpu.CompilerParams(vmem_limit_bytes=8 << 20),
    )(*pieces, *raw)


def per_device(hidden, out_grad, lengths, proj_in, proj_out, test_proj):
    k_in, k_out = proj_in.shape[1], proj_out.shape[1]
    flat = k_in * k_out
    rows = hidden.shape[0]
    group = ("dp", "sub")
    sharers = lax.axis_size(group)
    examples = lengths.shape[0] * sharers
    n_sub = lax.axis_size("sub")

    paired = lax.axis_size("mp") == 2
    scales = (128.0, 4.0) if paired else (1.0, 1.0)
    both = project(hidden, out_grad, proj_in, proj_out, scales)
    if paired:
        sent = lax.optimization_barrier(both.astype(jnp.float16))
        came = lax.ppermute(sent, "mp", [(0, 1), (1, 0)])
        pieces = [sent.astype(jnp.float32), came.astype(jnp.float32)]
    else:
        pieces = [lax.psum(both, "mp")]
    lengths, _ = lax.optimization_barrier((lengths, both))
    slots = jnp.arange(SEQ, dtype=jnp.int32)
    mask = (slots[None, :] < lengths[:, None]).astype(jnp.float32).reshape(1, rows)
    grads = example_grads(mask, pieces, k_in, k_out, scales)

    if n_sub == 2 and lax.axis_size("dp") == 4:
        swap = [(i, i ^ 1) for i in range(sharers)]
        came = lax.ppermute(grads, group, swap)
        held = jnp.concatenate([grads, came], axis=0)
        direct = lax.ppermute(held, group, list(enumerate(DIRECT_SEND)))
        fetched = lax.ppermute(held, group, list(enumerate(SWAPPED_SEND)))
        gathered = [held, direct, fetched, lax.ppermute(fetched, group, swap)]
        near = jnp.einsum("ep,qp->eq", grads, test_proj, preferred_element_type=jnp.float32)
        for_other = jnp.einsum("ep,qp->eq", came, test_proj, preferred_element_type=jnp.float32)
        raw = [near, lax.ppermute(for_other, group, swap)]
    else:
        tests = lax.all_gather(test_proj, "sub", axis=0, tiled=True)
        raw = [jnp.einsum("ep,qp->eq", grads, tests, preferred_element_type=jnp.float32)]
        gathered = [lax.all_gather(grads, group, axis=0, tiled=True)]
    return finish(examples, flat // sharers, gathered, raw)


def solution(mesh):
    in_specs = (
        P(("groups", "dp", "sub"), "mp"),
        P(("groups", "dp", "sub"), "mp"),
        P(("groups", "dp", "sub")),
        P("mp", None),
        P("mp", None),
        P(("mp", "sub"), None),
    )
    out_specs = (P(("groups", "dp", "sub"), None), P(("groups", "dp", "sub"), "mp"))
    return jax.shard_map(
        per_device, mesh=mesh, in_specs=in_specs, out_specs=out_specs, check_vma=False
    )
```

```python
import functools

import jax
import jax.numpy as jnp
from jax import lax
from jax.experimental import pallas as pl
from jax.experimental.pallas import tpu as pltpu
from jax.sharding import PartitionSpec as P

SEQ = 64
DEPTH = 256
SWAPPED_SEND = (2, 5, 4, 7, 6, 0, 3, 1)
DIRECT_SEND = (7, 6, 1, 0, 2, 3, 5, 4)
CONTRACT_LAST = (((1,), (1,)), ((), ()))
CONTRACT_FIRST = (((0,), (0,)), ((), ()))


def first_chunk(width):
    small = width // 7
    return small if width % 7 == 0 and small % 128 == 0 else 0


def tree_sum(terms):
    while len(terms) > 1:
        terms = [a + b for a, b in zip(terms[::2], terms[1::2])] + terms[len(terms) // 2 * 2:]
    return terms[0]


def project_kernel(scales, hidden, out_grad, lengths, proj_in, proj_out, out, hid, og, pin, pout, limits, sems):
    rows, width = hidden.shape
    k_in = pin.shape[0]
    small = first_chunk(width)
    half = (width - small) // 2

    def copies_of(n):
        if isinstance(n, int) and n == 0:
            lanes = pl.ds(0, small)
        elif isinstance(n, int) and n == 1:
            return [pltpu.make_async_copy(proj_out, pout, sems.at[0, 1]), pltpu.make_async_copy(out_grad, og, sems.at[1, 1])]
        else:
            lanes = pl.ds(small + (n - 2) * half, half)
        return [
            pltpu.make_async_copy(proj_in.at[:, lanes], pin.at[:, lanes], sems.at[0, n]),
            pltpu.make_async_copy(hidden.at[:, lanes], hid.at[:, lanes], sems.at[1, n]),
        ]

    def partial(weights, data, at, size):
        depth = min(size, DEPTH)
        terms = []
        for k in range(0, size, depth):
            lanes = pl.ds(at + k if isinstance(at, int) else pl.multiple_of(at + k, 128), depth)
            terms.append(lax.dot_general(weights[:, lanes], data[:, lanes], CONTRACT_LAST,
                                         preferred_element_type=jnp.float32))
        return tree_sum(terms)

    steps = range(0 if small else 1, 4)
    for n in steps:
        for copy in copies_of(n):
            copy.start()
    bounds = pltpu.make_async_copy(lengths, limits, sems.at[0, 4])
    bounds.start()
    total = jnp.zeros((k_in, rows), jnp.float32)
    if small:
        for copy in copies_of(0):
            copy.wait()
        total = partial(pin, hid, 0, small)
    for copy in copies_of(1):
        copy.wait()
    out[k_in:] = partial(pout, og, 0, og.shape[1]) * scales[1]

    def step(n, total):
        for copy in copies_of(n):
            copy.wait()
        return total + partial(pin, hid, small + (n - 2) * half, half)

    total = lax.fori_loop(2, 4, step, total)
    bounds.wait()
    slot = lax.broadcasted_iota(jnp.int32, (1, rows), 1)
    limit = jnp.zeros((1, rows), jnp.int32)
    for e in range(lengths.shape[0]):
        limit = jnp.where(slot >= e * SEQ, e * SEQ + limits[e], limit)
    out[:k_in] = jnp.where(slot < limit, total * scales[0], 0.0)


def project(hidden, out_grad, lengths, proj_in, proj_out, scales):
    rows, width = hidden.shape
    narrow = out_grad.shape[1]
    k_in, k_out = proj_in.shape[1], proj_out.shape[1]
    operands = (hidden, out_grad, lengths, proj_in.T, proj_out.T)
    return pl.pallas_call(
        functools.partial(project_kernel, scales),
        out_shape=jax.ShapeDtypeStruct((k_in + k_out, rows), jnp.float32),
        in_specs=[pl.BlockSpec(memory_space=pltpu.HBM)] * 5,
        out_specs=pl.BlockSpec(memory_space=pltpu.VMEM),
        scratch_shapes=[
            pltpu.VMEM((rows, width), jnp.bfloat16),
            pltpu.VMEM((rows, narrow), jnp.bfloat16),
            pltpu.VMEM((k_in, width), jnp.bfloat16),
            pltpu.VMEM((k_out, narrow), jnp.bfloat16),
            pltpu.SMEM(lengths.shape, jnp.int32),
            pltpu.SemaphoreType.DMA((2, 5)),
        ],
        compiler_params=pltpu.CompilerParams(vmem_limit_bytes=24 << 20),
        cost_estimate=pl.CostEstimate(
            flops=2 * rows * (width * k_in + narrow * k_out),
            bytes_accessed=2 * rows * (width + narrow) + 2 * (width * k_in + narrow * k_out),
            transcendentals=0,
        ),
    )(*(pltpu.with_memory_space_constraint(x, pltpu.HBM) for x in operands))


def grads_kernel(k_in, scales, *refs):
    *pieces, out = refs
    both = pieces[0][...]
    for piece in pieces[1:]:
        both = both + piece[...]
    rows = both.shape[1]
    act = both[:k_in] * (1.0 / scales[0])
    grad = both[k_in:] * (1.0 / scales[1])
    row = lax.broadcasted_iota(jnp.int32, (16, rows), 0)
    col = lax.broadcasted_iota(jnp.int32, (16, rows), 1)
    pick = jnp.where((col >= row * SEQ) & (col < (row + 1) * SEQ), 1.0, 0.0).astype(jnp.bfloat16)
    per = 8
    k_out = grad.shape[0]
    for at in range(0, k_in, per):
        rest = jnp.concatenate([act[i:i + 1] * grad for i in range(at, at + per)], axis=0)
        total = None
        for _ in range(2):
            high = rest.astype(jnp.bfloat16)
            rest = rest - high.astype(jnp.float32)
            part = lax.dot_general(pick, high, CONTRACT_LAST, preferred_element_type=jnp.float32)
            total = part if total is None else total + part
        out[:, at * k_out:(at + per) * k_out] = total[:out.shape[0]].astype(jnp.bfloat16)


def example_grads(pieces, k_in, k_out, scales):
    vmem = pl.BlockSpec(memory_space=pltpu.VMEM)
    return pl.pallas_call(
        functools.partial(grads_kernel, k_in, scales),
        out_shape=jax.ShapeDtypeStruct((pieces[0].shape[1] // SEQ, k_in * k_out), jnp.bfloat16),
        in_specs=[vmem] * len(pieces),
        out_specs=vmem,
        compiler_params=pltpu.CompilerParams(vmem_limit_bytes=6 << 20),
        cost_estimate=pl.CostEstimate(flops=1 << 33, bytes_accessed=0, transcendentals=0),
    )(*pieces)


def finish_kernel(examples, n_pieces, n_raw, *refs):
    pieces, raw = refs[:n_pieces], refs[n_pieces:n_pieces + n_raw]
    cov, scores, block, row, sems = refs[n_pieces + n_raw:]
    own_rows, flat = cov.shape
    place = lax.axis_index(("dp", "sub"))
    every = jnp.concatenate([p[...] for p in pieces], axis=0)
    if own_rows % 128 == 0:
        at = pl.multiple_of(place * own_rows, own_rows)
        own = jnp.concatenate([p[:, pl.ds(at, own_rows)] for p in pieces], axis=0)
    else:
        at = pl.multiple_of((place * own_rows) // 128 * 128, 128)
        wider = jnp.concatenate([p[:, pl.ds(at, 128)] for p in pieces], axis=0)
        own = pltpu.roll(wider.astype(jnp.float32), at - place * own_rows + 128, 1)[:, :own_rows].astype(jnp.bfloat16)
    copies = []
    for n, at in enumerate(range(0, flat, flat // 4)):
        lanes = pl.ds(at, flat // 4)
        block[:, lanes] = lax.dot_general(own, every[:, at:at + flat // 4], CONTRACT_FIRST,
                                          preferred_element_type=jnp.float32) * (1.0 / examples)
        copies.append(pltpu.make_async_copy(block.at[:, lanes], cov.at[:, lanes], sems.at[n]))
        copies[-1].start()
    wide = every.astype(jnp.float32)
    factor = lax.rsqrt(jnp.sum(wide * wide) / examples + 1e-06)
    if n_raw == 2:
        near, far = raw[0][...], raw[1][...]
        first = lax.axis_index("sub") == 0
        half = near.shape[1]
        row[:, :half] = jnp.where(first, near, far) * factor
        row[:, half:] = jnp.where(first, far, near) * factor
    else:
        row[...] = raw[0][...] * factor
    copies.append(pltpu.make_async_copy(row, scores, sems.at[4]))
    copies[-1].start()
    for copy in copies:
        copy.wait()


def finish(examples, own_rows, pieces, raw):
    flat = pieces[0].shape[1]
    vmem = pl.BlockSpec(memory_space=pltpu.VMEM)
    hbm = pl.BlockSpec(memory_space=pltpu.HBM)
    cov = (own_rows, flat)
    scores = (raw[0].shape[0], sum(r.shape[1] for r in raw))
    return pl.pallas_call(
        functools.partial(finish_kernel, examples, len(pieces), len(raw)),
        out_shape=(jax.ShapeDtypeStruct(cov, jnp.float32), jax.ShapeDtypeStruct(scores, jnp.float32)),
        in_specs=[vmem] * (len(pieces) + len(raw)),
        out_specs=(hbm, hbm),
        scratch_shapes=[pltpu.VMEM(cov, jnp.float32), pltpu.VMEM(scores, jnp.float32), pltpu.SemaphoreType.DMA((5,))],
        compiler_params=pltpu.CompilerParams(vmem_limit_bytes=8 << 20),
    )(*pieces, *raw)


def per_device(hidden, out_grad, lengths, proj_in, proj_out, test_proj):
    k_in, k_out = proj_in.shape[1], proj_out.shape[1]
    flat = k_in * k_out
    group = ("dp", "sub")
    sharers = lax.axis_size(group)
    examples = lengths.shape[0] * sharers
    crossed = lax.axis_size("mp") == 2 and lax.axis_size("sub") == 2
    scales = (128.0, 4.0) if crossed else (1.0, 1.0)
    both = project(hidden, out_grad, lengths, proj_in, proj_out, scales)
    if crossed:
        sent = lax.optimization_barrier(both.astype(jnp.float16))
        far = lax.ppermute(sent, ("mp", "sub"), [(0, 3), (1, 2), (2, 1), (3, 0)])
        near = lax.ppermute(sent, "sub", [(0, 1), (1, 0)])
        made = example_grads([near.astype(jnp.float32), far.astype(jnp.float32)], k_in, k_out, scales)
        grads = lax.ppermute(made, "sub", [(0, 1), (1, 0)])
    else:
        grads = example_grads([lax.psum(both, "mp")], k_in, k_out, scales)

    if crossed and lax.axis_size("dp") == 4:
        swap = [(i, i ^ 1) for i in range(sharers)]
        for_other = jnp.einsum("ep,qp->eq", made, test_proj, preferred_element_type=jnp.float32)
        grads, for_other = lax.optimization_barrier((grads, for_other))
        held = jnp.concatenate([made, grads], axis=0)
        fetched = lax.ppermute(held, group, list(enumerate(SWAPPED_SEND)))
        direct = lax.ppermute(held, group, list(enumerate(DIRECT_SEND)))
        gathered = [held, direct, fetched, lax.ppermute(fetched, group, swap)]
        own = jnp.einsum("ep,qp->eq", grads, test_proj, preferred_element_type=jnp.float32)
        raw = [own, lax.ppermute(for_other, group, swap)]
    else:
        tests = lax.all_gather(test_proj, "sub", axis=0, tiled=True)
        raw = [jnp.einsum("ep,qp->eq", grads, tests, preferred_element_type=jnp.float32)]
        gathered = [lax.all_gather(grads, group, axis=0, tiled=True)]
    return finish(examples, flat // sharers, gathered, raw)


def solution(mesh):
    in_specs = (
        P(("groups", "dp", "sub"), "mp"),
        P(("groups", "dp", "sub"), "mp"),
        P(("groups", "dp", "sub")),
        P("mp", None),
        P("mp", None),
        P(("mp", "sub"), None),
    )
    out_specs = (P(("groups", "dp", "sub"), None), P(("groups", "dp", "sub"), "mp"))
    return jax.shard_map(
        per_device, mesh=mesh, in_specs=in_specs, out_specs=out_specs, check_vma=False
    )
```

```python
import functools

import jax
import jax.numpy as jnp
from jax import lax
from jax.experimental import pallas as pl
from jax.experimental.pallas import tpu as pltpu
from jax.sharding import PartitionSpec as P

SEQ = 64
DEPTH = 256
SWAPPED_SEND = (2, 5, 4, 7, 6, 0, 3, 1)
DIRECT_SEND = (7, 6, 1, 0, 2, 3, 5, 4)
CONTRACT_LAST = (((1,), (1,)), ((), ()))
CONTRACT_FIRST = (((0,), (0,)), ((), ()))


def first_chunk(width):
    small = width // 7
    return small if width % 7 == 0 and small % 128 == 0 else 0


def tree_sum(terms):
    while len(terms) > 1:
        terms = [a + b for a, b in zip(terms[::2], terms[1::2])] + terms[len(terms) // 2 * 2:]
    return terms[0]


def project_kernel(scales, hidden, out_grad, lengths, proj_in, proj_out, out, hid, og, pin, pout, limits, sems):
    rows, width = hidden.shape
    k_in = pin.shape[0]
    small = first_chunk(width)
    half = (width - small) // 2

    def copies_of(n):
        if isinstance(n, int) and n == 0:
            lanes = pl.ds(0, small)
        elif isinstance(n, int) and n == 1:
            return [pltpu.make_async_copy(proj_out, pout, sems.at[0, 1]), pltpu.make_async_copy(out_grad, og, sems.at[1, 1])]
        else:
            lanes = pl.ds(small + (n - 2) * half, half)
        return [
            pltpu.make_async_copy(proj_in.at[:, lanes], pin.at[:, lanes], sems.at[0, n]),
            pltpu.make_async_copy(hidden.at[:, lanes], hid.at[:, lanes], sems.at[1, n]),
        ]

    def partial(weights, data, at, size):
        depth = min(size, DEPTH)
        terms = [], []
        for n, k in enumerate(range(0, size, depth)):
            lanes = pl.ds(at + k if isinstance(at, int) else pl.multiple_of(at + k, 128), depth)
            left, right = (weights, data) if n % 2 == 0 else (data, weights)
            terms[n % 2].append(lax.dot_general(left[:, lanes], right[:, lanes], CONTRACT_LAST,
                                                preferred_element_type=jnp.float32))
        return tree_sum(terms[0]), tree_sum(terms[1])

    steps = range(0 if small else 1, 4)
    for n in steps:
        for copy in copies_of(n):
            copy.start()
    bounds = pltpu.make_async_copy(lengths, limits, sems.at[0, 4])
    bounds.start()
    act = jnp.zeros((k_in, rows), jnp.float32), jnp.zeros((rows, k_in), jnp.float32)
    if small:
        for copy in copies_of(0):
            copy.wait()
        act = partial(pin, hid, 0, small)
    for copy in copies_of(1):
        copy.wait()
    grad = partial(pout, og, 0, og.shape[1])

    def step(n, act):
        for copy in copies_of(n):
            copy.wait()
        more = partial(pin, hid, small + (n - 2) * half, half)
        return act[0] + more[0], act[1] + more[1]

    act = lax.fori_loop(2, 4, step, act)
    turned = jnp.concatenate([act[1], grad[1]], axis=1).T
    total = act[0] + turned[:k_in]
    out[k_in:] = (grad[0] + turned[k_in:]) * scales[1]
    bounds.wait()
    slot = lax.broadcasted_iota(jnp.int32, (1, rows), 1)
    limit = jnp.zeros((1, rows), jnp.int32)
    for e in range(lengths.shape[0]):
        limit = jnp.where(slot >= e * SEQ, e * SEQ + limits[e], limit)
    out[:k_in] = jnp.where(slot < limit, total * scales[0], 0.0)


def project(hidden, out_grad, lengths, proj_in, proj_out, scales):
    rows, width = hidden.shape
    narrow = out_grad.shape[1]
    k_in, k_out = proj_in.shape[1], proj_out.shape[1]
    operands = (hidden, out_grad, lengths, proj_in.T, proj_out.T)
    return pl.pallas_call(
        functools.partial(project_kernel, scales),
        out_shape=jax.ShapeDtypeStruct((k_in + k_out, rows), jnp.float32),
        in_specs=[pl.BlockSpec(memory_space=pltpu.HBM)] * 5,
        out_specs=pl.BlockSpec(memory_space=pltpu.VMEM),
        scratch_shapes=[
            pltpu.VMEM((rows, width), jnp.bfloat16),
            pltpu.VMEM((rows, narrow), jnp.bfloat16),
            pltpu.VMEM((k_in, width), jnp.bfloat16),
            pltpu.VMEM((k_out, narrow), jnp.bfloat16),
            pltpu.SMEM(lengths.shape, jnp.int32),
            pltpu.SemaphoreType.DMA((2, 5)),
        ],
        compiler_params=pltpu.CompilerParams(vmem_limit_bytes=24 << 20),
        cost_estimate=pl.CostEstimate(
            flops=2 * rows * (width * k_in + narrow * k_out),
            bytes_accessed=2 * rows * (width + narrow) + 2 * (width * k_in + narrow * k_out),
            transcendentals=0,
        ),
    )(*(pltpu.with_memory_space_constraint(x, pltpu.HBM) for x in operands))


def grads_kernel(k_in, scales, *refs):
    *pieces, out = refs
    both = pieces[0][...]
    for piece in pieces[1:]:
        both = both + piece[...]
    rows = both.shape[1]
    act = both[:k_in] * (1.0 / scales[0])
    grad = both[k_in:] * (1.0 / scales[1])
    row = lax.broadcasted_iota(jnp.int32, (16, rows), 0)
    col = lax.broadcasted_iota(jnp.int32, (16, rows), 1)
    pick = jnp.where((col >= row * SEQ) & (col < (row + 1) * SEQ), 1.0, 0.0).astype(jnp.bfloat16)
    per = 8
    k_out = grad.shape[0]
    for at in range(0, k_in, per):
        rest = jnp.concatenate([act[i:i + 1] * grad for i in range(at, at + per)], axis=0)
        total = None
        for _ in range(2):
            high = rest.astype(jnp.bfloat16)
            rest = rest - high.astype(jnp.float32)
            part = lax.dot_general(pick, high, CONTRACT_LAST, preferred_element_type=jnp.float32)
            total = part if total is None else total + part
        out[:, at * k_out:(at + per) * k_out] = total[:out.shape[0]].astype(jnp.bfloat16)


def example_grads(pieces, k_in, k_out, scales):
    vmem = pl.BlockSpec(memory_space=pltpu.VMEM)
    return pl.pallas_call(
        functools.partial(grads_kernel, k_in, scales),
        out_shape=jax.ShapeDtypeStruct((pieces[0].shape[1] // SEQ, k_in * k_out), jnp.bfloat16),
        in_specs=[vmem] * len(pieces),
        out_specs=vmem,
        compiler_params=pltpu.CompilerParams(vmem_limit_bytes=6 << 20),
        cost_estimate=pl.CostEstimate(flops=1 << 33, bytes_accessed=0, transcendentals=0),
    )(*pieces)


def finish_kernel(examples, n_pieces, n_raw, *refs):
    pieces, raw = refs[:n_pieces], refs[n_pieces:n_pieces + n_raw]
    cov, scores, block, row, sems = refs[n_pieces + n_raw:]
    own_rows, flat = cov.shape
    place = lax.axis_index(("dp", "sub"))
    every = jnp.concatenate([p[...] for p in pieces], axis=0)
    if own_rows % 128 == 0:
        at = pl.multiple_of(place * own_rows, own_rows)
        own = jnp.concatenate([p[:, pl.ds(at, own_rows)] for p in pieces], axis=0)
    else:
        at = pl.multiple_of((place * own_rows) // 128 * 128, 128)
        wider = jnp.concatenate([p[:, pl.ds(at, 128)] for p in pieces], axis=0)
        own = pltpu.roll(wider.astype(jnp.float32), at - place * own_rows + 128, 1)[:, :own_rows].astype(jnp.bfloat16)
    copies = []
    for n, at in enumerate(range(0, flat, flat // 4)):
        lanes = pl.ds(at, flat // 4)
        block[:, lanes] = lax.dot_general(own, every[:, at:at + flat // 4], CONTRACT_FIRST,
                                          preferred_element_type=jnp.float32) * (1.0 / examples)
        copies.append(pltpu.make_async_copy(block.at[:, lanes], cov.at[:, lanes], sems.at[n]))
        copies[-1].start()
    wide = every.astype(jnp.float32)
    factor = lax.rsqrt(jnp.sum(wide * wide) / examples + 1e-06)
    if n_raw == 2:
        near, far = raw[0][...], raw[1][...]
        first = lax.axis_index("sub") == 0
        half = near.shape[1]
        row[:, :half] = jnp.where(first, near, far) * factor
        row[:, half:] = jnp.where(first, far, near) * factor
    else:
        row[...] = raw[0][...] * factor
    copies.append(pltpu.make_async_copy(row, scores, sems.at[4]))
    copies[-1].start()
    for copy in copies:
        copy.wait()


def finish(examples, own_rows, pieces, raw):
    flat = pieces[0].shape[1]
    vmem = pl.BlockSpec(memory_space=pltpu.VMEM)
    hbm = pl.BlockSpec(memory_space=pltpu.HBM)
    cov = (own_rows, flat)
    scores = (raw[0].shape[0], sum(r.shape[1] for r in raw))
    return pl.pallas_call(
        functools.partial(finish_kernel, examples, len(pieces), len(raw)),
        out_shape=(jax.ShapeDtypeStruct(cov, jnp.float32), jax.ShapeDtypeStruct(scores, jnp.float32)),
        in_specs=[vmem] * (len(pieces) + len(raw)),
        out_specs=(hbm, hbm),
        scratch_shapes=[pltpu.VMEM(cov, jnp.float32), pltpu.VMEM(scores, jnp.float32), pltpu.SemaphoreType.DMA((5,))],
        compiler_params=pltpu.CompilerParams(vmem_limit_bytes=8 << 20),
    )(*pieces, *raw)


def per_device(hidden, out_grad, lengths, proj_in, proj_out, test_proj):
    k_in, k_out = proj_in.shape[1], proj_out.shape[1]
    flat = k_in * k_out
    group = ("dp", "sub")
    sharers = lax.axis_size(group)
    examples = lengths.shape[0] * sharers
    crossed = lax.axis_size("mp") == 2 and lax.axis_size("sub") == 2
    scales = (128.0, 4.0) if crossed else (1.0, 1.0)
    both = project(hidden, out_grad, lengths, proj_in, proj_out, scales)
    if crossed:
        sent = lax.optimization_barrier(both.astype(jnp.float16))
        far = lax.ppermute(sent, ("mp", "sub"), [(0, 3), (1, 2), (2, 1), (3, 0)])
        near = lax.ppermute(sent, "sub", [(0, 1), (1, 0)])
        made = example_grads([near.astype(jnp.float32), far.astype(jnp.float32)], k_in, k_out, scales)
        grads = lax.ppermute(made, "sub", [(0, 1), (1, 0)])
    else:
        grads = example_grads([lax.psum(both, "mp")], k_in, k_out, scales)

    if crossed and lax.axis_size("dp") == 4:
        swap = [(i, i ^ 1) for i in range(sharers)]
        for_other = jnp.einsum("ep,qp->eq", made, test_proj, preferred_element_type=jnp.float32)
        grads, for_other = lax.optimization_barrier((grads, for_other))
        held = jnp.concatenate([made, grads], axis=0)
        fetched = lax.ppermute(held, group, list(enumerate(SWAPPED_SEND)))
        direct = lax.ppermute(held, group, list(enumerate(DIRECT_SEND)))
        gathered = [held, direct, fetched, lax.ppermute(fetched, group, swap)]
        own = jnp.einsum("ep,qp->eq", grads, test_proj, preferred_element_type=jnp.float32)
        raw = [own, lax.ppermute(for_other, group, swap)]
    else:
        tests = lax.all_gather(test_proj, "sub", axis=0, tiled=True)
        raw = [jnp.einsum("ep,qp->eq", grads, tests, preferred_element_type=jnp.float32)]
        gathered = [lax.all_gather(grads, group, axis=0, tiled=True)]
    return finish(examples, flat // sharers, gathered, raw)


def solution(mesh):
    in_specs = (
        P(("groups", "dp", "sub"), "mp"),
        P(("groups", "dp", "sub"), "mp"),
        P(("groups", "dp", "sub")),
        P("mp", None),
        P("mp", None),
        P(("mp", "sub"), None),
    )
    out_specs = (P(("groups", "dp", "sub"), None), P(("groups", "dp", "sub"), "mp"))
    return jax.shard_map(
        per_device, mesh=mesh, in_specs=in_specs, out_specs=out_specs, check_vma=False
    )
```

```python
import functools

import jax
import jax.numpy as jnp
from jax import lax
from jax.experimental import pallas as pl
from jax.experimental.pallas import tpu as pltpu
from jax.sharding import PartitionSpec as P

SEQ = 64
DEPTH = 256
SWAPPED_SEND = (2, 5, 4, 7, 6, 0, 3, 1)
DIRECT_SEND = (7, 6, 1, 0, 2, 3, 5, 4)
CONTRACT_LAST = (((1,), (1,)), ((), ()))
CONTRACT_FIRST = (((0,), (0,)), ((), ()))


def first_chunk(width):
    small = width // 7
    return small if width % 7 == 0 and small % 128 == 0 else 0


def tree_sum(terms):
    while len(terms) > 1:
        terms = [a + b for a, b in zip(terms[::2], terms[1::2])] + terms[len(terms) // 2 * 2:]
    return terms[0]


def project_kernel(scales, hidden, out_grad, lengths, proj_in, proj_out, out, hid, og, pin, pout, limits, sems):
    rows, width = hidden.shape
    k_in = pin.shape[0]
    small = first_chunk(width)
    half = (width - small) // 2

    def copies_of(n):
        if isinstance(n, int) and n == 0:
            lanes = pl.ds(0, small)
        elif isinstance(n, int) and n == 1:
            return [pltpu.make_async_copy(proj_out, pout, sems.at[0, 1]), pltpu.make_async_copy(out_grad, og, sems.at[1, 1])]
        else:
            lanes = pl.ds(small + (n - 2) * half, half)
        return [
            pltpu.make_async_copy(proj_in.at[:, lanes], pin.at[:, lanes], sems.at[0, n]),
            pltpu.make_async_copy(hidden.at[:, lanes], hid.at[:, lanes], sems.at[1, n]),
        ]

    def partial(weights, data, at, size):
        depth = min(size, DEPTH)
        terms = []
        for k in range(0, size, depth):
            lanes = pl.ds(at + k if isinstance(at, int) else pl.multiple_of(at + k, 128), depth)
            terms.append(lax.dot_general(weights[:, lanes], data[:, lanes], CONTRACT_LAST,
                                         preferred_element_type=jnp.float32))
        return tree_sum(terms)

    steps = range(0 if small else 1, 4)
    for n in steps:
        for copy in copies_of(n):
            copy.start()
    bounds = pltpu.make_async_copy(lengths, limits, sems.at[0, 4])
    bounds.start()
    total = jnp.zeros((k_in, rows), jnp.float32)
    if small:
        for copy in copies_of(0):
            copy.wait()
        total = partial(pin, hid, 0, small)
    for copy in copies_of(1):
        copy.wait()
    out[k_in:] = partial(pout, og, 0, og.shape[1]) * scales[1]

    def step(n, total):
        for copy in copies_of(n):
            copy.wait()
        return total + partial(pin, hid, small + (n - 2) * half, half)

    total = lax.fori_loop(2, 4, step, total)
    bounds.wait()
    slot = lax.broadcasted_iota(jnp.int32, (1, rows), 1)
    limit = jnp.zeros((1, rows), jnp.int32)
    for e in range(lengths.shape[0]):
        limit = jnp.where(slot >= e * SEQ, e * SEQ + limits[e], limit)
    out[:k_in] = jnp.where(slot < limit, total * scales[0], 0.0)


def project(hidden, out_grad, lengths, proj_in, proj_out, scales):
    rows, width = hidden.shape
    narrow = out_grad.shape[1]
    k_in, k_out = proj_in.shape[1], proj_out.shape[1]
    operands = (hidden, out_grad, lengths, proj_in.T, proj_out.T)
    return pl.pallas_call(
        functools.partial(project_kernel, scales),
        out_shape=jax.ShapeDtypeStruct((k_in + k_out, rows), jnp.float32),
        in_specs=[pl.BlockSpec(memory_space=pltpu.HBM)] * 5,
        out_specs=pl.BlockSpec(memory_space=pltpu.VMEM),
        scratch_shapes=[
            pltpu.VMEM((rows, width), jnp.bfloat16),
            pltpu.VMEM((rows, narrow), jnp.bfloat16),
            pltpu.VMEM((k_in, width), jnp.bfloat16),
            pltpu.VMEM((k_out, narrow), jnp.bfloat16),
            pltpu.SMEM(lengths.shape, jnp.int32),
            pltpu.SemaphoreType.DMA((2, 5)),
        ],
        compiler_params=pltpu.CompilerParams(vmem_limit_bytes=24 << 20),
        cost_estimate=pl.CostEstimate(
            flops=2 * rows * (width * k_in + narrow * k_out),
            bytes_accessed=2 * rows * (width + narrow) + 2 * (width * k_in + narrow * k_out),
            transcendentals=0,
        ),
    )(*(pltpu.with_memory_space_constraint(x, pltpu.HBM) for x in operands))


def halves(x):
    high = x.astype(jnp.bfloat16)
    return high, (x - high.astype(jnp.float32)).astype(jnp.bfloat16)


def grads_kernel(k_in, scales, *refs):
    *pieces, out = refs
    both = pieces[0][...]
    for piece in pieces[1:]:
        both = both + piece[...]
    k_out, rows = both.shape[0] - k_in, both.shape[1]
    count = rows // SEQ
    across = 128 // k_out
    act_high, act_low = halves(both[:k_in])
    grad_high, grad_low = halves(both[k_in:])
    slot = lax.broadcasted_iota(jnp.int32, (1, rows), 1)

    def by_example(act):
        return jnp.concatenate(
            [jnp.where((slot >= e * SEQ) & (slot < (e + 1) * SEQ), act, jnp.zeros_like(act)) for e in range(count)], axis=0)

    def tiled(grad):
        return jnp.concatenate([grad] * across, axis=0)

    high = by_example(act_high)
    left = jnp.concatenate([high, high, by_example(act_low)], axis=1)
    high = tiled(grad_high)
    right = jnp.concatenate([high, tiled(grad_low), high], axis=1)
    product = lax.dot_general(left, right, CONTRACT_LAST, preferred_element_type=jnp.float32)
    product = (product * (1.0 / (scales[0] * scales[1]))).astype(jnp.bfloat16).astype(jnp.float32)
    row = lax.broadcasted_iota(jnp.int32, product.shape, 0)
    lane = lax.broadcasted_iota(jnp.int32, product.shape, 1)
    product = jnp.where(row % across == lane // k_out, product, 0.0).astype(jnp.bfloat16)
    groups = k_in // across
    shape = (groups * count, count * k_in)
    to = lax.broadcasted_iota(jnp.int32, shape, 0)
    source = lax.broadcasted_iota(jnp.int32, shape, 1)
    pick = (source // k_in == to % count) & (source % k_in // across == to // count)
    picked = jnp.dot(jnp.where(pick, 1.0, 0.0).astype(jnp.bfloat16), product, preferred_element_type=jnp.float32)
    for group in range(groups):
        out[:, group * 128:(group + 1) * 128] = picked[group * count:(group + 1) * count].astype(jnp.bfloat16)


def example_grads(pieces, k_in, k_out, scales):
    vmem = pl.BlockSpec(memory_space=pltpu.VMEM)
    return pl.pallas_call(
        functools.partial(grads_kernel, k_in, scales),
        out_shape=jax.ShapeDtypeStruct((pieces[0].shape[1] // SEQ, k_in * k_out), jnp.bfloat16),
        in_specs=[vmem] * len(pieces),
        out_specs=vmem,
        compiler_params=pltpu.CompilerParams(vmem_limit_bytes=6 << 20),
        cost_estimate=pl.CostEstimate(flops=1 << 33, bytes_accessed=0, transcendentals=0),
    )(*pieces)


def finish_kernel(examples, n_pieces, n_raw, *refs):
    pieces, raw = refs[:n_pieces], refs[n_pieces:n_pieces + n_raw]
    cov, scores, block, row, sems = refs[n_pieces + n_raw:]
    own_rows, flat = cov.shape
    place = lax.axis_index(("dp", "sub"))
    every = jnp.concatenate([p[...] for p in pieces], axis=0)
    if own_rows % 128 == 0:
        at = pl.multiple_of(place * own_rows, own_rows)
        own = jnp.concatenate([p[:, pl.ds(at, own_rows)] for p in pieces], axis=0)
    else:
        at = pl.multiple_of((place * own_rows) // 128 * 128, 128)
        wider = jnp.concatenate([p[:, pl.ds(at, 128)] for p in pieces], axis=0)
        own = pltpu.roll(wider.astype(jnp.float32), at - place * own_rows + 128, 1)[:, :own_rows].astype(jnp.bfloat16)
    copies = []
    step = max(own_rows // 4, 8)
    for n, at in enumerate(range(0, own_rows, step)):
        part = pl.ds(at, step)
        block[part] = lax.dot_general(own[:, at:at + step], every, CONTRACT_FIRST,
                                      preferred_element_type=jnp.float32) * (1.0 / examples)
        copies.append(pltpu.make_async_copy(block.at[part], cov.at[part], sems.at[n]))
        copies[-1].start()
    wide = every.astype(jnp.float32)
    factor = lax.rsqrt(jnp.sum(wide * wide) / examples + 1e-06)
    if n_raw == 2:
        near, far = raw[0][...], raw[1][...]
        first = lax.axis_index("sub") == 0
        half = near.shape[1]
        row[:, :half] = jnp.where(first, near, far) * factor
        row[:, half:] = jnp.where(first, far, near) * factor
    else:
        row[...] = raw[0][...] * factor
    copies.append(pltpu.make_async_copy(row, scores, sems.at[4]))
    copies[-1].start()
    for copy in copies:
        copy.wait()


def finish(examples, own_rows, pieces, raw):
    flat = pieces[0].shape[1]
    vmem = pl.BlockSpec(memory_space=pltpu.VMEM)
    hbm = pl.BlockSpec(memory_space=pltpu.HBM)
    cov = (own_rows, flat)
    scores = (raw[0].shape[0], sum(r.shape[1] for r in raw))
    return pl.pallas_call(
        functools.partial(finish_kernel, examples, len(pieces), len(raw)),
        out_shape=(jax.ShapeDtypeStruct(cov, jnp.float32), jax.ShapeDtypeStruct(scores, jnp.float32)),
        in_specs=[vmem] * (len(pieces) + len(raw)),
        out_specs=(hbm, hbm),
        scratch_shapes=[pltpu.VMEM(cov, jnp.float32), pltpu.VMEM(scores, jnp.float32), pltpu.SemaphoreType.DMA((5,))],
        compiler_params=pltpu.CompilerParams(vmem_limit_bytes=8 << 20),
    )(*pieces, *raw)


def per_device(hidden, out_grad, lengths, proj_in, proj_out, test_proj):
    k_in, k_out = proj_in.shape[1], proj_out.shape[1]
    flat = k_in * k_out
    group = ("dp", "sub")
    sharers = lax.axis_size(group)
    examples = lengths.shape[0] * sharers
    crossed = lax.axis_size("mp") == 2 and lax.axis_size("sub") == 2
    scales = (128.0, 4.0) if crossed else (1.0, 1.0)
    both = project(hidden, out_grad, lengths, proj_in, proj_out, scales)
    if crossed:
        sent = lax.optimization_barrier(both.astype(jnp.float16))
        far = lax.ppermute(sent, ("mp", "sub"), [(0, 3), (1, 2), (2, 1), (3, 0)])
        near = lax.ppermute(sent, "sub", [(0, 1), (1, 0)])
        made = example_grads([near.astype(jnp.float32), far.astype(jnp.float32)], k_in, k_out, scales)
        grads = lax.ppermute(made, "sub", [(0, 1), (1, 0)])
    else:
        grads = example_grads([lax.psum(both, "mp")], k_in, k_out, scales)

    if crossed and lax.axis_size("dp") == 4:
        swap = [(i, i ^ 1) for i in range(sharers)]
        for_other = jnp.einsum("ep,qp->eq", made, test_proj, preferred_element_type=jnp.float32)
        grads, for_other = lax.optimization_barrier((grads, for_other))
        held = jnp.concatenate([made, grads], axis=0)
        fetched = lax.ppermute(held, group, list(enumerate(SWAPPED_SEND)))
        direct = lax.ppermute(held, group, list(enumerate(DIRECT_SEND)))
        gathered = [held, direct, fetched, lax.ppermute(fetched, group, swap)]
        own = jnp.einsum("ep,qp->eq", grads, test_proj, preferred_element_type=jnp.float32)
        raw = [own, lax.ppermute(for_other, group, swap)]
    else:
        tests = lax.all_gather(test_proj, "sub", axis=0, tiled=True)
        raw = [jnp.einsum("ep,qp->eq", grads, tests, preferred_element_type=jnp.float32)]
        gathered = [lax.all_gather(grads, group, axis=0, tiled=True)]
    return finish(examples, flat // sharers, gathered, raw)


def solution(mesh):
    in_specs = (
        P(("groups", "dp", "sub"), "mp"),
        P(("groups", "dp", "sub"), "mp"),
        P(("groups", "dp", "sub")),
        P("mp", None),
        P("mp", None),
        P(("mp", "sub"), None),
    )
    out_specs = (P(("groups", "dp", "sub"), None), P(("groups", "dp", "sub"), "mp"))
    return jax.shard_map(
        per_device, mesh=mesh, in_specs=in_specs, out_specs=out_specs, check_vma=False
    )
```

```python
import functools

import jax
import jax.numpy as jnp
from jax import lax
from jax.experimental import pallas as pl
from jax.experimental.pallas import tpu as pltpu
from jax.sharding import PartitionSpec as P

SEQ = 64
DEPTH = 256
SWAPPED_SEND = (2, 5, 4, 7, 6, 0, 3, 1)
DIRECT_SEND = (7, 6, 1, 0, 2, 3, 5, 4)
CONTRACT_LAST = (((1,), (1,)), ((), ()))
CONTRACT_FIRST = (((0,), (0,)), ((), ()))


def first_chunk(width):
    small = width // 7
    return small if width % 7 == 0 and small % 128 == 0 else 0


def tree_sum(terms):
    while len(terms) > 1:
        terms = [a + b for a, b in zip(terms[::2], terms[1::2])] + terms[len(terms) // 2 * 2:]
    return terms[0]


def project_kernel(scales, hidden, out_grad, lengths, proj_in, proj_out, tests, out, near_tests, hid, og, pin, pout, limits, sems):
    rows, width = hidden.shape
    k_in = pin.shape[0]
    small = first_chunk(width)
    half = (width - small) // 2

    def copies_of(n):
        if isinstance(n, int) and n == 0:
            lanes = pl.ds(0, small)
        elif isinstance(n, int) and n == 1:
            return [pltpu.make_async_copy(proj_out, pout, sems.at[0, 1]), pltpu.make_async_copy(out_grad, og, sems.at[1, 1])]
        else:
            lanes = pl.ds(small + (n - 2) * half, half)
        return [
            pltpu.make_async_copy(proj_in.at[:, lanes], pin.at[:, lanes], sems.at[0, n]),
            pltpu.make_async_copy(hidden.at[:, lanes], hid.at[:, lanes], sems.at[1, n]),
        ]

    def partial(weights, data, at, size):
        depth = min(size, DEPTH)
        terms = []
        for k in range(0, size, depth):
            lanes = pl.ds(at + k if isinstance(at, int) else pl.multiple_of(at + k, 128), depth)
            terms.append(lax.dot_general(weights[:, lanes], data[:, lanes], CONTRACT_LAST,
                                         preferred_element_type=jnp.float32))
        return tree_sum(terms)

    steps = range(0 if small else 1, 4)
    for n in steps:
        for copy in copies_of(n):
            copy.start()
    bounds = pltpu.make_async_copy(lengths, limits, sems.at[0, 4])
    bounds.start()
    fetch = pltpu.make_async_copy(tests, near_tests, sems.at[1, 4])
    fetch.start()
    total = jnp.zeros((k_in, rows), jnp.float32)
    if small:
        for copy in copies_of(0):
            copy.wait()
        total = partial(pin, hid, 0, small)
    for copy in copies_of(1):
        copy.wait()
    out[k_in:] = partial(pout, og, 0, og.shape[1]) * scales[1]

    def step(n, total):
        for copy in copies_of(n):
            copy.wait()
        return total + partial(pin, hid, small + (n - 2) * half, half)

    total = lax.fori_loop(2, 4, step, total)
    bounds.wait()
    slot = lax.broadcasted_iota(jnp.int32, (1, rows), 1)
    limit = jnp.zeros((1, rows), jnp.int32)
    for e in range(lengths.shape[0]):
        limit = jnp.where(slot >= e * SEQ, e * SEQ + limits[e], limit)
    out[:k_in] = jnp.where(slot < limit, total * scales[0], 0.0)
    fetch.wait()


def project(hidden, out_grad, lengths, proj_in, proj_out, test_proj, scales):
    rows, width = hidden.shape
    narrow = out_grad.shape[1]
    k_in, k_out = proj_in.shape[1], proj_out.shape[1]
    operands = (hidden, out_grad, lengths, proj_in.T, proj_out.T, test_proj)
    return pl.pallas_call(
        functools.partial(project_kernel, scales),
        out_shape=(
            jax.ShapeDtypeStruct((k_in + k_out, rows), jnp.float32),
            jax.ShapeDtypeStruct(test_proj.shape, test_proj.dtype),
        ),
        in_specs=[pl.BlockSpec(memory_space=pltpu.HBM)] * 6,
        out_specs=(pl.BlockSpec(memory_space=pltpu.VMEM),) * 2,
        scratch_shapes=[
            pltpu.VMEM((rows, width), jnp.bfloat16),
            pltpu.VMEM((rows, narrow), jnp.bfloat16),
            pltpu.VMEM((k_in, width), jnp.bfloat16),
            pltpu.VMEM((k_out, narrow), jnp.bfloat16),
            pltpu.SMEM(lengths.shape, jnp.int32),
            pltpu.SemaphoreType.DMA((2, 5)),
        ],
        compiler_params=pltpu.CompilerParams(vmem_limit_bytes=24 << 20),
        cost_estimate=pl.CostEstimate(
            flops=2 * rows * (width * k_in + narrow * k_out),
            bytes_accessed=2 * rows * (width + narrow) + 2 * (width * k_in + narrow * k_out),
            transcendentals=0,
        ),
    )(*(pltpu.with_memory_space_constraint(x, pltpu.HBM) for x in operands))


def halves(x):
    high = x.astype(jnp.bfloat16)
    return high, (x - high.astype(jnp.float32)).astype(jnp.bfloat16)


def grads_kernel(k_in, scales, *refs):
    *pieces, out = refs
    both = pieces[0][...]
    for piece in pieces[1:]:
        both = both + piece[...]
    k_out, rows = both.shape[0] - k_in, both.shape[1]
    count = rows // SEQ
    across = 128 // k_out
    act_high, act_low = halves(both[:k_in])
    grad_high, grad_low = halves(both[k_in:])
    slot = lax.broadcasted_iota(jnp.int32, (1, rows), 1)

    def by_example(act):
        return jnp.concatenate(
            [jnp.where((slot >= e * SEQ) & (slot < (e + 1) * SEQ), act, jnp.zeros_like(act)) for e in range(count)], axis=0)

    def tiled(grad):
        return jnp.concatenate([grad] * across, axis=0)

    high = by_example(act_high)
    left = jnp.concatenate([high, high, by_example(act_low)], axis=1)
    high = tiled(grad_high)
    right = jnp.concatenate([high, tiled(grad_low), high], axis=1)
    product = lax.dot_general(left, right, CONTRACT_LAST, preferred_element_type=jnp.float32)
    product = (product * (1.0 / (scales[0] * scales[1]))).astype(jnp.bfloat16).astype(jnp.float32)
    row = lax.broadcasted_iota(jnp.int32, product.shape, 0)
    lane = lax.broadcasted_iota(jnp.int32, product.shape, 1)
    product = jnp.where(row % across == lane // k_out, product, 0.0).astype(jnp.bfloat16)
    groups = k_in // across
    shape = (groups * count, count * k_in)
    to = lax.broadcasted_iota(jnp.int32, shape, 0)
    source = lax.broadcasted_iota(jnp.int32, shape, 1)
    pick = (source // k_in == to % count) & (source % k_in // across == to // count)
    picked = jnp.dot(jnp.where(pick, 1.0, 0.0).astype(jnp.bfloat16), product, preferred_element_type=jnp.float32)
    for group in range(groups):
        out[:, group * 128:(group + 1) * 128] = picked[group * count:(group + 1) * count].astype(jnp.bfloat16)


def example_grads(pieces, k_in, k_out, scales):
    vmem = pl.BlockSpec(memory_space=pltpu.VMEM)
    return pl.pallas_call(
        functools.partial(grads_kernel, k_in, scales),
        out_shape=jax.ShapeDtypeStruct((pieces[0].shape[1] // SEQ, k_in * k_out), jnp.bfloat16),
        in_specs=[vmem] * len(pieces),
        out_specs=vmem,
        compiler_params=pltpu.CompilerParams(vmem_limit_bytes=6 << 20),
        cost_estimate=pl.CostEstimate(flops=1 << 33, bytes_accessed=0, transcendentals=0),
    )(*pieces)


def finish_kernel(examples, n_pieces, n_raw, *refs):
    pieces, raw = refs[:n_pieces], refs[n_pieces:n_pieces + n_raw]
    cov, scores, block, row, sems = refs[n_pieces + n_raw:]
    own_rows, flat = cov.shape
    place = lax.axis_index(("dp", "sub"))
    every = jnp.concatenate([p[...] for p in pieces], axis=0)
    if own_rows % 128 == 0:
        at = pl.multiple_of(place * own_rows, own_rows)
        own = jnp.concatenate([p[:, pl.ds(at, own_rows)] for p in pieces], axis=0)
    else:
        at = pl.multiple_of((place * own_rows) // 128 * 128, 128)
        wider = jnp.concatenate([p[:, pl.ds(at, 128)] for p in pieces], axis=0)
        own = pltpu.roll(wider.astype(jnp.float32), at - place * own_rows + 128, 1)[:, :own_rows].astype(jnp.bfloat16)
    copies = []
    step = max(own_rows // 4, 8)
    for n, at in enumerate(range(0, own_rows, step)):
        part = pl.ds(at, step)
        block[part] = lax.dot_general(own[:, at:at + step], every, CONTRACT_FIRST,
                                      preferred_element_type=jnp.float32) * (1.0 / examples)
        copies.append(pltpu.make_async_copy(block.at[part], cov.at[part], sems.at[n]))
        copies[-1].start()
    wide = every.astype(jnp.float32)
    factor = lax.rsqrt(jnp.sum(wide * wide) / examples + 1e-06)
    if n_raw == 2:
        near, far = raw[0][...], raw[1][...]
        first = lax.axis_index("sub") == 0
        half = near.shape[1]
        row[:, :half] = jnp.where(first, near, far) * factor
        row[:, half:] = jnp.where(first, far, near) * factor
    else:
        row[...] = raw[0][...] * factor
    copies.append(pltpu.make_async_copy(row, scores, sems.at[4]))
    copies[-1].start()
    for copy in copies:
        copy.wait()


def finish(examples, own_rows, pieces, raw):
    flat = pieces[0].shape[1]
    vmem = pl.BlockSpec(memory_space=pltpu.VMEM)
    hbm = pl.BlockSpec(memory_space=pltpu.HBM)
    cov = (own_rows, flat)
    scores = (raw[0].shape[0], sum(r.shape[1] for r in raw))
    return pl.pallas_call(
        functools.partial(finish_kernel, examples, len(pieces), len(raw)),
        out_shape=(jax.ShapeDtypeStruct(cov, jnp.float32), jax.ShapeDtypeStruct(scores, jnp.float32)),
        in_specs=[vmem] * (len(pieces) + len(raw)),
        out_specs=(hbm, hbm),
        scratch_shapes=[pltpu.VMEM(cov, jnp.float32), pltpu.VMEM(scores, jnp.float32), pltpu.SemaphoreType.DMA((5,))],
        compiler_params=pltpu.CompilerParams(vmem_limit_bytes=8 << 20),
    )(*pieces, *raw)


def per_device(hidden, out_grad, lengths, proj_in, proj_out, test_proj):
    k_in, k_out = proj_in.shape[1], proj_out.shape[1]
    flat = k_in * k_out
    group = ("dp", "sub")
    sharers = lax.axis_size(group)
    examples = lengths.shape[0] * sharers
    crossed = lax.axis_size("mp") == 2 and lax.axis_size("sub") == 2
    scales = (128.0, 4.0) if crossed else (1.0, 1.0)
    both, test_proj = project(hidden, out_grad, lengths, proj_in, proj_out, test_proj, scales)
    if crossed:
        sent = lax.optimization_barrier(both.astype(jnp.float16))
        far = lax.ppermute(sent, ("mp", "sub"), [(0, 3), (1, 2), (2, 1), (3, 0)])
        near = lax.ppermute(sent, "sub", [(0, 1), (1, 0)])
        made = example_grads([near.astype(jnp.float32), far.astype(jnp.float32)], k_in, k_out, scales)
        grads = lax.ppermute(made, "sub", [(0, 1), (1, 0)])
    else:
        grads = example_grads([lax.psum(both, "mp")], k_in, k_out, scales)

    if crossed and lax.axis_size("dp") == 4:
        swap = [(i, i ^ 1) for i in range(sharers)]
        for_other = jnp.einsum("ep,qp->eq", made, test_proj, preferred_element_type=jnp.float32)
        grads, for_other = lax.optimization_barrier((grads, for_other))
        held = jnp.concatenate([made, grads], axis=0)
        fetched = lax.ppermute(held, group, list(enumerate(SWAPPED_SEND)))
        direct = lax.ppermute(held, group, list(enumerate(DIRECT_SEND)))
        gathered = [held, direct, fetched, lax.ppermute(fetched, group, swap)]
        own = jnp.einsum("ep,qp->eq", grads, test_proj, preferred_element_type=jnp.float32)
        raw = [own, lax.ppermute(for_other, group, swap)]
    else:
        tests = lax.all_gather(test_proj, "sub", axis=0, tiled=True)
        raw = [jnp.einsum("ep,qp->eq", grads, tests, preferred_element_type=jnp.float32)]
        gathered = [lax.all_gather(grads, group, axis=0, tiled=True)]
    return finish(examples, flat // sharers, gathered, raw)


def solution(mesh):
    in_specs = (
        P(("groups", "dp", "sub"), "mp"),
        P(("groups", "dp", "sub"), "mp"),
        P(("groups", "dp", "sub")),
        P("mp", None),
        P("mp", None),
        P(("mp", "sub"), None),
    )
    out_specs = (P(("groups", "dp", "sub"), None), P(("groups", "dp", "sub"), "mp"))
    return jax.shard_map(
        per_device, mesh=mesh, in_specs=in_specs, out_specs=out_specs, check_vma=False
    )
```

```python
import functools

import jax
import jax.numpy as jnp
from jax import lax
from jax.experimental import pallas as pl
from jax.experimental.pallas import tpu as pltpu
from jax.sharding import PartitionSpec as P

SEQ = 64
DEPTH = 256
SWAPPED_SEND = (2, 5, 4, 7, 6, 0, 3, 1)
DIRECT_SEND = (7, 6, 1, 0, 2, 3, 5, 4)
CONTRACT_LAST = (((1,), (1,)), ((), ()))
CONTRACT_FIRST = (((0,), (0,)), ((), ()))


def first_chunk(width):
    small = width // 7
    return small if width % 7 == 0 and small % 128 == 0 else 0


def tree_sum(terms):
    while len(terms) > 1:
        terms = [a + b for a, b in zip(terms[::2], terms[1::2])] + terms[len(terms) // 2 * 2:]
    return terms[0]


def project_kernel(scales, hidden, out_grad, lengths, proj_in, proj_out, tests, out, near_tests, hid, og, pin, pout, limits, sems):
    rows, width = hidden.shape
    k_in = pin.shape[0]
    small = first_chunk(width)
    half = (width - small) // 2

    def copies_of(n):
        if isinstance(n, int) and n == 0:
            lanes = pl.ds(0, small)
        elif isinstance(n, int) and n == 1:
            return [pltpu.make_async_copy(proj_out, pout, sems.at[0, 1]), pltpu.make_async_copy(out_grad, og, sems.at[1, 1])]
        else:
            lanes = pl.ds(small + (n - 2) * half, half)
        return [
            pltpu.make_async_copy(proj_in.at[:, lanes], pin.at[:, lanes], sems.at[0, n]),
            pltpu.make_async_copy(hidden.at[:, lanes], hid.at[:, lanes], sems.at[1, n]),
        ]

    def partial(weights, data, at, size):
        depth = min(size, DEPTH)
        terms = []
        for k in range(0, size, depth):
            lanes = pl.ds(at + k if isinstance(at, int) else pl.multiple_of(at + k, 128), depth)
            terms.append(lax.dot_general(weights[:, lanes], data[:, lanes], CONTRACT_LAST,
                                         preferred_element_type=jnp.float32))
        return tree_sum(terms)

    steps = range(0 if small else 1, 4)
    for n in steps:
        for copy in copies_of(n):
            copy.start()
    bounds = pltpu.make_async_copy(lengths, limits, sems.at[0, 4])
    bounds.start()
    fetch = pltpu.make_async_copy(tests, near_tests, sems.at[1, 4])
    fetch.start()
    total = jnp.zeros((k_in, rows), jnp.float32)
    if small:
        for copy in copies_of(0):
            copy.wait()
        total = partial(pin, hid, 0, small)
    for copy in copies_of(1):
        copy.wait()
    out[k_in:] = partial(pout, og, 0, og.shape[1]) * scales[1]

    def step(n, total):
        for copy in copies_of(n):
            copy.wait()
        return total + partial(pin, hid, small + (n - 2) * half, half)

    total = lax.fori_loop(2, 4, step, total)
    bounds.wait()
    slot = lax.broadcasted_iota(jnp.int32, (1, rows), 1)
    limit = jnp.zeros((1, rows), jnp.int32)
    for e in range(lengths.shape[0]):
        limit = jnp.where(slot >= e * SEQ, e * SEQ + limits[e], limit)
    out[:k_in] = jnp.where(slot < limit, total * scales[0], 0.0)
    fetch.wait()


def project(hidden, out_grad, lengths, proj_in, proj_out, test_proj, scales):
    rows, width = hidden.shape
    narrow = out_grad.shape[1]
    k_in, k_out = proj_in.shape[1], proj_out.shape[1]
    operands = (hidden, out_grad, lengths, proj_in.T, proj_out.T, test_proj)
    return pl.pallas_call(
        functools.partial(project_kernel, scales),
        out_shape=(
            jax.ShapeDtypeStruct((k_in + k_out, rows), jnp.float32),
            jax.ShapeDtypeStruct(test_proj.shape, test_proj.dtype),
        ),
        in_specs=[pl.BlockSpec(memory_space=pltpu.HBM)] * 6,
        out_specs=(pl.BlockSpec(memory_space=pltpu.VMEM),) * 2,
        scratch_shapes=[
            pltpu.VMEM((rows, width), jnp.bfloat16),
            pltpu.VMEM((rows, narrow), jnp.bfloat16),
            pltpu.VMEM((k_in, width), jnp.bfloat16),
            pltpu.VMEM((k_out, narrow), jnp.bfloat16),
            pltpu.SMEM(lengths.shape, jnp.int32),
            pltpu.SemaphoreType.DMA((2, 5)),
        ],
        compiler_params=pltpu.CompilerParams(vmem_limit_bytes=24 << 20),
        cost_estimate=pl.CostEstimate(
            flops=2 * rows * (width * k_in + narrow * k_out),
            bytes_accessed=2 * rows * (width + narrow) + 2 * (width * k_in + narrow * k_out),
            transcendentals=0,
        ),
    )(*(pltpu.with_memory_space_constraint(x, pltpu.HBM) for x in operands))


def halves(x):
    high = x.astype(jnp.bfloat16)
    return high, (x - high.astype(jnp.float32)).astype(jnp.bfloat16)


def grads_kernel(k_in, scales, *refs):
    *pieces, out = refs
    both = pieces[0][...]
    for piece in pieces[1:]:
        both = both + piece[...]
    k_out, rows = both.shape[0] - k_in, both.shape[1]
    count = rows // SEQ
    across = 128 // k_out
    act_high, act_low = halves(both[:k_in])
    grad_high, grad_low = halves(both[k_in:])
    slot = lax.broadcasted_iota(jnp.int32, (1, rows), 1)

    def by_example(act):
        return jnp.concatenate(
            [jnp.where((slot >= e * SEQ) & (slot < (e + 1) * SEQ), act, jnp.zeros_like(act)) for e in range(count)], axis=0)

    def tiled(grad):
        return jnp.concatenate([grad] * across, axis=0)

    high = by_example(act_high)
    left = jnp.concatenate([high, high, by_example(act_low)], axis=1)
    high = tiled(grad_high)
    right = jnp.concatenate([high, tiled(grad_low), high], axis=1)
    product = lax.dot_general(left, right, CONTRACT_LAST, preferred_element_type=jnp.float32)
    product = (product * (1.0 / (scales[0] * scales[1]))).astype(jnp.bfloat16).astype(jnp.float32)
    row = lax.broadcasted_iota(jnp.int32, product.shape, 0)
    lane = lax.broadcasted_iota(jnp.int32, product.shape, 1)
    product = jnp.where(row % across == lane // k_out, product, 0.0).astype(jnp.bfloat16)
    groups = k_in // across
    shape = (groups * count, count * k_in)
    to = lax.broadcasted_iota(jnp.int32, shape, 0)
    source = lax.broadcasted_iota(jnp.int32, shape, 1)
    pick = (source // k_in == to % count) & (source % k_in // across == to // count)
    picked = jnp.dot(jnp.where(pick, 1.0, 0.0).astype(jnp.bfloat16), product, preferred_element_type=jnp.float32)
    for group in range(groups):
        out[:, group * 128:(group + 1) * 128] = picked[group * count:(group + 1) * count].astype(jnp.bfloat16)


def example_grads(pieces, k_in, k_out, scales):
    vmem = pl.BlockSpec(memory_space=pltpu.VMEM)
    return pl.pallas_call(
        functools.partial(grads_kernel, k_in, scales),
        out_shape=jax.ShapeDtypeStruct((pieces[0].shape[1] // SEQ, k_in * k_out), jnp.bfloat16),
        in_specs=[vmem] * len(pieces),
        out_specs=vmem,
        compiler_params=pltpu.CompilerParams(vmem_limit_bytes=6 << 20),
        cost_estimate=pl.CostEstimate(flops=1 << 33, bytes_accessed=0, transcendentals=0),
    )(*pieces)


def finish_kernel(examples, n_pieces, n_raw, *refs):
    pieces, raw = refs[:n_pieces], refs[n_pieces:n_pieces + n_raw]
    cov, scores, block, row, sems = refs[n_pieces + n_raw:]
    own_rows, flat = cov.shape
    place = lax.axis_index(("dp", "sub"))
    every = jnp.concatenate([p[...] for p in pieces], axis=0)
    if own_rows % 128 == 0:
        at = pl.multiple_of(place * own_rows, own_rows)
        own = jnp.concatenate([p[:, pl.ds(at, own_rows)] for p in pieces], axis=0)
    else:
        at = pl.multiple_of((place * own_rows) // 128 * 128, 128)
        wider = jnp.concatenate([p[:, pl.ds(at, 128)] for p in pieces], axis=0)
        own = pltpu.roll(wider.astype(jnp.float32), at - place * own_rows + 128, 1)[:, :own_rows].astype(jnp.bfloat16)
    wide = every.astype(jnp.float32)
    total = jnp.sum(jnp.sum(wide * wide, axis=0, keepdims=True), axis=1, keepdims=True)
    factor = lax.rsqrt(total * (1.0 / examples) + 1e-06)
    if n_raw == 2:
        near, far = raw[0][...] * factor, raw[1][...] * factor
        first = lax.axis_index("sub") == 0
        half = near.shape[1]
        row[:, :half] = jnp.where(first, near, far)
        row[:, half:] = jnp.where(first, far, near)
    else:
        row[...] = raw[0][...] * factor
    copies = [pltpu.make_async_copy(row, scores, sems.at[4])]
    copies[0].start()
    step = max(own_rows // 4, 8)
    for n, at in enumerate(range(0, own_rows, step)):
        part = pl.ds(at, step)
        block[part] = lax.dot_general(own[:, at:at + step], every, CONTRACT_FIRST,
                                      preferred_element_type=jnp.float32) * (1.0 / examples)
        copies.append(pltpu.make_async_copy(block.at[part], cov.at[part], sems.at[n]))
        copies[-1].start()
    for copy in copies:
        copy.wait()


def finish(examples, own_rows, pieces, raw):
    flat = pieces[0].shape[1]
    vmem = pl.BlockSpec(memory_space=pltpu.VMEM)
    hbm = pl.BlockSpec(memory_space=pltpu.HBM)
    cov = (own_rows, flat)
    scores = (raw[0].shape[0], sum(r.shape[1] for r in raw))
    return pl.pallas_call(
        functools.partial(finish_kernel, examples, len(pieces), len(raw)),
        out_shape=(jax.ShapeDtypeStruct(cov, jnp.float32), jax.ShapeDtypeStruct(scores, jnp.float32)),
        in_specs=[vmem] * (len(pieces) + len(raw)),
        out_specs=(hbm, hbm),
        scratch_shapes=[pltpu.VMEM(cov, jnp.float32), pltpu.VMEM(scores, jnp.float32), pltpu.SemaphoreType.DMA((5,))],
        compiler_params=pltpu.CompilerParams(vmem_limit_bytes=8 << 20),
    )(*pieces, *raw)


def per_device(hidden, out_grad, lengths, proj_in, proj_out, test_proj):
    k_in, k_out = proj_in.shape[1], proj_out.shape[1]
    flat = k_in * k_out
    group = ("dp", "sub")
    sharers = lax.axis_size(group)
    examples = lengths.shape[0] * sharers
    crossed = lax.axis_size("mp") == 2 and lax.axis_size("sub") == 2
    scales = (128.0, 4.0) if crossed else (1.0, 1.0)
    both, test_proj = project(hidden, out_grad, lengths, proj_in, proj_out, test_proj, scales)
    if crossed:
        sent = lax.optimization_barrier(both.astype(jnp.float16))
        far = lax.ppermute(sent, ("mp", "sub"), [(0, 3), (1, 2), (2, 1), (3, 0)])
        near = lax.ppermute(sent, "sub", [(0, 1), (1, 0)])
        made = example_grads([near.astype(jnp.float32), far.astype(jnp.float32)], k_in, k_out, scales)
        grads = lax.ppermute(made, "sub", [(0, 1), (1, 0)])
    else:
        grads = example_grads([lax.psum(both, "mp")], k_in, k_out, scales)

    if crossed and lax.axis_size("dp") == 4:
        swap = [(i, i ^ 1) for i in range(sharers)]
        for_other = jnp.einsum("ep,qp->eq", made, test_proj, preferred_element_type=jnp.float32)
        grads, for_other = lax.optimization_barrier((grads, for_other))
        held = jnp.concatenate([made, grads], axis=0)
        fetched = lax.ppermute(held, group, list(enumerate(SWAPPED_SEND)))
        direct = lax.ppermute(held, group, list(enumerate(DIRECT_SEND)))
        gathered = [held, direct, fetched, lax.ppermute(fetched, group, swap)]
        own = jnp.einsum("ep,qp->eq", grads, test_proj, preferred_element_type=jnp.float32)
        raw = [own, lax.ppermute(for_other, group, swap)]
    else:
        tests = lax.all_gather(test_proj, "sub", axis=0, tiled=True)
        raw = [jnp.einsum("ep,qp->eq", grads, tests, preferred_element_type=jnp.float32)]
        gathered = [lax.all_gather(grads, group, axis=0, tiled=True)]
    return finish(examples, flat // sharers, gathered, raw)


def solution(mesh):
    in_specs = (
        P(("groups", "dp", "sub"), "mp"),
        P(("groups", "dp", "sub"), "mp"),
        P(("groups", "dp", "sub")),
        P("mp", None),
        P("mp", None),
        P(("mp", "sub"), None),
    )
    out_specs = (P(("groups", "dp", "sub"), None), P(("groups", "dp", "sub"), "mp"))
    return jax.shard_map(
        per_device, mesh=mesh, in_specs=in_specs, out_specs=out_specs, check_vma=False
    )
```

```python
import functools

import jax
import jax.numpy as jnp
from jax import lax
from jax.experimental import pallas as pl
from jax.experimental.pallas import tpu as pltpu
from jax.sharding import PartitionSpec as P

SEQ = 64
DEPTHS = (1024, 512, 256, 128)
SWAPPED_SEND = (3, 5, 4, 7, 6, 0, 2, 1)
DIRECT_SEND = (7, 6, 0, 1, 2, 3, 5, 4)
CONTRACT_LAST = (((1,), (1,)), ((), ()))
CONTRACT_FIRST = (((0,), (0,)), ((), ()))


def first_chunk(width):
    small = width // 7
    return small if width % 7 == 0 and small % 128 == 0 else 0


def tree_sum(terms):
    while len(terms) > 1:
        terms = [a + b for a, b in zip(terms[::2], terms[1::2])] + terms[len(terms) // 2 * 2:]
    return terms[0]


def project_kernel(scales, hidden, out_grad, lengths, proj_in, proj_out, tests, out, near_tests, hid, og, pin, pout, limits, sems):
    rows, width = hidden.shape
    k_in = pin.shape[0]
    small = first_chunk(width)
    half = (width - small) // 2

    def copies_of(n):
        if isinstance(n, int) and n == 0:
            lanes = pl.ds(0, small)
        elif isinstance(n, int) and n == 1:
            return [pltpu.make_async_copy(proj_out, pout, sems.at[0, 1]), pltpu.make_async_copy(out_grad, og, sems.at[1, 1])]
        else:
            lanes = pl.ds(small + (n - 2) * half, half)
        return [
            pltpu.make_async_copy(proj_in.at[:, lanes], pin.at[:, lanes], sems.at[0, n]),
            pltpu.make_async_copy(hidden.at[:, lanes], hid.at[:, lanes], sems.at[1, n]),
        ]

    def partial(weights, data, at, size):
        depth = next(depth for depth in DEPTHS if size % depth == 0)
        terms = []
        for k in range(0, size, depth):
            lanes = pl.ds(at + k if isinstance(at, int) else pl.multiple_of(at + k, 128), depth)
            terms.append(lax.dot_general(weights[:, lanes], data[:, lanes], CONTRACT_LAST,
                                         preferred_element_type=jnp.float32))
        return tree_sum(terms)

    steps = range(0 if small else 1, 4)
    for n in steps:
        for copy in copies_of(n):
            copy.start()
    bounds = pltpu.make_async_copy(lengths, limits, sems.at[0, 4])
    bounds.start()
    fetch = pltpu.make_async_copy(tests, near_tests, sems.at[1, 4])
    fetch.start()
    total = jnp.zeros((k_in, rows), jnp.float32)
    if small:
        for copy in copies_of(0):
            copy.wait()
        total = partial(pin, hid, 0, small)
    for copy in copies_of(1):
        copy.wait()
    out[k_in:] = partial(pout, og, 0, og.shape[1]) * scales[1]

    def step(n, total):
        for copy in copies_of(n):
            copy.wait()
        return total + partial(pin, hid, small + (n - 2) * half, half)

    total = lax.fori_loop(2, 4, step, total)
    bounds.wait()
    slot = lax.broadcasted_iota(jnp.int32, (1, rows), 1)
    limit = jnp.zeros((1, rows), jnp.int32)
    for e in range(lengths.shape[0]):
        limit = jnp.where(slot >= e * SEQ, e * SEQ + limits[e], limit)
    out[:k_in] = jnp.where(slot < limit, total * scales[0], 0.0)
    fetch.wait()


def project(hidden, out_grad, lengths, proj_in, proj_out, test_proj, scales):
    rows, width = hidden.shape
    narrow = out_grad.shape[1]
    k_in, k_out = proj_in.shape[1], proj_out.shape[1]
    operands = (hidden, out_grad, lengths, proj_in.T, proj_out.T, test_proj)
    return pl.pallas_call(
        functools.partial(project_kernel, scales),
        out_shape=(
            jax.ShapeDtypeStruct((k_in + k_out, rows), jnp.float32),
            jax.ShapeDtypeStruct(test_proj.shape, test_proj.dtype),
        ),
        in_specs=[pl.BlockSpec(memory_space=pltpu.HBM)] * 6,
        out_specs=(pl.BlockSpec(memory_space=pltpu.VMEM),) * 2,
        scratch_shapes=[
            pltpu.VMEM((rows, width), jnp.bfloat16),
            pltpu.VMEM((rows, narrow), jnp.bfloat16),
            pltpu.VMEM((k_in, width), jnp.bfloat16),
            pltpu.VMEM((k_out, narrow), jnp.bfloat16),
            pltpu.SMEM(lengths.shape, jnp.int32),
            pltpu.SemaphoreType.DMA((2, 5)),
        ],
        compiler_params=pltpu.CompilerParams(vmem_limit_bytes=24 << 20),
        cost_estimate=pl.CostEstimate(
            flops=2 * rows * (width * k_in + narrow * k_out),
            bytes_accessed=2 * rows * (width + narrow) + 2 * (width * k_in + narrow * k_out),
            transcendentals=0,
        ),
    )(*(pltpu.with_memory_space_constraint(x, pltpu.HBM) for x in operands))


def halves(x):
    high = x.astype(jnp.bfloat16)
    return high, (x - high.astype(jnp.float32)).astype(jnp.bfloat16)


def grads_kernel(k_in, scales, *refs):
    *pieces, out = refs
    both = pieces[0][...]
    for piece in pieces[1:]:
        both = both + piece[...]
    k_out, rows = both.shape[0] - k_in, both.shape[1]
    count = rows // SEQ
    across = 128 // k_out
    act_high, act_low = halves(both[:k_in])
    grad_high, grad_low = halves(both[k_in:])
    slot = lax.broadcasted_iota(jnp.int32, (1, rows), 1)

    def by_example(act):
        return jnp.concatenate(
            [jnp.where((slot >= e * SEQ) & (slot < (e + 1) * SEQ), act, jnp.zeros_like(act)) for e in range(count)], axis=0)

    def tiled(grad):
        return jnp.concatenate([grad] * across, axis=0)

    high = by_example(act_high)
    left = jnp.concatenate([high, high, by_example(act_low)], axis=1)
    high = tiled(grad_high)
    right = jnp.concatenate([high, tiled(grad_low), high], axis=1)
    product = lax.dot_general(left, right, CONTRACT_LAST, preferred_element_type=jnp.float32)
    product = (product * (1.0 / (scales[0] * scales[1]))).astype(jnp.bfloat16).astype(jnp.float32)
    row = lax.broadcasted_iota(jnp.int32, product.shape, 0)
    lane = lax.broadcasted_iota(jnp.int32, product.shape, 1)
    product = jnp.where(row % across == lane // k_out, product, 0.0).astype(jnp.bfloat16)
    groups = k_in // across
    shape = (groups * count, count * k_in)
    to = lax.broadcasted_iota(jnp.int32, shape, 0)
    source = lax.broadcasted_iota(jnp.int32, shape, 1)
    pick = (source // k_in == to % count) & (source % k_in // across == to // count)
    picked = jnp.dot(jnp.where(pick, 1.0, 0.0).astype(jnp.bfloat16), product, preferred_element_type=jnp.float32)
    for group in range(groups):
        out[:, group * 128:(group + 1) * 128] = picked[group * count:(group + 1) * count].astype(jnp.bfloat16)


def example_grads(pieces, k_in, k_out, scales):
    vmem = pl.BlockSpec(memory_space=pltpu.VMEM)
    return pl.pallas_call(
        functools.partial(grads_kernel, k_in, scales),
        out_shape=jax.ShapeDtypeStruct((pieces[0].shape[1] // SEQ, k_in * k_out), jnp.bfloat16),
        in_specs=[vmem] * len(pieces),
        out_specs=vmem,
        compiler_params=pltpu.CompilerParams(vmem_limit_bytes=6 << 20),
        cost_estimate=pl.CostEstimate(flops=1 << 33, bytes_accessed=0, transcendentals=0),
    )(*pieces)


def finish_kernel(examples, n_pieces, n_raw, *refs):
    pieces, raw = refs[:n_pieces], refs[n_pieces:n_pieces + n_raw]
    cov, scores, block, row, sems = refs[n_pieces + n_raw:]
    own_rows, flat = cov.shape
    place = lax.axis_index(("dp", "sub"))
    every = jnp.concatenate([p[...] for p in pieces], axis=0)
    if own_rows % 128 == 0:
        at = pl.multiple_of(place * own_rows, own_rows)
        own = jnp.concatenate([p[:, pl.ds(at, own_rows)] for p in pieces], axis=0)
    else:
        at = pl.multiple_of((place * own_rows) // 128 * 128, 128)
        wider = jnp.concatenate([p[:, pl.ds(at, 128)] for p in pieces], axis=0)
        own = pltpu.roll(wider.astype(jnp.float32), at - place * own_rows + 128, 1)[:, :own_rows].astype(jnp.bfloat16)
    wide = every.astype(jnp.float32)
    total = jnp.sum(jnp.sum(wide * wide, axis=0, keepdims=True), axis=1, keepdims=True)
    factor = lax.rsqrt(total * (1.0 / examples) + 1e-06)
    if n_raw == 2:
        near, far = raw[0][...] * factor, raw[1][...] * factor
        first = lax.axis_index("sub") == 0
        half = near.shape[1]
        row[:, :half] = jnp.where(first, near, far)
        row[:, half:] = jnp.where(first, far, near)
    else:
        row[...] = raw[0][...] * factor
    copies = [pltpu.make_async_copy(row, scores, sems.at[4])]
    copies[0].start()
    step = max(own_rows // 4, 8)
    for n, at in enumerate(range(0, own_rows, step)):
        part = pl.ds(at, step)
        block[part] = lax.dot_general(own[:, at:at + step], every, CONTRACT_FIRST,
                                      preferred_element_type=jnp.float32) * (1.0 / examples)
        copies.append(pltpu.make_async_copy(block.at[part], cov.at[part], sems.at[n]))
        copies[-1].start()
    for copy in copies:
        copy.wait()


def finish(examples, own_rows, pieces, raw):
    flat = pieces[0].shape[1]
    vmem = pl.BlockSpec(memory_space=pltpu.VMEM)
    hbm = pl.BlockSpec(memory_space=pltpu.HBM)
    cov = (own_rows, flat)
    scores = (raw[0].shape[0], sum(r.shape[1] for r in raw))
    return pl.pallas_call(
        functools.partial(finish_kernel, examples, len(pieces), len(raw)),
        out_shape=(jax.ShapeDtypeStruct(cov, jnp.float32), jax.ShapeDtypeStruct(scores, jnp.float32)),
        in_specs=[vmem] * (len(pieces) + len(raw)),
        out_specs=(hbm, hbm),
        scratch_shapes=[pltpu.VMEM(cov, jnp.float32), pltpu.VMEM(scores, jnp.float32), pltpu.SemaphoreType.DMA((5,))],
        compiler_params=pltpu.CompilerParams(vmem_limit_bytes=8 << 20),
    )(*pieces, *raw)


def per_device(hidden, out_grad, lengths, proj_in, proj_out, test_proj):
    k_in, k_out = proj_in.shape[1], proj_out.shape[1]
    flat = k_in * k_out
    group = ("dp", "sub")
    sharers = lax.axis_size(group)
    examples = lengths.shape[0] * sharers
    crossed = lax.axis_size("mp") == 2 and lax.axis_size("sub") == 2
    scales = (128.0, 4.0) if crossed else (1.0, 1.0)
    both, test_proj = project(hidden, out_grad, lengths, proj_in, proj_out, test_proj, scales)
    if crossed:
        sent = lax.optimization_barrier(both.astype(jnp.float16))
        far = lax.ppermute(sent, ("mp", "sub"), [(0, 3), (1, 2), (2, 1), (3, 0)])
        near = lax.ppermute(sent, "sub", [(0, 1), (1, 0)])
        made = example_grads([near.astype(jnp.float32), far.astype(jnp.float32)], k_in, k_out, scales)
        grads = lax.ppermute(made, "sub", [(0, 1), (1, 0)])
    else:
        grads = example_grads([lax.psum(both, "mp")], k_in, k_out, scales)

    if crossed and lax.axis_size("dp") == 4:
        swap = [(i, i ^ 1) for i in range(sharers)]
        for_other = jnp.einsum("ep,qp->eq", made, test_proj, preferred_element_type=jnp.float32)
        grads, for_other = lax.optimization_barrier((grads, for_other))
        held = jnp.concatenate([made, grads], axis=0)
        fetched = lax.ppermute(held, group, list(enumerate(SWAPPED_SEND)))
        direct = lax.ppermute(held, group, list(enumerate(DIRECT_SEND)))
        gathered = [held, direct, fetched, lax.ppermute(fetched, group, swap)]
        own = jnp.einsum("ep,qp->eq", grads, test_proj, preferred_element_type=jnp.float32)
        raw = [own, lax.ppermute(for_other, group, swap)]
    else:
        tests = lax.all_gather(test_proj, "sub", axis=0, tiled=True)
        raw = [jnp.einsum("ep,qp->eq", grads, tests, preferred_element_type=jnp.float32)]
        gathered = [lax.all_gather(grads, group, axis=0, tiled=True)]
    return finish(examples, flat // sharers, gathered, raw)


def solution(mesh):
    in_specs = (
        P(("groups", "dp", "sub"), "mp"),
        P(("groups", "dp", "sub"), "mp"),
        P(("groups", "dp", "sub")),
        P("mp", None),
        P("mp", None),
        P(("mp", "sub"), None),
    )
    out_specs = (P(("groups", "dp", "sub"), None), P(("groups", "dp", "sub"), "mp"))
    return jax.shard_map(
        per_device, mesh=mesh, in_specs=in_specs, out_specs=out_specs, check_vma=False
    )
```

```python
import functools

import jax
import jax.numpy as jnp
from jax import lax
from jax.experimental import pallas as pl
from jax.experimental.pallas import tpu as pltpu
from jax.sharding import PartitionSpec as P

SEQ = 64
DEPTHS = (1024, 512, 256, 128)
SWAPPED_SEND = (3, 5, 4, 7, 6, 0, 2, 1)
DIRECT_SEND = (7, 6, 0, 1, 2, 3, 5, 4)
CONTRACT_LAST = (((1,), (1,)), ((), ()))
CONTRACT_FIRST = (((0,), (0,)), ((), ()))


def first_chunk(width):
    small = width // 7
    return small if width % 7 == 0 and small % 128 == 0 else 0


def tree_sum(terms):
    while len(terms) > 1:
        terms = [a + b for a, b in zip(terms[::2], terms[1::2])] + terms[len(terms) // 2 * 2:]
    return terms[0]


def project_kernel(scales, hidden, out_grad, lengths, proj_in, proj_out, tests, out, near_tests, hid, og, pin, pout, limits, sems):
    rows, width = hidden.shape
    k_in = pin.shape[0]
    small = first_chunk(width)
    half = (width - small) // 2

    def copies_of(n):
        if isinstance(n, int) and n == 0:
            lanes = pl.ds(0, small)
        elif isinstance(n, int) and n == 1:
            return [pltpu.make_async_copy(proj_out, pout, sems.at[0, 1]), pltpu.make_async_copy(out_grad, og, sems.at[1, 1])]
        else:
            lanes = pl.ds(small + (n - 2) * half, half)
        return [
            pltpu.make_async_copy(proj_in.at[:, lanes], pin.at[:, lanes], sems.at[0, n]),
            pltpu.make_async_copy(hidden.at[:, lanes], hid.at[:, lanes], sems.at[1, n]),
        ]

    def partial(weights, data, at, size):
        depth = next(depth for depth in DEPTHS if size % depth == 0)
        terms = []
        for k in range(0, size, depth):
            lanes = pl.ds(at + k if isinstance(at, int) else pl.multiple_of(at + k, 128), depth)
            terms.append(lax.dot_general(weights[:, lanes], data[:, lanes], CONTRACT_LAST,
                                         preferred_element_type=jnp.float32))
        return tree_sum(terms)

    steps = range(0 if small else 1, 4)
    for n in steps:
        for copy in copies_of(n):
            copy.start()
    bounds = pltpu.make_async_copy(lengths, limits, sems.at[0, 4])
    bounds.start()
    fetch = pltpu.make_async_copy(tests, near_tests, sems.at[1, 4])
    fetch.start()
    total = jnp.zeros((k_in, rows), jnp.float32)
    if small:
        for copy in copies_of(0):
            copy.wait()
        total = partial(pin, hid, 0, small)
    for copy in copies_of(1):
        copy.wait()
    out[k_in:] = partial(pout, og, 0, og.shape[1]) * scales[1]

    def step(n, total):
        for copy in copies_of(n):
            copy.wait()
        return total + partial(pin, hid, small + (n - 2) * half, half)

    total = lax.fori_loop(2, 4, step, total)
    bounds.wait()
    slot = lax.broadcasted_iota(jnp.int32, (1, rows), 1)
    limit = jnp.zeros((1, rows), jnp.int32)
    for e in range(lengths.shape[0]):
        limit = jnp.where(slot >= e * SEQ, e * SEQ + limits[e], limit)
    out[:k_in] = jnp.where(slot < limit, total * scales[0], 0.0)
    fetch.wait()


def project(hidden, out_grad, lengths, proj_in, proj_out, test_proj, scales):
    rows, width = hidden.shape
    narrow = out_grad.shape[1]
    k_in, k_out = proj_in.shape[1], proj_out.shape[1]
    operands = (hidden, out_grad, lengths, proj_in.T, proj_out.T, test_proj)
    return pl.pallas_call(
        functools.partial(project_kernel, scales),
        out_shape=(
            jax.ShapeDtypeStruct((k_in + k_out, rows), jnp.float32),
            jax.ShapeDtypeStruct(test_proj.shape, test_proj.dtype),
        ),
        in_specs=[pl.BlockSpec(memory_space=pltpu.HBM)] * 6,
        out_specs=(pl.BlockSpec(memory_space=pltpu.VMEM),) * 2,
        scratch_shapes=[
            pltpu.VMEM((rows, width), jnp.bfloat16),
            pltpu.VMEM((rows, narrow), jnp.bfloat16),
            pltpu.VMEM((k_in, width), jnp.bfloat16),
            pltpu.VMEM((k_out, narrow), jnp.bfloat16),
            pltpu.SMEM(lengths.shape, jnp.int32),
            pltpu.SemaphoreType.DMA((2, 5)),
        ],
        compiler_params=pltpu.CompilerParams(vmem_limit_bytes=24 << 20),
        cost_estimate=pl.CostEstimate(
            flops=2 * rows * (width * k_in + narrow * k_out),
            bytes_accessed=2 * rows * (width + narrow) + 2 * (width * k_in + narrow * k_out),
            transcendentals=0,
        ),
    )(*(pltpu.with_memory_space_constraint(x, pltpu.HBM) for x in operands))


def halves(x):
    high = x.astype(jnp.bfloat16)
    return high, (x - high.astype(jnp.float32)).astype(jnp.bfloat16)


def grads_kernel(k_in, scales, *refs):
    *pieces, out = refs
    both = pieces[0][...]
    for piece in pieces[1:]:
        both = both + piece[...]
    k_out, rows = both.shape[0] - k_in, both.shape[1]
    count = rows // SEQ
    across = 128 // k_out
    act_high, act_low = halves(both[:k_in])
    grad_high, grad_low = halves(both[k_in:])
    slot = lax.broadcasted_iota(jnp.int32, (1, rows), 1)

    def by_example(act):
        return jnp.concatenate(
            [jnp.where((slot >= e * SEQ) & (slot < (e + 1) * SEQ), act, jnp.zeros_like(act)) for e in range(count)], axis=0)

    def tiled(grad):
        return jnp.concatenate([grad] * across, axis=0)

    high = by_example(act_high)
    left = jnp.concatenate([high, high, by_example(act_low)], axis=1)
    high = tiled(grad_high)
    right = jnp.concatenate([high, tiled(grad_low), high], axis=1)
    product = lax.dot_general(left, right, CONTRACT_LAST, preferred_element_type=jnp.float32)
    product = (product * (1.0 / (scales[0] * scales[1]))).astype(jnp.bfloat16).astype(jnp.float32)
    row = lax.broadcasted_iota(jnp.int32, product.shape, 0)
    lane = lax.broadcasted_iota(jnp.int32, product.shape, 1)
    product = jnp.where(row % across == lane // k_out, product, 0.0).astype(jnp.bfloat16)
    groups = k_in // across
    shape = (groups * count, count * k_in)
    to = lax.broadcasted_iota(jnp.int32, shape, 0)
    source = lax.broadcasted_iota(jnp.int32, shape, 1)
    pick = (source // k_in == to % count) & (source % k_in // across == to // count)
    picked = jnp.dot(jnp.where(pick, 1.0, 0.0).astype(jnp.bfloat16), product, preferred_element_type=jnp.float32)
    for group in range(groups):
        out[:, group * 128:(group + 1) * 128] = picked[group * count:(group + 1) * count].astype(jnp.bfloat16)


def example_grads(pieces, k_in, k_out, scales):
    vmem = pl.BlockSpec(memory_space=pltpu.VMEM)
    return pl.pallas_call(
        functools.partial(grads_kernel, k_in, scales),
        out_shape=jax.ShapeDtypeStruct((pieces[0].shape[1] // SEQ, k_in * k_out), jnp.bfloat16),
        in_specs=[vmem] * len(pieces),
        out_specs=vmem,
        compiler_params=pltpu.CompilerParams(vmem_limit_bytes=6 << 20),
        cost_estimate=pl.CostEstimate(flops=1 << 33, bytes_accessed=0, transcendentals=0),
    )(*pieces)


def finish_kernel(examples, n_pieces, n_raw, *refs):
    pieces, raw = refs[:n_pieces], refs[n_pieces:n_pieces + n_raw]
    cov, scores, block, row, sems = refs[n_pieces + n_raw:]
    own_rows, flat = cov.shape
    place = lax.axis_index(("dp", "sub"))
    every = jnp.concatenate([p[...] for p in pieces], axis=0)
    if own_rows % 128 == 0:
        at = pl.multiple_of(place * own_rows, own_rows)
        own = jnp.concatenate([p[:, pl.ds(at, own_rows)] for p in pieces], axis=0)
    else:
        at = pl.multiple_of((place * own_rows) // 128 * 128, 128)
        wider = jnp.concatenate([p[:, pl.ds(at, 128)] for p in pieces], axis=0)
        own = pltpu.roll(wider.astype(jnp.float32), at - place * own_rows + 128, 1)[:, :own_rows].astype(jnp.bfloat16)
    wide = every.astype(jnp.float32)
    total = jnp.sum(jnp.sum(wide * wide, axis=0, keepdims=True), axis=1, keepdims=True)
    factor = lax.rsqrt(total * (1.0 / examples) + 1e-06)
    if n_raw == 2:
        near, far = raw[0][...] * factor, raw[1][...] * factor
        first = lax.axis_index("sub") == 0
        half = near.shape[1]
        row[:, :half] = jnp.where(first, near, far)
        row[:, half:] = jnp.where(first, far, near)
    else:
        row[...] = raw[0][...] * factor
    copies = [pltpu.make_async_copy(row, scores, sems.at[4])]
    copies[0].start()
    step = max(own_rows // 4, 8)
    for n, at in enumerate(range(0, own_rows, step)):
        part = pl.ds(at, step)
        block[part] = lax.dot_general(own[:, at:at + step], every, CONTRACT_FIRST,
                                      preferred_element_type=jnp.float32) * (1.0 / examples)
        copies.append(pltpu.make_async_copy(block.at[part], cov.at[part], sems.at[n]))
        copies[-1].start()
    for copy in copies:
        copy.wait()


def finish(examples, own_rows, pieces, raw):
    flat = pieces[0].shape[1]
    vmem = pl.BlockSpec(memory_space=pltpu.VMEM)
    hbm = pl.BlockSpec(memory_space=pltpu.HBM)
    cov = (own_rows, flat)
    scores = (raw[0].shape[0], sum(r.shape[1] for r in raw))
    return pl.pallas_call(
        functools.partial(finish_kernel, examples, len(pieces), len(raw)),
        out_shape=(jax.ShapeDtypeStruct(cov, jnp.float32), jax.ShapeDtypeStruct(scores, jnp.float32)),
        in_specs=[vmem] * (len(pieces) + len(raw)),
        out_specs=(hbm, hbm),
        scratch_shapes=[pltpu.VMEM(cov, jnp.float32), pltpu.VMEM(scores, jnp.float32), pltpu.SemaphoreType.DMA((5,))],
        compiler_params=pltpu.CompilerParams(vmem_limit_bytes=8 << 20),
    )(*pieces, *raw)


def per_device(hidden, out_grad, lengths, proj_in, proj_out, test_proj):
    k_in, k_out = proj_in.shape[1], proj_out.shape[1]
    flat = k_in * k_out
    group = ("dp", "sub")
    sharers = lax.axis_size(group)
    examples = lengths.shape[0] * sharers
    crossed = lax.axis_size("mp") == 2 and lax.axis_size("sub") == 2
    scales = (128.0, 4.0) if crossed else (1.0, 1.0)
    both, test_proj = project(hidden, out_grad, lengths, proj_in, proj_out, test_proj, scales)
    if crossed:
        sent = lax.optimization_barrier(both.astype(jnp.float16))
        far = lax.ppermute(sent, ("mp", "sub"), [(0, 3), (1, 2), (2, 1), (3, 0)])
        near = lax.ppermute(sent, "sub", [(0, 1), (1, 0)])
        made = example_grads([far.astype(jnp.float32), near.astype(jnp.float32)], k_in, k_out, scales)
        grads = lax.ppermute(made, "sub", [(0, 1), (1, 0)])
    else:
        grads = example_grads([lax.psum(both, "mp")], k_in, k_out, scales)

    if crossed and lax.axis_size("dp") == 4:
        swap = [(i, i ^ 1) for i in range(sharers)]
        for_other = jnp.einsum("ep,qp->eq", made, test_proj, preferred_element_type=jnp.float32)
        grads, for_other = lax.optimization_barrier((grads, for_other))
        held = jnp.concatenate([made, grads], axis=0)
        fetched = lax.ppermute(held, group, list(enumerate(SWAPPED_SEND)))
        direct = lax.ppermute(held, group, list(enumerate(DIRECT_SEND)))
        gathered = [held, direct, fetched, lax.ppermute(fetched, group, swap)]
        own = jnp.einsum("ep,qp->eq", grads, test_proj, preferred_element_type=jnp.float32)
        raw = [own, lax.ppermute(for_other, group, swap)]
    else:
        tests = lax.all_gather(test_proj, "sub", axis=0, tiled=True)
        raw = [jnp.einsum("ep,qp->eq", grads, tests, preferred_element_type=jnp.float32)]
        gathered = [lax.all_gather(grads, group, axis=0, tiled=True)]
    return finish(examples, flat // sharers, gathered, raw)


def solution(mesh):
    in_specs = (
        P(("groups", "dp", "sub"), "mp"),
        P(("groups", "dp", "sub"), "mp"),
        P(("groups", "dp", "sub")),
        P("mp", None),
        P("mp", None),
        P(("mp", "sub"), None),
    )
    out_specs = (P(("groups", "dp", "sub"), None), P(("groups", "dp", "sub"), "mp"))
    return jax.shard_map(
        per_device, mesh=mesh, in_specs=in_specs, out_specs=out_specs, check_vma=False
    )
```

```python
import functools

import jax
import jax.numpy as jnp
from jax import lax
from jax.experimental import pallas as pl
from jax.experimental.pallas import tpu as pltpu
from jax.sharding import PartitionSpec as P

SEQ = 64
DEPTHS = (1024, 512, 256, 128)
SWAPPED_SEND = (3, 5, 4, 7, 6, 0, 2, 1)
DIRECT_SEND = (7, 6, 0, 1, 2, 3, 5, 4)
CONTRACT_LAST = (((1,), (1,)), ((), ()))
CONTRACT_FIRST = (((0,), (0,)), ((), ()))


def first_chunk(width):
    small = width // 7
    return small if width % 7 == 0 and small % 128 == 0 else 0


def tree_sum(terms):
    while len(terms) > 1:
        terms = [a + b for a, b in zip(terms[::2], terms[1::2])] + terms[len(terms) // 2 * 2:]
    return terms[0]


def project_kernel(scales, hidden, out_grad, lengths, proj_in, proj_out, tests, out, near_tests, hid, og, pin, pout, limits, sems):
    rows, width = hidden.shape
    k_in = pin.shape[0]
    small = first_chunk(width)
    half = (width - small) // 2

    def copies_of(n):
        if isinstance(n, int) and n == 0:
            lanes = pl.ds(0, small)
        elif isinstance(n, int) and n == 1:
            return [pltpu.make_async_copy(proj_out, pout, sems.at[0, 1]), pltpu.make_async_copy(out_grad, og, sems.at[1, 1])]
        else:
            lanes = pl.ds(small + (n - 2) * half, half)
        return [
            pltpu.make_async_copy(proj_in.at[:, lanes], pin.at[:, lanes], sems.at[0, n]),
            pltpu.make_async_copy(hidden.at[:, lanes], hid.at[:, lanes], sems.at[1, n]),
        ]

    def partial(weights, data, at, size):
        depth = next(depth for depth in DEPTHS if size % depth == 0)
        terms = []
        for k in range(0, size, depth):
            lanes = pl.ds(at + k if isinstance(at, int) else pl.multiple_of(at + k, 128), depth)
            terms.append(lax.dot_general(weights[:, lanes], data[:, lanes], CONTRACT_LAST,
                                         preferred_element_type=jnp.float32))
        return tree_sum(terms)

    steps = range(0 if small else 1, 4)
    for n in steps:
        for priority, copy in enumerate(copies_of(n)):
            copy.start(priority=(priority + n) % 2)
    bounds = pltpu.make_async_copy(lengths, limits, sems.at[0, 4])
    bounds.start()
    fetch = pltpu.make_async_copy(tests, near_tests, sems.at[1, 4])
    fetch.start()
    total = jnp.zeros((k_in, rows), jnp.float32)
    if small:
        for copy in copies_of(0):
            copy.wait()
        total = partial(pin, hid, 0, small)
    for copy in copies_of(1):
        copy.wait()
    out[k_in:] = partial(pout, og, 0, og.shape[1]) * scales[1]

    def step(n, total):
        for copy in copies_of(n):
            copy.wait()
        return total + partial(pin, hid, small + (n - 2) * half, half)

    total = lax.fori_loop(2, 4, step, total)
    bounds.wait()
    slot = lax.broadcasted_iota(jnp.int32, (1, rows), 1)
    limit = jnp.zeros((1, rows), jnp.int32)
    for e in range(lengths.shape[0]):
        limit = jnp.where(slot >= e * SEQ, e * SEQ + limits[e], limit)
    out[:k_in] = jnp.where(slot < limit, total * scales[0], 0.0)
    fetch.wait()


def project(hidden, out_grad, lengths, proj_in, proj_out, test_proj, scales):
    rows, width = hidden.shape
    narrow = out_grad.shape[1]
    k_in, k_out = proj_in.shape[1], proj_out.shape[1]
    operands = (hidden, out_grad, lengths, proj_in.T, proj_out.T, test_proj)
    return pl.pallas_call(
        functools.partial(project_kernel, scales),
        out_shape=(
            jax.ShapeDtypeStruct((k_in + k_out, rows), jnp.float32),
            jax.ShapeDtypeStruct(test_proj.shape, test_proj.dtype),
        ),
        in_specs=[pl.BlockSpec(memory_space=pltpu.HBM)] * 6,
        out_specs=(pl.BlockSpec(memory_space=pltpu.VMEM),) * 2,
        scratch_shapes=[
            pltpu.VMEM((rows, width), jnp.bfloat16),
            pltpu.VMEM((rows, narrow), jnp.bfloat16),
            pltpu.VMEM((k_in, width), jnp.bfloat16),
            pltpu.VMEM((k_out, narrow), jnp.bfloat16),
            pltpu.SMEM(lengths.shape, jnp.int32),
            pltpu.SemaphoreType.DMA((2, 5)),
        ],
        compiler_params=pltpu.CompilerParams(vmem_limit_bytes=24 << 20),
        cost_estimate=pl.CostEstimate(
            flops=2 * rows * (width * k_in + narrow * k_out),
            bytes_accessed=2 * rows * (width + narrow) + 2 * (width * k_in + narrow * k_out),
            transcendentals=0,
        ),
    )(*(pltpu.with_memory_space_constraint(x, pltpu.HBM) for x in operands))


def halves(x):
    high = x.astype(jnp.bfloat16)
    return high, (x - high.astype(jnp.float32)).astype(jnp.bfloat16)


def grads_kernel(k_in, scales, *refs):
    *pieces, out = refs
    both = pieces[0][...]
    for piece in pieces[1:]:
        both = both + piece[...]
    k_out, rows = both.shape[0] - k_in, both.shape[1]
    count = rows // SEQ
    across = 128 // k_out
    act_high, act_low = halves(both[:k_in])
    grad_high, grad_low = halves(both[k_in:])
    slot = lax.broadcasted_iota(jnp.int32, (1, rows), 1)

    def by_example(act):
        return jnp.concatenate(
            [jnp.where((slot >= e * SEQ) & (slot < (e + 1) * SEQ), act, jnp.zeros_like(act)) for e in range(count)], axis=0)

    def tiled(grad):
        return jnp.concatenate([grad] * across, axis=0)

    high = by_example(act_high)
    left = jnp.concatenate([high, high, by_example(act_low)], axis=1)
    high = tiled(grad_high)
    right = jnp.concatenate([high, tiled(grad_low), high], axis=1)
    product = lax.dot_general(left, right, CONTRACT_LAST, preferred_element_type=jnp.float32)
    product = (product * (1.0 / (scales[0] * scales[1]))).astype(jnp.bfloat16).astype(jnp.float32)
    row = lax.broadcasted_iota(jnp.int32, product.shape, 0)
    lane = lax.broadcasted_iota(jnp.int32, product.shape, 1)
    product = jnp.where(row % across == lane // k_out, product, 0.0).astype(jnp.bfloat16)
    groups = k_in // across
    shape = (groups * count, count * k_in)
    to = lax.broadcasted_iota(jnp.int32, shape, 0)
    source = lax.broadcasted_iota(jnp.int32, shape, 1)
    pick = (source // k_in == to % count) & (source % k_in // across == to // count)
    picked = jnp.dot(jnp.where(pick, 1.0, 0.0).astype(jnp.bfloat16), product, preferred_element_type=jnp.float32)
    for group in range(groups):
        out[:, group * 128:(group + 1) * 128] = picked[group * count:(group + 1) * count].astype(jnp.bfloat16)


def example_grads(pieces, k_in, k_out, scales):
    vmem = pl.BlockSpec(memory_space=pltpu.VMEM)
    return pl.pallas_call(
        functools.partial(grads_kernel, k_in, scales),
        out_shape=jax.ShapeDtypeStruct((pieces[0].shape[1] // SEQ, k_in * k_out), jnp.bfloat16),
        in_specs=[vmem] * len(pieces),
        out_specs=vmem,
        compiler_params=pltpu.CompilerParams(vmem_limit_bytes=6 << 20),
        cost_estimate=pl.CostEstimate(flops=1 << 33, bytes_accessed=0, transcendentals=0),
    )(*pieces)


def finish_kernel(examples, n_pieces, n_raw, *refs):
    pieces, raw = refs[:n_pieces], refs[n_pieces:n_pieces + n_raw]
    cov, scores, block, row, sems = refs[n_pieces + n_raw:]
    own_rows, flat = cov.shape
    place = lax.axis_index(("dp", "sub"))
    every = jnp.concatenate([p[...] for p in pieces], axis=0)
    if own_rows % 128 == 0:
        at = pl.multiple_of(place * own_rows, own_rows)
        own = jnp.concatenate([p[:, pl.ds(at, own_rows)] for p in pieces], axis=0)
    else:
        at = pl.multiple_of((place * own_rows) // 128 * 128, 128)
        wider = jnp.concatenate([p[:, pl.ds(at, 128)] for p in pieces], axis=0)
        own = pltpu.roll(wider.astype(jnp.float32), at - place * own_rows + 128, 1)[:, :own_rows].astype(jnp.bfloat16)
    wide = every.astype(jnp.float32)
    total = jnp.sum(jnp.sum(wide * wide, axis=0, keepdims=True), axis=1, keepdims=True)
    factor = lax.rsqrt(total * (1.0 / examples) + 1e-06)
    if n_raw == 2:
        near, far = raw[0][...] * factor, raw[1][...] * factor
        first = lax.axis_index("sub") == 0
        half = near.shape[1]
        row[:, :half] = jnp.where(first, near, far)
        row[:, half:] = jnp.where(first, far, near)
    else:
        row[...] = raw[0][...] * factor
    copies = [pltpu.make_async_copy(row, scores, sems.at[4])]
    copies[0].start()
    step = max(own_rows // 4, 8)
    for n, at in enumerate(range(0, own_rows, step)):
        part = pl.ds(at, step)
        block[part] = lax.dot_general(own[:, at:at + step], every, CONTRACT_FIRST,
                                      preferred_element_type=jnp.float32) * (1.0 / examples)
        copies.append(pltpu.make_async_copy(block.at[part], cov.at[part], sems.at[n]))
        copies[-1].start(priority=n % 2)
    for copy in copies:
        copy.wait()


def finish(examples, own_rows, pieces, raw):
    flat = pieces[0].shape[1]
    vmem = pl.BlockSpec(memory_space=pltpu.VMEM)
    hbm = pl.BlockSpec(memory_space=pltpu.HBM)
    cov = (own_rows, flat)
    scores = (raw[0].shape[0], sum(r.shape[1] for r in raw))
    return pl.pallas_call(
        functools.partial(finish_kernel, examples, len(pieces), len(raw)),
        out_shape=(jax.ShapeDtypeStruct(cov, jnp.float32), jax.ShapeDtypeStruct(scores, jnp.float32)),
        in_specs=[vmem] * (len(pieces) + len(raw)),
        out_specs=(hbm, hbm),
        scratch_shapes=[pltpu.VMEM(cov, jnp.float32), pltpu.VMEM(scores, jnp.float32), pltpu.SemaphoreType.DMA((5,))],
        compiler_params=pltpu.CompilerParams(vmem_limit_bytes=8 << 20),
    )(*pieces, *raw)


def per_device(hidden, out_grad, lengths, proj_in, proj_out, test_proj):
    k_in, k_out = proj_in.shape[1], proj_out.shape[1]
    flat = k_in * k_out
    group = ("dp", "sub")
    sharers = lax.axis_size(group)
    examples = lengths.shape[0] * sharers
    crossed = lax.axis_size("mp") == 2 and lax.axis_size("sub") == 2
    scales = (128.0, 4.0) if crossed else (1.0, 1.0)
    both, test_proj = project(hidden, out_grad, lengths, proj_in, proj_out, test_proj, scales)
    if crossed:
        sent = lax.optimization_barrier(both.astype(jnp.float16))
        far = lax.ppermute(sent, ("mp", "sub"), [(0, 3), (1, 2), (2, 1), (3, 0)])
        near = lax.ppermute(sent, "sub", [(0, 1), (1, 0)])
        made = example_grads([far.astype(jnp.float32), near.astype(jnp.float32)], k_in, k_out, scales)
        grads = lax.ppermute(made, "sub", [(0, 1), (1, 0)])
    else:
        grads = example_grads([lax.psum(both, "mp")], k_in, k_out, scales)

    if crossed and lax.axis_size("dp") == 4:
        swap = [(i, i ^ 1) for i in range(sharers)]
        for_other = jnp.einsum("ep,qp->eq", made, test_proj, preferred_element_type=jnp.float32)
        grads, for_other = lax.optimization_barrier((grads, for_other))
        held = jnp.concatenate([made, grads], axis=0)
        fetched = lax.ppermute(held, group, list(enumerate(SWAPPED_SEND)))
        direct = lax.ppermute(held, group, list(enumerate(DIRECT_SEND)))
        gathered = [held, direct, fetched, lax.ppermute(fetched, group, swap)]
        own = jnp.einsum("ep,qp->eq", grads, test_proj, preferred_element_type=jnp.float32)
        raw = [own, lax.ppermute(for_other, group, swap)]
    else:
        tests = lax.all_gather(test_proj, "sub", axis=0, tiled=True)
        raw = [jnp.einsum("ep,qp->eq", grads, tests, preferred_element_type=jnp.float32)]
        gathered = [lax.all_gather(grads, group, axis=0, tiled=True)]
    return finish(examples, flat // sharers, gathered, raw)


def solution(mesh):
    in_specs = (
        P(("groups", "dp", "sub"), "mp"),
        P(("groups", "dp", "sub"), "mp"),
        P(("groups", "dp", "sub")),
        P("mp", None),
        P("mp", None),
        P(("mp", "sub"), None),
    )
    out_specs = (P(("groups", "dp", "sub"), None), P(("groups", "dp", "sub"), "mp"))
    return jax.shard_map(
        per_device, mesh=mesh, in_specs=in_specs, out_specs=out_specs, check_vma=False
    )
```

```python
import functools

import jax
import jax.numpy as jnp
from jax import lax
from jax.experimental import pallas as pl
from jax.experimental.pallas import tpu as pltpu
from jax.sharding import PartitionSpec as P

SEQ = 64
DEPTHS = (1024, 512, 256, 128)
SWAPPED_SEND = (3, 5, 4, 7, 6, 0, 2, 1)
DIRECT_SEND = (7, 6, 0, 1, 2, 3, 5, 4)
CONTRACT_LAST = (((1,), (1,)), ((), ()))
CONTRACT_FIRST = (((0,), (0,)), ((), ()))


def first_chunk(width):
    small = width // 7
    return small if width % 7 == 0 and small % 128 == 0 else 0


def tree_sum(terms):
    while len(terms) > 1:
        terms = [a + b for a, b in zip(terms[::2], terms[1::2])] + terms[len(terms) // 2 * 2:]
    return terms[0]


def project_kernel(scales, hidden, out_grad, lengths, proj_in, proj_out, out, hid, og, pin, pout, limits, sems):
    rows, width = hidden.shape
    k_in = pin.shape[0]
    small = first_chunk(width)
    half = (width - small) // 2

    def copies_of(n):
        if isinstance(n, int) and n == 0:
            lanes = pl.ds(0, small)
        elif isinstance(n, int) and n == 1:
            return [pltpu.make_async_copy(proj_out, pout, sems.at[0, 1]), pltpu.make_async_copy(out_grad, og, sems.at[1, 1])]
        else:
            lanes = pl.ds(small + (n - 2) * half, half)
        return [
            pltpu.make_async_copy(proj_in.at[:, lanes], pin.at[:, lanes], sems.at[0, n]),
            pltpu.make_async_copy(hidden.at[:, lanes], hid.at[:, lanes], sems.at[1, n]),
        ]

    def partial(weights, data, at, size):
        depth = next(depth for depth in DEPTHS if size % depth == 0)
        terms = []
        for k in range(0, size, depth):
            lanes = pl.ds(at + k if isinstance(at, int) else pl.multiple_of(at + k, 128), depth)
            terms.append(lax.dot_general(weights[:, lanes], data[:, lanes], CONTRACT_LAST,
                                         preferred_element_type=jnp.float32))
        return tree_sum(terms)

    steps = range(0 if small else 1, 4)
    for n in steps:
        for copy in copies_of(n):
            copy.start()
    bounds = pltpu.make_async_copy(lengths, limits, sems.at[0, 4])
    bounds.start()
    total = jnp.zeros((k_in, rows), jnp.float32)
    if small:
        for copy in copies_of(0):
            copy.wait()
        total = partial(pin, hid, 0, small)
    for copy in copies_of(1):
        copy.wait()
    out[k_in:] = partial(pout, og, 0, og.shape[1]) * scales[1]

    def step(n, total):
        for copy in copies_of(n):
            copy.wait()
        return total + partial(pin, hid, small + (n - 2) * half, half)

    total = lax.fori_loop(2, 4, step, total)
    bounds.wait()
    slot = lax.broadcasted_iota(jnp.int32, (1, rows), 1)
    limit = jnp.zeros((1, rows), jnp.int32)
    for e in range(lengths.shape[0]):
        limit = jnp.where(slot >= e * SEQ, e * SEQ + limits[e], limit)
    out[:k_in] = jnp.where(slot < limit, total * scales[0], 0.0)


def project(hidden, out_grad, lengths, proj_in, proj_out, scales):
    rows, width = hidden.shape
    narrow = out_grad.shape[1]
    k_in, k_out = proj_in.shape[1], proj_out.shape[1]
    operands = (hidden, out_grad, lengths, proj_in.T, proj_out.T)
    return pl.pallas_call(
        functools.partial(project_kernel, scales),
        out_shape=jax.ShapeDtypeStruct((k_in + k_out, rows), jnp.float32),
        in_specs=[pl.BlockSpec(memory_space=pltpu.HBM)] * 5,
        out_specs=pl.BlockSpec(memory_space=pltpu.VMEM),
        scratch_shapes=[
            pltpu.VMEM((rows, width), jnp.bfloat16),
            pltpu.VMEM((rows, narrow), jnp.bfloat16),
            pltpu.VMEM((k_in, width), jnp.bfloat16),
            pltpu.VMEM((k_out, narrow), jnp.bfloat16),
            pltpu.SMEM(lengths.shape, jnp.int32),
            pltpu.SemaphoreType.DMA((2, 5)),
        ],
        compiler_params=pltpu.CompilerParams(vmem_limit_bytes=24 << 20),
        cost_estimate=pl.CostEstimate(
            flops=2 * rows * (width * k_in + narrow * k_out),
            bytes_accessed=2 * rows * (width + narrow) + 2 * (width * k_in + narrow * k_out),
            transcendentals=0,
        ),
    )(*(pltpu.with_memory_space_constraint(x, pltpu.HBM) for x in operands))


def fetch_kernel(_, src, dst, sem):
    copy = pltpu.make_async_copy(src, dst, sem)
    copy.start()
    copy.wait()


def fetch(array, after):
    return pl.pallas_call(
        fetch_kernel,
        out_shape=jax.ShapeDtypeStruct(array.shape, array.dtype),
        in_specs=[pl.BlockSpec(memory_space=pl.ANY), pl.BlockSpec(memory_space=pltpu.HBM)],
        out_specs=pl.BlockSpec(memory_space=pltpu.VMEM),
        scratch_shapes=[pltpu.SemaphoreType.DMA(())],
        compiler_params=pltpu.CompilerParams(vmem_limit_bytes=8 << 20),
        cost_estimate=pl.CostEstimate(flops=0, bytes_accessed=4 << 20, transcendentals=0),
    )(after, pltpu.with_memory_space_constraint(array, pltpu.HBM))


def halves(x):
    high = x.astype(jnp.bfloat16)
    return high, (x - high.astype(jnp.float32)).astype(jnp.bfloat16)


def grads_kernel(k_in, scales, *refs):
    *pieces, out = refs
    both = pieces[0][...]
    for piece in pieces[1:]:
        both = both + piece[...]
    k_out, rows = both.shape[0] - k_in, both.shape[1]
    count = rows // SEQ
    across = 128 // k_out
    act_high, act_low = halves(both[:k_in])
    grad_high, grad_low = halves(both[k_in:])
    slot = lax.broadcasted_iota(jnp.int32, (1, rows), 1)

    def by_example(act):
        return jnp.concatenate(
            [jnp.where((slot >= e * SEQ) & (slot < (e + 1) * SEQ), act, jnp.zeros_like(act)) for e in range(count)], axis=0)

    def tiled(grad):
        return jnp.concatenate([grad] * across, axis=0)

    high = by_example(act_high)
    left = jnp.concatenate([high, high, by_example(act_low)], axis=1)
    high = tiled(grad_high)
    right = jnp.concatenate([high, tiled(grad_low), high], axis=1)
    product = lax.dot_general(left, right, CONTRACT_LAST, preferred_element_type=jnp.float32)
    product = (product * (1.0 / (scales[0] * scales[1]))).astype(jnp.bfloat16).astype(jnp.float32)
    row = lax.broadcasted_iota(jnp.int32, product.shape, 0)
    lane = lax.broadcasted_iota(jnp.int32, product.shape, 1)
    product = jnp.where(row % across == lane // k_out, product, 0.0).astype(jnp.bfloat16)
    groups = k_in // across
    shape = (groups * count, count * k_in)
    to = lax.broadcasted_iota(jnp.int32, shape, 0)
    source = lax.broadcasted_iota(jnp.int32, shape, 1)
    pick = (source // k_in == to % count) & (source % k_in // across == to // count)
    picked = jnp.dot(jnp.where(pick, 1.0, 0.0).astype(jnp.bfloat16), product, preferred_element_type=jnp.float32)
    for group in range(groups):
        out[:, group * 128:(group + 1) * 128] = picked[group * count:(group + 1) * count].astype(jnp.bfloat16)


def example_grads(pieces, k_in, k_out, scales):
    vmem = pl.BlockSpec(memory_space=pltpu.VMEM)
    return pl.pallas_call(
        functools.partial(grads_kernel, k_in, scales),
        out_shape=jax.ShapeDtypeStruct((pieces[0].shape[1] // SEQ, k_in * k_out), jnp.bfloat16),
        in_specs=[vmem] * len(pieces),
        out_specs=vmem,
        compiler_params=pltpu.CompilerParams(vmem_limit_bytes=6 << 20),
        cost_estimate=pl.CostEstimate(flops=1 << 33, bytes_accessed=0, transcendentals=0),
    )(*pieces)


def finish_kernel(examples, n_pieces, n_raw, *refs):
    pieces, raw = refs[:n_pieces], refs[n_pieces:n_pieces + n_raw]
    cov, scores, block, row, sems = refs[n_pieces + n_raw:]
    own_rows, flat = cov.shape
    place = lax.axis_index(("dp", "sub"))
    every = jnp.concatenate([p[...] for p in pieces], axis=0)
    if own_rows % 128 == 0:
        at = pl.multiple_of(place * own_rows, own_rows)
        own = jnp.concatenate([p[:, pl.ds(at, own_rows)] for p in pieces], axis=0)
    else:
        at = pl.multiple_of((place * own_rows) // 128 * 128, 128)
        wider = jnp.concatenate([p[:, pl.ds(at, 128)] for p in pieces], axis=0)
        own = pltpu.roll(wider.astype(jnp.float32), at - place * own_rows + 128, 1)[:, :own_rows].astype(jnp.bfloat16)
    wide = every.astype(jnp.float32)
    total = jnp.sum(jnp.sum(wide * wide, axis=0, keepdims=True), axis=1, keepdims=True)
    factor = lax.rsqrt(total * (1.0 / examples) + 1e-06)
    if n_raw == 2:
        near, far = raw[0][...] * factor, raw[1][...] * factor
        first = lax.axis_index("sub") == 0
        half = near.shape[1]
        row[:, :half] = jnp.where(first, near, far)
        row[:, half:] = jnp.where(first, far, near)
    else:
        row[...] = raw[0][...] * factor
    copies = [pltpu.make_async_copy(row, scores, sems.at[4])]
    copies[0].start()
    step = max(own_rows // 4, 8)
    for n, at in enumerate(range(0, own_rows, step)):
        part = pl.ds(at, step)
        block[part] = lax.dot_general(own[:, at:at + step], every, CONTRACT_FIRST,
                                      preferred_element_type=jnp.float32) * (1.0 / examples)
        copies.append(pltpu.make_async_copy(block.at[part], cov.at[part], sems.at[n]))
        copies[-1].start()
    for copy in copies:
        copy.wait()


def finish(examples, own_rows, pieces, raw):
    flat = pieces[0].shape[1]
    vmem = pl.BlockSpec(memory_space=pltpu.VMEM)
    hbm = pl.BlockSpec(memory_space=pltpu.HBM)
    cov = (own_rows, flat)
    scores = (raw[0].shape[0], sum(r.shape[1] for r in raw))
    return pl.pallas_call(
        functools.partial(finish_kernel, examples, len(pieces), len(raw)),
        out_shape=(jax.ShapeDtypeStruct(cov, jnp.float32), jax.ShapeDtypeStruct(scores, jnp.float32)),
        in_specs=[vmem] * (len(pieces) + len(raw)),
        out_specs=(hbm, hbm),
        scratch_shapes=[pltpu.VMEM(cov, jnp.float32), pltpu.VMEM(scores, jnp.float32), pltpu.SemaphoreType.DMA((5,))],
        compiler_params=pltpu.CompilerParams(vmem_limit_bytes=8 << 20),
    )(*pieces, *raw)


def per_device(hidden, out_grad, lengths, proj_in, proj_out, test_proj):
    k_in, k_out = proj_in.shape[1], proj_out.shape[1]
    flat = k_in * k_out
    group = ("dp", "sub")
    sharers = lax.axis_size(group)
    examples = lengths.shape[0] * sharers
    crossed = lax.axis_size("mp") == 2 and lax.axis_size("sub") == 2
    scales = (128.0, 4.0) if crossed else (1.0, 1.0)
    both = project(hidden, out_grad, lengths, proj_in, proj_out, scales)
    if crossed:
        sent = lax.optimization_barrier(both.astype(jnp.float16))
        far = lax.ppermute(sent, ("mp", "sub"), [(0, 3), (1, 2), (2, 1), (3, 0)])
        test_proj = fetch(test_proj, both)
        swapped, test_proj = lax.optimization_barrier((sent, test_proj))
        near = lax.ppermute(swapped, "sub", [(0, 1), (1, 0)])
        made = example_grads([near.astype(jnp.float32), far.astype(jnp.float32)], k_in, k_out, scales)
        grads = lax.ppermute(made, "sub", [(0, 1), (1, 0)])
    else:
        grads = example_grads([lax.psum(both, "mp")], k_in, k_out, scales)

    if crossed and lax.axis_size("dp") == 4:
        swap = [(i, i ^ 1) for i in range(sharers)]
        for_other = jnp.einsum("ep,qp->eq", made, test_proj, preferred_element_type=jnp.float32)
        grads, for_other = lax.optimization_barrier((grads, for_other))
        held = jnp.concatenate([made, grads], axis=0)
        fetched = lax.ppermute(held, group, list(enumerate(SWAPPED_SEND)))
        direct = lax.ppermute(held, group, list(enumerate(DIRECT_SEND)))
        gathered = [held, direct, fetched, lax.ppermute(fetched, group, swap)]
        own = jnp.einsum("ep,qp->eq", grads, test_proj, preferred_element_type=jnp.float32)
        raw = [own, lax.ppermute(for_other, group, swap)]
    else:
        tests = lax.all_gather(test_proj, "sub", axis=0, tiled=True)
        raw = [jnp.einsum("ep,qp->eq", grads, tests, preferred_element_type=jnp.float32)]
        gathered = [lax.all_gather(grads, group, axis=0, tiled=True)]
    return finish(examples, flat // sharers, gathered, raw)


def solution(mesh):
    in_specs = (
        P(("groups", "dp", "sub"), "mp"),
        P(("groups", "dp", "sub"), "mp"),
        P(("groups", "dp", "sub")),
        P("mp", None),
        P("mp", None),
        P(("mp", "sub"), None),
    )
    out_specs = (P(("groups", "dp", "sub"), None), P(("groups", "dp", "sub"), "mp"))
    return jax.shard_map(
        per_device, mesh=mesh, in_specs=in_specs, out_specs=out_specs, check_vma=False
    )
```

```python
import functools

import jax
import jax.numpy as jnp
from jax import lax
from jax.experimental import pallas as pl
from jax.experimental.pallas import tpu as pltpu
from jax.sharding import PartitionSpec as P

SEQ = 64
DEPTHS = (1024, 512, 256, 128)
SWAPPED_SEND = (3, 5, 4, 7, 6, 0, 2, 1)
DIRECT_SEND = (7, 6, 0, 1, 2, 3, 5, 4)
CONTRACT_LAST = (((1,), (1,)), ((), ()))
CONTRACT_FIRST = (((0,), (0,)), ((), ()))


def first_chunk(width):
    small = width // 7
    return small if width % 7 == 0 and small % 128 == 0 else 0


def tree_sum(terms):
    while len(terms) > 1:
        terms = [a + b for a, b in zip(terms[::2], terms[1::2])] + terms[len(terms) // 2 * 2:]
    return terms[0]


def project_kernel(scales, hidden, out_grad, lengths, proj_in, proj_out, tests, out, near_tests, hid, og, pin, pout, limits, sems):
    rows, width = hidden.shape
    k_in = pin.shape[0]
    small = first_chunk(width)
    half = (width - small) // 2

    def copies_of(n):
        if isinstance(n, int) and n == 0:
            lanes = pl.ds(0, small)
        elif isinstance(n, int) and n == 1:
            return [pltpu.make_async_copy(proj_out, pout, sems.at[0, 1]), pltpu.make_async_copy(out_grad, og, sems.at[1, 1])]
        else:
            lanes = pl.ds(small + (n - 2) * half, half)
        return [
            pltpu.make_async_copy(proj_in.at[:, lanes], pin.at[:, lanes], sems.at[0, n]),
            pltpu.make_async_copy(hidden.at[:, lanes], hid.at[:, lanes], sems.at[1, n]),
        ]

    def partial(weights, data, at, size):
        depth = next(depth for depth in DEPTHS if size % depth == 0)
        terms = []
        for k in range(0, size, depth):
            lanes = pl.ds(at + k if isinstance(at, int) else pl.multiple_of(at + k, 128), depth)
            terms.append(lax.dot_general(weights[:, lanes], data[:, lanes], CONTRACT_LAST,
                                         preferred_element_type=jnp.float32))
        return tree_sum(terms)

    steps = range(0 if small else 1, 4)
    for n in steps:
        for copy in copies_of(n):
            copy.start()
    bounds = pltpu.make_async_copy(lengths, limits, sems.at[0, 4])
    bounds.start()
    fetch = pltpu.make_async_copy(tests, near_tests, sems.at[1, 4])
    fetch.start()
    total = jnp.zeros((k_in, rows), jnp.float32)
    if small:
        for copy in copies_of(0):
            copy.wait()
        total = partial(pin, hid, 0, small)
    for copy in copies_of(1):
        copy.wait()
    out[k_in:] = partial(pout, og, 0, og.shape[1]) * scales[1]

    def step(n, total):
        for copy in copies_of(n):
            copy.wait()
        return total + partial(pin, hid, small + (n - 2) * half, half)

    total = lax.fori_loop(2, 4, step, total)
    bounds.wait()
    slot = lax.broadcasted_iota(jnp.int32, (1, rows), 1)
    limit = jnp.zeros((1, rows), jnp.int32)
    for e in range(lengths.shape[0]):
        limit = jnp.where(slot >= e * SEQ, e * SEQ + limits[e], limit)
    out[:k_in] = jnp.where(slot < limit, total * scales[0], 0.0)
    fetch.wait()


def project(hidden, out_grad, lengths, proj_in, proj_out, test_proj, scales):
    rows, width = hidden.shape
    narrow = out_grad.shape[1]
    k_in, k_out = proj_in.shape[1], proj_out.shape[1]
    operands = (hidden, out_grad, lengths, proj_in.T, proj_out.T, test_proj)
    return pl.pallas_call(
        functools.partial(project_kernel, scales),
        out_shape=(
            jax.ShapeDtypeStruct((k_in + k_out, rows), jnp.float32),
            jax.ShapeDtypeStruct(test_proj.shape, test_proj.dtype),
        ),
        in_specs=[pl.BlockSpec(memory_space=pltpu.HBM)] * 6,
        out_specs=(pl.BlockSpec(memory_space=pltpu.VMEM),) * 2,
        scratch_shapes=[
            pltpu.VMEM((rows, width), jnp.bfloat16),
            pltpu.VMEM((rows, narrow), jnp.bfloat16),
            pltpu.VMEM((k_in, width), jnp.bfloat16),
            pltpu.VMEM((k_out, narrow), jnp.bfloat16),
            pltpu.SMEM(lengths.shape, jnp.int32),
            pltpu.SemaphoreType.DMA((2, 5)),
        ],
        compiler_params=pltpu.CompilerParams(vmem_limit_bytes=24 << 20),
        cost_estimate=pl.CostEstimate(
            flops=2 * rows * (width * k_in + narrow * k_out),
            bytes_accessed=2 * rows * (width + narrow) + 2 * (width * k_in + narrow * k_out),
            transcendentals=0,
        ),
    )(*(pltpu.with_memory_space_constraint(x, pltpu.HBM) for x in operands))


def halves(x):
    high = x.astype(jnp.bfloat16)
    return high, (x - high.astype(jnp.float32)).astype(jnp.bfloat16)


def grads_kernel(k_in, scales, *refs):
    *pieces, out, summed, placed = refs
    both = pieces[0][...]
    for piece in pieces[1:]:
        both = both + piece[...]
    k_out, slots = both.shape[0] - k_in, both.shape[1]
    for n in range(slots // 128):
        summed[n] = both[:k_in, n * 128:(n + 1) * 128]
    count = slots // SEQ
    across = 128 // k_out
    groups = k_in // across
    slot = lax.broadcasted_iota(jnp.int32, (1, slots), 1)
    left = []
    for first in range(across):
        act = jnp.concatenate([summed[n, pl.ds(first, groups, stride=across), :] for n in range(slots // 128)], axis=1)
        left += [jnp.where((slot >= e * SEQ) & (slot < (e + 1) * SEQ), act, 0.0) for e in range(count)]
    high, low = halves(jnp.concatenate(left, axis=0))
    left = jnp.concatenate([high, high, low], axis=1)
    high, low = (jnp.concatenate([part] * across, axis=0) for part in halves(both[k_in:]))
    right = jnp.concatenate([high, low, high], axis=1)
    product = lax.dot_general(left, right, CONTRACT_LAST, preferred_element_type=jnp.float32)
    size = count * groups
    lane = lax.broadcasted_iota(jnp.int32, (size, 128), 1)
    kept = product[:size]
    for first in range(1, across):
        kept = jnp.where(lane // k_out == first, product[first * size:(first + 1) * size], kept)
    placed[...] = kept * (1.0 / (scales[0] * scales[1]))
    for group in range(groups):
        out[:, group * 128:(group + 1) * 128] = placed[pl.ds(group, count, stride=groups), :].astype(jnp.bfloat16)


def example_grads(pieces, k_in, k_out, scales):
    vmem = pl.BlockSpec(memory_space=pltpu.VMEM)
    return pl.pallas_call(
        functools.partial(grads_kernel, k_in, scales),
        out_shape=jax.ShapeDtypeStruct((pieces[0].shape[1] // SEQ, k_in * k_out), jnp.bfloat16),
        in_specs=[vmem] * len(pieces),
        out_specs=vmem,
        scratch_shapes=[
            pltpu.VMEM((pieces[0].shape[1] // 128, k_in, 128), jnp.float32),
            pltpu.VMEM((pieces[0].shape[1] // SEQ * k_in * k_out // 128, 128), jnp.float32),
        ],
        compiler_params=pltpu.CompilerParams(vmem_limit_bytes=6 << 20),
        cost_estimate=pl.CostEstimate(flops=1 << 33, bytes_accessed=0, transcendentals=0),
    )(*pieces)


def finish_kernel(examples, n_pieces, n_raw, *refs):
    pieces, raw = refs[:n_pieces], refs[n_pieces:n_pieces + n_raw]
    cov, scores, block, row, sems = refs[n_pieces + n_raw:]
    own_rows, flat = cov.shape
    place = lax.axis_index(("dp", "sub"))
    every = jnp.concatenate([p[...] for p in pieces], axis=0)
    if own_rows % 128 == 0:
        at = pl.multiple_of(place * own_rows, own_rows)
        own = jnp.concatenate([p[:, pl.ds(at, own_rows)] for p in pieces], axis=0)
    else:
        at = pl.multiple_of((place * own_rows) // 128 * 128, 128)
        wider = jnp.concatenate([p[:, pl.ds(at, 128)] for p in pieces], axis=0)
        own = pltpu.roll(wider.astype(jnp.float32), (at - place * own_rows + 128) % 128, 1)[:, :own_rows].astype(jnp.bfloat16)
    wide = every.astype(jnp.float32)
    total = jnp.sum(jnp.sum(wide * wide, axis=0, keepdims=True), axis=1, keepdims=True)
    factor = lax.rsqrt(total * (1.0 / examples) + 1e-06)
    if n_raw == 2:
        near, far = raw[0][...] * factor, raw[1][...] * factor
        first = lax.axis_index("sub") == 0
        half = near.shape[1]
        row[:, :half] = jnp.where(first, near, far)
        row[:, half:] = jnp.where(first, far, near)
    else:
        row[...] = raw[0][...] * factor
    copies = [pltpu.make_async_copy(row, scores, sems.at[4])]
    copies[0].start()
    step = max(own_rows // 4, 8)
    for n, at in enumerate(range(0, own_rows, step)):
        part = pl.ds(at, step)
        block[part] = lax.dot_general(own[:, at:at + step], every, CONTRACT_FIRST,
                                      preferred_element_type=jnp.float32) * (1.0 / examples)
        copies.append(pltpu.make_async_copy(block.at[part], cov.at[part], sems.at[n]))
        copies[-1].start()
    for copy in copies:
        copy.wait()


def finish(examples, own_rows, pieces, raw):
    flat = pieces[0].shape[1]
    vmem = pl.BlockSpec(memory_space=pltpu.VMEM)
    hbm = pl.BlockSpec(memory_space=pltpu.HBM)
    cov = (own_rows, flat)
    scores = (raw[0].shape[0], sum(r.shape[1] for r in raw))
    return pl.pallas_call(
        functools.partial(finish_kernel, examples, len(pieces), len(raw)),
        out_shape=(jax.ShapeDtypeStruct(cov, jnp.float32), jax.ShapeDtypeStruct(scores, jnp.float32)),
        in_specs=[vmem] * (len(pieces) + len(raw)),
        out_specs=(hbm, hbm),
        scratch_shapes=[pltpu.VMEM(cov, jnp.float32), pltpu.VMEM(scores, jnp.float32), pltpu.SemaphoreType.DMA((5,))],
        compiler_params=pltpu.CompilerParams(vmem_limit_bytes=8 << 20),
    )(*pieces, *raw)


def per_device(hidden, out_grad, lengths, proj_in, proj_out, test_proj):
    k_in, k_out = proj_in.shape[1], proj_out.shape[1]
    flat = k_in * k_out
    group = ("dp", "sub")
    sharers = lax.axis_size(group)
    examples = lengths.shape[0] * sharers
    crossed = lax.axis_size("mp") == 2 and lax.axis_size("sub") == 2
    scales = (128.0, 4.0) if crossed else (1.0, 1.0)
    both, test_proj = project(hidden, out_grad, lengths, proj_in, proj_out, test_proj, scales)
    if crossed:
        sent = lax.optimization_barrier(both.astype(jnp.float16))
        far = lax.ppermute(sent, ("mp", "sub"), [(0, 3), (1, 2), (2, 1), (3, 0)])
        near = lax.ppermute(sent, "sub", [(0, 1), (1, 0)])
        made = example_grads([far.astype(jnp.float32), near.astype(jnp.float32)], k_in, k_out, scales)
        grads = lax.ppermute(made, "sub", [(0, 1), (1, 0)])
    else:
        grads = example_grads([lax.psum(both, "mp")], k_in, k_out, scales)

    if crossed and lax.axis_size("dp") == 4:
        swap = [(i, i ^ 1) for i in range(sharers)]
        for_other = jnp.einsum("ep,qp->eq", made, test_proj, preferred_element_type=jnp.float32)
        grads, for_other = lax.optimization_barrier((grads, for_other))
        held = jnp.concatenate([made, grads], axis=0)
        fetched = lax.ppermute(held, group, list(enumerate(SWAPPED_SEND)))
        direct = lax.ppermute(held, group, list(enumerate(DIRECT_SEND)))
        gathered = [held, direct, fetched, lax.ppermute(fetched, group, swap)]
        own = jnp.einsum("ep,qp->eq", grads, test_proj, preferred_element_type=jnp.float32)
        raw = [own, lax.ppermute(for_other, group, swap)]
    else:
        tests = lax.all_gather(test_proj, "sub", axis=0, tiled=True)
        raw = [jnp.einsum("ep,qp->eq", grads, tests, preferred_element_type=jnp.float32)]
        gathered = [lax.all_gather(grads, group, axis=0, tiled=True)]
    return finish(examples, flat // sharers, gathered, raw)


def solution(mesh):
    in_specs = (
        P(("groups", "dp", "sub"), "mp"),
        P(("groups", "dp", "sub"), "mp"),
        P(("groups", "dp", "sub")),
        P("mp", None),
        P("mp", None),
        P(("mp", "sub"), None),
    )
    out_specs = (P(("groups", "dp", "sub"), None), P(("groups", "dp", "sub"), "mp"))
    return jax.shard_map(
        per_device, mesh=mesh, in_specs=in_specs, out_specs=out_specs, check_vma=False
    )
```

```python
import functools

import jax
import jax.numpy as jnp
from jax import lax
from jax.experimental import pallas as pl
from jax.experimental.pallas import tpu as pltpu
from jax.sharding import PartitionSpec as P

SEQ = 64
DEPTHS = (1024, 512, 256, 128)
SWAPPED_SEND = (3, 5, 4, 7, 6, 0, 2, 1)
DIRECT_SEND = (7, 6, 0, 1, 2, 3, 5, 4)
CONTRACT_LAST = (((1,), (1,)), ((), ()))
CONTRACT_FIRST = (((0,), (0,)), ((), ()))


def first_chunk(width):
    small = width // 7
    return small if width % 7 == 0 and small % 128 == 0 else 0


def tree_sum(terms):
    while len(terms) > 1:
        terms = [a + b for a, b in zip(terms[::2], terms[1::2])] + terms[len(terms) // 2 * 2:]
    return terms[0]


def project_kernel(scales, hidden, out_grad, lengths, proj_in, proj_out, tests, out, near_tests, hid, og, pin, pout, limits, sems):
    rows, width = hidden.shape
    k_in = pin.shape[0]
    small = first_chunk(width)
    half = (width - small) // 2

    def copies_of(n):
        if isinstance(n, int) and n == 0:
            lanes = pl.ds(0, small)
        elif isinstance(n, int) and n == 1:
            return [pltpu.make_async_copy(proj_out, pout, sems.at[0, 1]), pltpu.make_async_copy(out_grad, og, sems.at[1, 1])]
        else:
            lanes = pl.ds(small + (n - 2) * half, half)
        return [
            pltpu.make_async_copy(proj_in.at[:, lanes], pin.at[:, lanes], sems.at[0, n]),
            pltpu.make_async_copy(hidden.at[:, lanes], hid.at[:, lanes], sems.at[1, n]),
        ]

    def partial(weights, data, at, size):
        depth = next(depth for depth in DEPTHS if size % depth == 0)
        terms = []
        for k in range(0, size, depth):
            lanes = pl.ds(at + k if isinstance(at, int) else pl.multiple_of(at + k, 128), depth)
            terms.append(lax.dot_general(weights[:, lanes], data[:, lanes], CONTRACT_LAST,
                                         preferred_element_type=jnp.float32))
        return tree_sum(terms)

    steps = range(0 if small else 1, 4)
    for n in steps:
        for copy in copies_of(n):
            copy.start()
    bounds = pltpu.make_async_copy(lengths, limits, sems.at[0, 4])
    bounds.start()
    fetch = pltpu.make_async_copy(tests, near_tests, sems.at[1, 4])
    fetch.start()
    total = jnp.zeros((k_in, rows), jnp.float32)
    if small:
        for copy in copies_of(0):
            copy.wait()
        total = partial(pin, hid, 0, small)
    for copy in copies_of(1):
        copy.wait()
    out[k_in:] = partial(pout, og, 0, og.shape[1]) * scales[1]

    def step(n, total):
        for copy in copies_of(n):
            copy.wait()
        return total + partial(pin, hid, small + (n - 2) * half, half)

    total = lax.fori_loop(2, 4, step, total)
    bounds.wait()
    slot = lax.broadcasted_iota(jnp.int32, (1, rows), 1)
    limit = jnp.zeros((1, rows), jnp.int32)
    for e in range(lengths.shape[0]):
        limit = jnp.where(slot >= e * SEQ, e * SEQ + limits[e], limit)
    out[:k_in] = jnp.where(slot < limit, total * scales[0], 0.0)
    fetch.wait()


def project(hidden, out_grad, lengths, proj_in, proj_out, test_proj, scales):
    rows, width = hidden.shape
    narrow = out_grad.shape[1]
    k_in, k_out = proj_in.shape[1], proj_out.shape[1]
    operands = (hidden, out_grad, lengths, proj_in.T, proj_out.T, test_proj)
    return pl.pallas_call(
        functools.partial(project_kernel, scales),
        out_shape=(
            jax.ShapeDtypeStruct((k_in + k_out, rows), jnp.float32),
            jax.ShapeDtypeStruct(test_proj.shape, test_proj.dtype),
        ),
        in_specs=[pl.BlockSpec(memory_space=pltpu.HBM)] * 6,
        out_specs=(pl.BlockSpec(memory_space=pltpu.VMEM),) * 2,
        scratch_shapes=[
            pltpu.VMEM((rows, width), jnp.bfloat16),
            pltpu.VMEM((rows, narrow), jnp.bfloat16),
            pltpu.VMEM((k_in, width), jnp.bfloat16),
            pltpu.VMEM((k_out, narrow), jnp.bfloat16),
            pltpu.SMEM(lengths.shape, jnp.int32),
            pltpu.SemaphoreType.DMA((2, 5)),
        ],
        compiler_params=pltpu.CompilerParams(vmem_limit_bytes=24 << 20),
        cost_estimate=pl.CostEstimate(
            flops=2 * rows * (width * k_in + narrow * k_out),
            bytes_accessed=2 * rows * (width + narrow) + 2 * (width * k_in + narrow * k_out),
            transcendentals=0,
        ),
    )(*(pltpu.with_memory_space_constraint(x, pltpu.HBM) for x in operands))


def halves(x):
    high = x.astype(jnp.bfloat16)
    return high, (x - high.astype(jnp.float32)).astype(jnp.bfloat16)


def grads_kernel(k_in, scales, *refs):
    *pieces, out, summed, placed = refs
    both = pieces[0][...]
    for piece in pieces[1:]:
        both = both + piece[...]
    k_out, slots = both.shape[0] - k_in, both.shape[1]
    for n in range(slots // 128):
        summed[n] = both[:k_in, n * 128:(n + 1) * 128]
    count = slots // SEQ
    across = 128 // k_out
    groups = k_in // across
    slot = lax.broadcasted_iota(jnp.int32, (1, slots), 1)
    left = []
    for first in range(across):
        act = jnp.concatenate([summed[n, pl.ds(first, groups, stride=across), :] for n in range(slots // 128)], axis=1)
        left += [jnp.where((slot >= e * SEQ) & (slot < (e + 1) * SEQ), act, 0.0) for e in range(count)]
    high, low = halves(jnp.concatenate(left, axis=0))
    left = jnp.concatenate([high, high, low], axis=1)
    high, low = (jnp.concatenate([part] * across, axis=0) for part in halves(both[k_in:]))
    right = jnp.concatenate([high, low, high], axis=1)
    product = lax.dot_general(left, right, CONTRACT_LAST, preferred_element_type=jnp.float32)
    size = count * groups
    lane = lax.broadcasted_iota(jnp.int32, (size, 128), 1)
    kept = product[:size]
    for first in range(1, across):
        kept = jnp.where(lane // k_out == first, product[first * size:(first + 1) * size], kept)
    placed[...] = kept * (1.0 / (scales[0] * scales[1]))
    for group in range(groups):
        out[:, group * 128:(group + 1) * 128] = placed[pl.ds(group, count, stride=groups), :].astype(jnp.bfloat16)


def example_grads(pieces, k_in, k_out, scales):
    vmem = pl.BlockSpec(memory_space=pltpu.VMEM)
    return pl.pallas_call(
        functools.partial(grads_kernel, k_in, scales),
        out_shape=jax.ShapeDtypeStruct((pieces[0].shape[1] // SEQ, k_in * k_out), jnp.bfloat16),
        in_specs=[vmem] * len(pieces),
        out_specs=vmem,
        scratch_shapes=[
            pltpu.VMEM((pieces[0].shape[1] // 128, k_in, 128), jnp.float32),
            pltpu.VMEM((pieces[0].shape[1] // SEQ * k_in * k_out // 128, 128), jnp.float32),
        ],
        compiler_params=pltpu.CompilerParams(vmem_limit_bytes=6 << 20),
        cost_estimate=pl.CostEstimate(flops=1 << 33, bytes_accessed=0, transcendentals=0),
    )(*pieces)


def finish_kernel(examples, n_pieces, n_raw, *refs):
    pieces, raw = refs[:n_pieces], refs[n_pieces:n_pieces + n_raw]
    cov, scores, block, row, sems = refs[n_pieces + n_raw:]
    own_rows, flat = cov.shape
    place = lax.axis_index(("dp", "sub"))
    every = jnp.concatenate([p[...] for p in pieces], axis=0)
    if own_rows % 128 == 0:
        at = pl.multiple_of(place * own_rows, own_rows)
        own = jnp.concatenate([p[:, pl.ds(at, own_rows)] for p in pieces], axis=0)
    else:
        at = pl.multiple_of((place * own_rows) // 128 * 128, 128)
        wider = jnp.concatenate([p[:, pl.ds(at, 128)] for p in pieces], axis=0)
        own = pltpu.roll(wider.astype(jnp.float32), (at - place * own_rows + 128) % 128, 1)[:, :own_rows].astype(jnp.bfloat16)
    wide = every.astype(jnp.float32)
    total = jnp.sum(jnp.sum(wide * wide, axis=0, keepdims=True), axis=1, keepdims=True)
    factor = lax.rsqrt(total * (1.0 / examples) + 1e-06)
    if n_raw == 2:
        near, far = raw[0][...] * factor, raw[1][...] * factor
        first = lax.axis_index("sub") == 0
        half = near.shape[1]
        row[:, :half] = jnp.where(first, near, far)
        row[:, half:] = jnp.where(first, far, near)
    else:
        row[...] = raw[0][...] * factor
    copies = [pltpu.make_async_copy(row, scores, sems.at[4])]
    copies[0].start()
    step = max(own_rows // 4, 8)
    for n, at in enumerate(range(0, own_rows, step)):
        part = pl.ds(at, step)
        block[part] = lax.dot_general(own[:, at:at + step], every, CONTRACT_FIRST,
                                      preferred_element_type=jnp.float32) * (1.0 / examples)
        copies.append(pltpu.make_async_copy(block.at[part], cov.at[part], sems.at[n]))
        copies[-1].start()
    for copy in copies:
        copy.wait()


def finish(examples, own_rows, pieces, raw):
    flat = pieces[0].shape[1]
    vmem = pl.BlockSpec(memory_space=pltpu.VMEM)
    hbm = pl.BlockSpec(memory_space=pltpu.HBM)
    cov = (own_rows, flat)
    scores = (raw[0].shape[0], sum(r.shape[1] for r in raw))
    return pl.pallas_call(
        functools.partial(finish_kernel, examples, len(pieces), len(raw)),
        out_shape=(jax.ShapeDtypeStruct(cov, jnp.float32), jax.ShapeDtypeStruct(scores, jnp.float32)),
        in_specs=[vmem] * (len(pieces) + len(raw)),
        out_specs=(hbm, hbm),
        scratch_shapes=[pltpu.VMEM(cov, jnp.float32), pltpu.VMEM(scores, jnp.float32), pltpu.SemaphoreType.DMA((5,))],
        compiler_params=pltpu.CompilerParams(vmem_limit_bytes=8 << 20),
    )(*pieces, *raw)


def per_device(hidden, out_grad, lengths, proj_in, proj_out, test_proj):
    k_in, k_out = proj_in.shape[1], proj_out.shape[1]
    flat = k_in * k_out
    group = ("dp", "sub")
    sharers = lax.axis_size(group)
    examples = lengths.shape[0] * sharers
    crossed = lax.axis_size("mp") == 2 and lax.axis_size("sub") == 2
    scales = (128.0, 4.0) if crossed else (1.0, 1.0)
    both, test_proj = project(hidden, out_grad, lengths, proj_in, proj_out, test_proj, scales)
    if crossed:
        sent = lax.optimization_barrier(both.astype(jnp.float16))
        far = lax.ppermute(sent, ("mp", "sub"), [(0, 3), (1, 2), (2, 1), (3, 0)])
        near = lax.ppermute(sent, "sub", [(0, 1), (1, 0)])
        made = example_grads([near.astype(jnp.float32), far.astype(jnp.float32)], k_in, k_out, scales)
        grads = lax.ppermute(made, "sub", [(0, 1), (1, 0)])
    else:
        grads = example_grads([lax.psum(both, "mp")], k_in, k_out, scales)

    if crossed and lax.axis_size("dp") == 4:
        swap = [(i, i ^ 1) for i in range(sharers)]
        for_other = jnp.einsum("ep,qp->eq", made, test_proj, preferred_element_type=jnp.float32)
        grads, for_other = lax.optimization_barrier((grads, for_other))
        held = jnp.concatenate([made, grads], axis=0)
        fetched = lax.ppermute(held, group, list(enumerate(SWAPPED_SEND)))
        direct = lax.ppermute(held, group, list(enumerate(DIRECT_SEND)))
        gathered = [held, direct, fetched, lax.ppermute(fetched, group, swap)]
        own = jnp.einsum("ep,qp->eq", grads, test_proj, preferred_element_type=jnp.float32)
        raw = [own, lax.ppermute(for_other, group, swap)]
    else:
        tests = lax.all_gather(test_proj, "sub", axis=0, tiled=True)
        raw = [jnp.einsum("ep,qp->eq", grads, tests, preferred_element_type=jnp.float32)]
        gathered = [lax.all_gather(grads, group, axis=0, tiled=True)]
    return finish(examples, flat // sharers, gathered, raw)


def solution(mesh):
    in_specs = (
        P(("groups", "dp", "sub"), "mp"),
        P(("groups", "dp", "sub"), "mp"),
        P(("groups", "dp", "sub")),
        P("mp", None),
        P("mp", None),
        P(("mp", "sub"), None),
    )
    out_specs = (P(("groups", "dp", "sub"), None), P(("groups", "dp", "sub"), "mp"))
    return jax.shard_map(
        per_device, mesh=mesh, in_specs=in_specs, out_specs=out_specs, check_vma=False
    )
```

```python
import functools

import jax
import jax.numpy as jnp
from jax import lax
from jax.experimental import pallas as pl
from jax.experimental.pallas import tpu as pltpu
from jax.sharding import PartitionSpec as P

SEQ = 64
DEPTHS = (1024, 512, 256, 128)
SWAPPED_SEND = (3, 5, 4, 7, 6, 0, 2, 1)
DIRECT_SEND = (7, 6, 0, 1, 2, 3, 5, 4)
CONTRACT_LAST = (((1,), (1,)), ((), ()))
CONTRACT_FIRST = (((0,), (0,)), ((), ()))


def first_chunk(width):
    small = width // 14 * 3
    return small if width % 14 == 0 and small % 128 == 0 and (width - small) % 256 == 0 else 0


def tree_sum(terms):
    while len(terms) > 1:
        terms = [a + b for a, b in zip(terms[::2], terms[1::2])] + terms[len(terms) // 2 * 2:]
    return terms[0]


def project_kernel(scales, hidden, out_grad, lengths, proj_in, proj_out, tests, out, near_tests, hid, og, pin, pout, limits, sems):
    rows, width = hidden.shape
    k_in = pin.shape[0]
    small = first_chunk(width)
    half = (width - small) // 2

    def copies_of(n):
        if isinstance(n, int) and n == 0:
            lanes = pl.ds(0, small)
        elif isinstance(n, int) and n == 1:
            return [pltpu.make_async_copy(proj_out, pout, sems.at[0, 1]), pltpu.make_async_copy(out_grad, og, sems.at[1, 1])]
        else:
            lanes = pl.ds(small + (n - 2) * half, half)
        return [
            pltpu.make_async_copy(proj_in.at[:, lanes], pin.at[:, lanes], sems.at[0, n]),
            pltpu.make_async_copy(hidden.at[:, lanes], hid.at[:, lanes], sems.at[1, n]),
        ]

    def partial(weights, data, at, size):
        depth = next(depth for depth in DEPTHS if size % depth == 0)
        terms = []
        for k in range(0, size, depth):
            lanes = pl.ds(at + k if isinstance(at, int) else pl.multiple_of(at + k, 128), depth)
            terms.append(lax.dot_general(weights[:, lanes], data[:, lanes], CONTRACT_LAST,
                                         preferred_element_type=jnp.float32))
        return tree_sum(terms)

    steps = range(0 if small else 1, 4)
    for n in steps:
        for copy in copies_of(n):
            copy.start()
    bounds = pltpu.make_async_copy(lengths, limits, sems.at[0, 4])
    bounds.start()
    fetch = pltpu.make_async_copy(tests, near_tests, sems.at[1, 4])
    fetch.start()
    total = jnp.zeros((k_in, rows), jnp.float32)
    if small:
        for copy in copies_of(0):
            copy.wait()
        total = partial(pin, hid, 0, small)
    for copy in copies_of(1):
        copy.wait()
    out[k_in:] = partial(pout, og, 0, og.shape[1]) * scales[1]

    def step(n, total):
        for copy in copies_of(n):
            copy.wait()
        return total + partial(pin, hid, small + (n - 2) * half, half)

    total = lax.fori_loop(2, 4, step, total)
    bounds.wait()
    slot = lax.broadcasted_iota(jnp.int32, (1, rows), 1)
    limit = jnp.zeros((1, rows), jnp.int32)
    for e in range(lengths.shape[0]):
        limit = jnp.where(slot >= e * SEQ, e * SEQ + limits[e], limit)
    out[:k_in] = jnp.where(slot < limit, total * scales[0], 0.0)
    fetch.wait()


def project(hidden, out_grad, lengths, proj_in, proj_out, test_proj, scales):
    rows, width = hidden.shape
    narrow = out_grad.shape[1]
    k_in, k_out = proj_in.shape[1], proj_out.shape[1]
    operands = (hidden, out_grad, lengths, proj_in.T, proj_out.T, test_proj)
    return pl.pallas_call(
        functools.partial(project_kernel, scales),
        out_shape=(
            jax.ShapeDtypeStruct((k_in + k_out, rows), jnp.float32),
            jax.ShapeDtypeStruct(test_proj.shape, test_proj.dtype),
        ),
        in_specs=[pl.BlockSpec(memory_space=pltpu.HBM)] * 6,
        out_specs=(pl.BlockSpec(memory_space=pltpu.VMEM),) * 2,
        scratch_shapes=[
            pltpu.VMEM((rows, width), jnp.bfloat16),
            pltpu.VMEM((rows, narrow), jnp.bfloat16),
            pltpu.VMEM((k_in, width), jnp.bfloat16),
            pltpu.VMEM((k_out, narrow), jnp.bfloat16),
            pltpu.SMEM(lengths.shape, jnp.int32),
            pltpu.SemaphoreType.DMA((2, 5)),
        ],
        compiler_params=pltpu.CompilerParams(vmem_limit_bytes=24 << 20),
        cost_estimate=pl.CostEstimate(
            flops=2 * rows * (width * k_in + narrow * k_out),
            bytes_accessed=2 * rows * (width + narrow) + 2 * (width * k_in + narrow * k_out),
            transcendentals=0,
        ),
    )(*(pltpu.with_memory_space_constraint(x, pltpu.HBM) for x in operands))


def halves(x):
    high = x.astype(jnp.bfloat16)
    return high, (x - high.astype(jnp.float32)).astype(jnp.bfloat16)


def grads_kernel(k_in, scales, *refs):
    *pieces, out, summed, placed = refs
    both = pieces[0][...]
    for piece in pieces[1:]:
        both = both + piece[...]
    k_out, slots = both.shape[0] - k_in, both.shape[1]
    for n in range(slots // 128):
        summed[n] = both[:k_in, n * 128:(n + 1) * 128]
    count = slots // SEQ
    across = 128 // k_out
    groups = k_in // across
    slot = lax.broadcasted_iota(jnp.int32, (1, slots), 1)
    left = []
    for first in range(across):
        act = jnp.concatenate([summed[n, pl.ds(first, groups, stride=across), :] for n in range(slots // 128)], axis=1)
        left += [jnp.where((slot >= e * SEQ) & (slot < (e + 1) * SEQ), act, 0.0) for e in range(count)]
    high, low = halves(jnp.concatenate(left, axis=0))
    left = jnp.concatenate([high, high, low], axis=1)
    high, low = (jnp.concatenate([part] * across, axis=0) for part in halves(both[k_in:]))
    right = jnp.concatenate([high, low, high], axis=1)
    product = lax.dot_general(left, right, CONTRACT_LAST, preferred_element_type=jnp.float32)
    size = count * groups
    lane = lax.broadcasted_iota(jnp.int32, (size, 128), 1)
    kept = product[:size]
    for first in range(1, across):
        kept = jnp.where(lane // k_out == first, product[first * size:(first + 1) * size], kept)
    placed[...] = kept * (1.0 / (scales[0] * scales[1]))
    for group in range(groups):
        out[:, group * 128:(group + 1) * 128] = placed[pl.ds(group, count, stride=groups), :].astype(jnp.bfloat16)


def example_grads(pieces, k_in, k_out, scales):
    vmem = pl.BlockSpec(memory_space=pltpu.VMEM)
    return pl.pallas_call(
        functools.partial(grads_kernel, k_in, scales),
        out_shape=jax.ShapeDtypeStruct((pieces[0].shape[1] // SEQ, k_in * k_out), jnp.bfloat16),
        in_specs=[vmem] * len(pieces),
        out_specs=vmem,
        scratch_shapes=[
            pltpu.VMEM((pieces[0].shape[1] // 128, k_in, 128), jnp.float32),
            pltpu.VMEM((pieces[0].shape[1] // SEQ * k_in * k_out // 128, 128), jnp.float32),
        ],
        compiler_params=pltpu.CompilerParams(vmem_limit_bytes=6 << 20),
        cost_estimate=pl.CostEstimate(flops=1 << 33, bytes_accessed=0, transcendentals=0),
    )(*pieces)


def finish_kernel(examples, n_pieces, n_raw, *refs):
    pieces, raw = refs[:n_pieces], refs[n_pieces:n_pieces + n_raw]
    cov, scores, block, row, sems = refs[n_pieces + n_raw:]
    own_rows, flat = cov.shape
    place = lax.axis_index(("dp", "sub"))
    every = jnp.concatenate([p[...] for p in pieces], axis=0)
    if own_rows % 128 == 0:
        at = pl.multiple_of(place * own_rows, own_rows)
        own = jnp.concatenate([p[:, pl.ds(at, own_rows)] for p in pieces], axis=0)
    else:
        at = pl.multiple_of((place * own_rows) // 128 * 128, 128)
        wider = jnp.concatenate([p[:, pl.ds(at, 128)] for p in pieces], axis=0)
        own = pltpu.roll(wider.astype(jnp.float32), (at - place * own_rows + 128) % 128, 1)[:, :own_rows].astype(jnp.bfloat16)
    wide = every.astype(jnp.float32)
    total = jnp.sum(jnp.sum(wide * wide, axis=0, keepdims=True), axis=1, keepdims=True)
    factor = lax.rsqrt(total * (1.0 / examples) + 1e-06)
    if n_raw == 2:
        near, far = raw[0][...] * factor, raw[1][...] * factor
        first = lax.axis_index("sub") == 0
        half = near.shape[1]
        row[:, :half] = jnp.where(first, near, far)
        row[:, half:] = jnp.where(first, far, near)
    else:
        row[...] = raw[0][...] * factor
    copies = [pltpu.make_async_copy(row, scores, sems.at[4])]
    copies[0].start()
    step = max(own_rows // 4, 8)
    for n, at in enumerate(range(0, own_rows, step)):
        part = pl.ds(at, step)
        block[part] = lax.dot_general(own[:, at:at + step], every, CONTRACT_FIRST,
                                      preferred_element_type=jnp.float32) * (1.0 / examples)
        copies.append(pltpu.make_async_copy(block.at[part], cov.at[part], sems.at[n]))
        copies[-1].start()
    for copy in copies:
        copy.wait()


def finish(examples, own_rows, pieces, raw):
    flat = pieces[0].shape[1]
    vmem = pl.BlockSpec(memory_space=pltpu.VMEM)
    hbm = pl.BlockSpec(memory_space=pltpu.HBM)
    cov = (own_rows, flat)
    scores = (raw[0].shape[0], sum(r.shape[1] for r in raw))
    return pl.pallas_call(
        functools.partial(finish_kernel, examples, len(pieces), len(raw)),
        out_shape=(jax.ShapeDtypeStruct(cov, jnp.float32), jax.ShapeDtypeStruct(scores, jnp.float32)),
        in_specs=[vmem] * (len(pieces) + len(raw)),
        out_specs=(hbm, hbm),
        scratch_shapes=[pltpu.VMEM(cov, jnp.float32), pltpu.VMEM(scores, jnp.float32), pltpu.SemaphoreType.DMA((5,))],
        compiler_params=pltpu.CompilerParams(vmem_limit_bytes=8 << 20),
    )(*pieces, *raw)


def per_device(hidden, out_grad, lengths, proj_in, proj_out, test_proj):
    k_in, k_out = proj_in.shape[1], proj_out.shape[1]
    flat = k_in * k_out
    group = ("dp", "sub")
    sharers = lax.axis_size(group)
    examples = lengths.shape[0] * sharers
    crossed = lax.axis_size("mp") == 2 and lax.axis_size("sub") == 2
    scales = (128.0, 4.0) if crossed else (1.0, 1.0)
    both, test_proj = project(hidden, out_grad, lengths, proj_in, proj_out, test_proj, scales)
    if crossed:
        sent = lax.optimization_barrier(both.astype(jnp.float16))
        far = lax.ppermute(sent, ("mp", "sub"), [(0, 3), (1, 2), (2, 1), (3, 0)])
        near = lax.ppermute(sent, "sub", [(0, 1), (1, 0)])
        made = example_grads([near.astype(jnp.float32), far.astype(jnp.float32)], k_in, k_out, scales)
        grads = lax.ppermute(made, "sub", [(0, 1), (1, 0)])
    else:
        grads = example_grads([lax.psum(both, "mp")], k_in, k_out, scales)

    if crossed and lax.axis_size("dp") == 4:
        swap = [(i, i ^ 1) for i in range(sharers)]
        for_other = jnp.einsum("ep,qp->eq", made, test_proj, preferred_element_type=jnp.float32)
        grads, for_other = lax.optimization_barrier((grads, for_other))
        held = jnp.concatenate([made, grads], axis=0)
        fetched = lax.ppermute(held, group, list(enumerate(SWAPPED_SEND)))
        direct = lax.ppermute(held, group, list(enumerate(DIRECT_SEND)))
        gathered = [held, direct, fetched, lax.ppermute(fetched, group, swap)]
        own = jnp.einsum("ep,qp->eq", grads, test_proj, preferred_element_type=jnp.float32)
        raw = [own, lax.ppermute(for_other, group, swap)]
    else:
        tests = lax.all_gather(test_proj, "sub", axis=0, tiled=True)
        raw = [jnp.einsum("ep,qp->eq", grads, tests, preferred_element_type=jnp.float32)]
        gathered = [lax.all_gather(grads, group, axis=0, tiled=True)]
    return finish(examples, flat // sharers, gathered, raw)


def solution(mesh):
    in_specs = (
        P(("groups", "dp", "sub"), "mp"),
        P(("groups", "dp", "sub"), "mp"),
        P(("groups", "dp", "sub")),
        P("mp", None),
        P("mp", None),
        P(("mp", "sub"), None),
    )
    out_specs = (P(("groups", "dp", "sub"), None), P(("groups", "dp", "sub"), "mp"))
    return jax.shard_map(
        per_device, mesh=mesh, in_specs=in_specs, out_specs=out_specs, check_vma=False
    )
```

```python
import functools

import jax
import jax.numpy as jnp
from jax import lax
from jax.experimental import pallas as pl
from jax.experimental.pallas import tpu as pltpu
from jax.sharding import PartitionSpec as P

SEQ = 64
DEPTHS = (1024, 512, 256, 128)
SWAPPED_SEND = (3, 5, 4, 7, 6, 0, 2, 1)
DIRECT_SEND = (7, 6, 0, 1, 2, 3, 5, 4)
CONTRACT_LAST = (((1,), (1,)), ((), ()))
CONTRACT_FIRST = (((0,), (0,)), ((), ()))


def first_chunk(width):
    small = width // 14
    return small if width % 14 == 0 and small % 128 == 0 and (width - small) % 256 == 0 else 0


def tree_sum(terms):
    while len(terms) > 1:
        terms = [a + b for a, b in zip(terms[::2], terms[1::2])] + terms[len(terms) // 2 * 2:]
    return terms[0]


def project_kernel(scales, hidden, out_grad, lengths, proj_in, proj_out, tests, out, near_tests, hid, og, pin, pout, limits, sems):
    rows, width = hidden.shape
    k_in = pin.shape[0]
    small = first_chunk(width)
    half = (width - small) // 2

    def copies_of(n):
        if isinstance(n, int) and n == 0:
            lanes = pl.ds(0, small)
        elif isinstance(n, int) and n == 1:
            return [pltpu.make_async_copy(proj_out, pout, sems.at[0, 1]), pltpu.make_async_copy(out_grad, og, sems.at[1, 1])]
        else:
            lanes = pl.ds(small + (n - 2) * half, half)
        return [
            pltpu.make_async_copy(proj_in.at[:, lanes], pin.at[:, lanes], sems.at[0, n]),
            pltpu.make_async_copy(hidden.at[:, lanes], hid.at[:, lanes], sems.at[1, n]),
        ]

    def partial(weights, data, at, size):
        depth = next(depth for depth in DEPTHS if size % depth == 0)
        terms = []
        for k in range(0, size, depth):
            lanes = pl.ds(at + k if isinstance(at, int) else pl.multiple_of(at + k, 128), depth)
            terms.append(lax.dot_general(weights[:, lanes], data[:, lanes], CONTRACT_LAST,
                                         preferred_element_type=jnp.float32))
        return tree_sum(terms)

    steps = range(0 if small else 1, 4)
    for n in steps:
        for copy in copies_of(n):
            copy.start()
    bounds = pltpu.make_async_copy(lengths, limits, sems.at[0, 4])
    bounds.start()
    fetch = pltpu.make_async_copy(tests, near_tests, sems.at[1, 4])
    fetch.start()
    total = jnp.zeros((k_in, rows), jnp.float32)
    if small:
        for copy in copies_of(0):
            copy.wait()
        total = partial(pin, hid, 0, small)
    for copy in copies_of(1):
        copy.wait()
    out[k_in:] = partial(pout, og, 0, og.shape[1]) * scales[1]

    def step(n, total):
        for copy in copies_of(n):
            copy.wait()
        return total + partial(pin, hid, small + (n - 2) * half, half)

    total = lax.fori_loop(2, 4, step, total)
    bounds.wait()
    slot = lax.broadcasted_iota(jnp.int32, (1, rows), 1)
    limit = jnp.zeros((1, rows), jnp.int32)
    for e in range(lengths.shape[0]):
        limit = jnp.where(slot >= e * SEQ, e * SEQ + limits[e], limit)
    out[:k_in] = jnp.where(slot < limit, total * scales[0], 0.0)
    fetch.wait()


def project(hidden, out_grad, lengths, proj_in, proj_out, test_proj, scales):
    rows, width = hidden.shape
    narrow = out_grad.shape[1]
    k_in, k_out = proj_in.shape[1], proj_out.shape[1]
    operands = (hidden, out_grad, lengths, proj_in.T, proj_out.T, test_proj)
    return pl.pallas_call(
        functools.partial(project_kernel, scales),
        out_shape=(
            jax.ShapeDtypeStruct((k_in + k_out, rows), jnp.float32),
            jax.ShapeDtypeStruct(test_proj.shape, test_proj.dtype),
        ),
        in_specs=[pl.BlockSpec(memory_space=pltpu.HBM)] * 6,
        out_specs=(pl.BlockSpec(memory_space=pltpu.VMEM),) * 2,
        scratch_shapes=[
            pltpu.VMEM((rows, width), jnp.bfloat16),
            pltpu.VMEM((rows, narrow), jnp.bfloat16),
            pltpu.VMEM((k_in, width), jnp.bfloat16),
            pltpu.VMEM((k_out, narrow), jnp.bfloat16),
            pltpu.SMEM(lengths.shape, jnp.int32),
            pltpu.SemaphoreType.DMA((2, 5)),
        ],
        compiler_params=pltpu.CompilerParams(vmem_limit_bytes=24 << 20),
        cost_estimate=pl.CostEstimate(
            flops=2 * rows * (width * k_in + narrow * k_out),
            bytes_accessed=2 * rows * (width + narrow) + 2 * (width * k_in + narrow * k_out),
            transcendentals=0,
        ),
    )(*(pltpu.with_memory_space_constraint(x, pltpu.HBM) for x in operands))


def halves(x):
    high = x.astype(jnp.bfloat16)
    return high, (x - high.astype(jnp.float32)).astype(jnp.bfloat16)


def grads_kernel(k_in, scales, *refs):
    *pieces, out, summed, placed = refs
    both = pieces[0][...]
    for piece in pieces[1:]:
        both = both + piece[...]
    k_out, slots = both.shape[0] - k_in, both.shape[1]
    for n in range(slots // 128):
        summed[n] = both[:k_in, n * 128:(n + 1) * 128]
    count = slots // SEQ
    across = 128 // k_out
    groups = k_in // across
    slot = lax.broadcasted_iota(jnp.int32, (1, slots), 1)
    left = []
    for first in range(across):
        act = jnp.concatenate([summed[n, pl.ds(first, groups, stride=across), :] for n in range(slots // 128)], axis=1)
        left += [jnp.where((slot >= e * SEQ) & (slot < (e + 1) * SEQ), act, 0.0) for e in range(count)]
    high, low = halves(jnp.concatenate(left, axis=0))
    left = jnp.concatenate([high, high, low], axis=1)
    high, low = (jnp.concatenate([part] * across, axis=0) for part in halves(both[k_in:]))
    right = jnp.concatenate([high, low, high], axis=1)
    product = lax.dot_general(left, right, CONTRACT_LAST, preferred_element_type=jnp.float32)
    size = count * groups
    lane = lax.broadcasted_iota(jnp.int32, (size, 128), 1)
    kept = product[:size]
    for first in range(1, across):
        kept = jnp.where(lane // k_out == first, product[first * size:(first + 1) * size], kept)
    placed[...] = kept * (1.0 / (scales[0] * scales[1]))
    for group in range(groups):
        out[:, group * 128:(group + 1) * 128] = placed[pl.ds(group, count, stride=groups), :].astype(jnp.bfloat16)


def example_grads(pieces, k_in, k_out, scales):
    vmem = pl.BlockSpec(memory_space=pltpu.VMEM)
    return pl.pallas_call(
        functools.partial(grads_kernel, k_in, scales),
        out_shape=jax.ShapeDtypeStruct((pieces[0].shape[1] // SEQ, k_in * k_out), jnp.bfloat16),
        in_specs=[vmem] * len(pieces),
        out_specs=vmem,
        scratch_shapes=[
            pltpu.VMEM((pieces[0].shape[1] // 128, k_in, 128), jnp.float32),
            pltpu.VMEM((pieces[0].shape[1] // SEQ * k_in * k_out // 128, 128), jnp.float32),
        ],
        compiler_params=pltpu.CompilerParams(vmem_limit_bytes=6 << 20),
        cost_estimate=pl.CostEstimate(flops=1 << 33, bytes_accessed=0, transcendentals=0),
    )(*pieces)


def finish_kernel(examples, n_pieces, n_raw, *refs):
    pieces, raw = refs[:n_pieces], refs[n_pieces:n_pieces + n_raw]
    cov, scores, block, row, sems = refs[n_pieces + n_raw:]
    own_rows, flat = cov.shape
    place = lax.axis_index(("dp", "sub"))
    every = jnp.concatenate([p[...] for p in pieces], axis=0)
    if own_rows % 128 == 0:
        at = pl.multiple_of(place * own_rows, own_rows)
        own = jnp.concatenate([p[:, pl.ds(at, own_rows)] for p in pieces], axis=0)
    else:
        at = pl.multiple_of((place * own_rows) // 128 * 128, 128)
        wider = jnp.concatenate([p[:, pl.ds(at, 128)] for p in pieces], axis=0)
        own = pltpu.roll(wider.astype(jnp.float32), (at - place * own_rows + 128) % 128, 1)[:, :own_rows].astype(jnp.bfloat16)
    wide = every.astype(jnp.float32)
    total = jnp.sum(jnp.sum(wide * wide, axis=0, keepdims=True), axis=1, keepdims=True)
    factor = lax.rsqrt(total * (1.0 / examples) + 1e-06)
    if n_raw == 2:
        near, far = raw[0][...] * factor, raw[1][...] * factor
        first = lax.axis_index("sub") == 0
        half = near.shape[1]
        row[:, :half] = jnp.where(first, near, far)
        row[:, half:] = jnp.where(first, far, near)
    else:
        row[...] = raw[0][...] * factor
    copies = [pltpu.make_async_copy(row, scores, sems.at[4])]
    copies[0].start()
    step = max(own_rows // 4, 8)
    for n, at in enumerate(range(0, own_rows, step)):
        part = pl.ds(at, step)
        block[part] = lax.dot_general(own[:, at:at + step], every, CONTRACT_FIRST,
                                      preferred_element_type=jnp.float32) * (1.0 / examples)
        copies.append(pltpu.make_async_copy(block.at[part], cov.at[part], sems.at[n]))
        copies[-1].start()
    for copy in copies:
        copy.wait()


def finish(examples, own_rows, pieces, raw):
    flat = pieces[0].shape[1]
    vmem = pl.BlockSpec(memory_space=pltpu.VMEM)
    hbm = pl.BlockSpec(memory_space=pltpu.HBM)
    cov = (own_rows, flat)
    scores = (raw[0].shape[0], sum(r.shape[1] for r in raw))
    return pl.pallas_call(
        functools.partial(finish_kernel, examples, len(pieces), len(raw)),
        out_shape=(jax.ShapeDtypeStruct(cov, jnp.float32), jax.ShapeDtypeStruct(scores, jnp.float32)),
        in_specs=[vmem] * (len(pieces) + len(raw)),
        out_specs=(hbm, hbm),
        scratch_shapes=[pltpu.VMEM(cov, jnp.float32), pltpu.VMEM(scores, jnp.float32), pltpu.SemaphoreType.DMA((5,))],
        compiler_params=pltpu.CompilerParams(vmem_limit_bytes=8 << 20),
    )(*pieces, *raw)


def per_device(hidden, out_grad, lengths, proj_in, proj_out, test_proj):
    k_in, k_out = proj_in.shape[1], proj_out.shape[1]
    flat = k_in * k_out
    group = ("dp", "sub")
    sharers = lax.axis_size(group)
    examples = lengths.shape[0] * sharers
    crossed = lax.axis_size("mp") == 2 and lax.axis_size("sub") == 2
    scales = (128.0, 4.0) if crossed else (1.0, 1.0)
    both, test_proj = project(hidden, out_grad, lengths, proj_in, proj_out, test_proj, scales)
    if crossed:
        sent = lax.optimization_barrier(both.astype(jnp.float16))
        far = lax.ppermute(sent, ("mp", "sub"), [(0, 3), (1, 2), (2, 1), (3, 0)])
        near = lax.ppermute(sent, "sub", [(0, 1), (1, 0)])
        made = example_grads([near.astype(jnp.float32), far.astype(jnp.float32)], k_in, k_out, scales)
        grads = lax.ppermute(made, "sub", [(0, 1), (1, 0)])
    else:
        grads = example_grads([lax.psum(both, "mp")], k_in, k_out, scales)

    if crossed and lax.axis_size("dp") == 4:
        swap = [(i, i ^ 1) for i in range(sharers)]
        for_other = jnp.einsum("ep,qp->eq", made, test_proj, preferred_element_type=jnp.float32)
        grads, for_other = lax.optimization_barrier((grads, for_other))
        held = jnp.concatenate([made, grads], axis=0)
        fetched = lax.ppermute(held, group, list(enumerate(SWAPPED_SEND)))
        direct = lax.ppermute(held, group, list(enumerate(DIRECT_SEND)))
        gathered = [held, direct, fetched, lax.ppermute(fetched, group, swap)]
        own = jnp.einsum("ep,qp->eq", grads, test_proj, preferred_element_type=jnp.float32)
        raw = [own, lax.ppermute(for_other, group, swap)]
    else:
        tests = lax.all_gather(test_proj, "sub", axis=0, tiled=True)
        raw = [jnp.einsum("ep,qp->eq", grads, tests, preferred_element_type=jnp.float32)]
        gathered = [lax.all_gather(grads, group, axis=0, tiled=True)]
    return finish(examples, flat // sharers, gathered, raw)


def solution(mesh):
    in_specs = (
        P(("groups", "dp", "sub"), "mp"),
        P(("groups", "dp", "sub"), "mp"),
        P(("groups", "dp", "sub")),
        P("mp", None),
        P("mp", None),
        P(("mp", "sub"), None),
    )
    out_specs = (P(("groups", "dp", "sub"), None), P(("groups", "dp", "sub"), "mp"))
    return jax.shard_map(
        per_device, mesh=mesh, in_specs=in_specs, out_specs=out_specs, check_vma=False
    )
```

```python
import functools

import jax
import jax.numpy as jnp
from jax import lax
from jax.experimental import pallas as pl
from jax.experimental.pallas import tpu as pltpu
from jax.sharding import PartitionSpec as P

SEQ = 64
DEPTHS = (1024, 512, 256, 128)
SWAPPED_SEND = (3, 5, 4, 7, 6, 0, 2, 1)
DIRECT_SEND = (7, 6, 0, 1, 2, 3, 5, 4)
CONTRACT_LAST = (((1,), (1,)), ((), ()))
CONTRACT_FIRST = (((0,), (0,)), ((), ()))


def first_chunk(width):
    small = width // 7
    return small if width % 7 == 0 and small % 128 == 0 else 0


def tree_sum(terms):
    while len(terms) > 1:
        terms = [a + b for a, b in zip(terms[::2], terms[1::2])] + terms[len(terms) // 2 * 2:]
    return terms[0]


def project_kernel(scales, hidden, out_grad, lengths, proj_in, proj_out, tests, out, near_tests, hid, og, pin, pout, limits, sems):
    rows, width = hidden.shape
    k_in = pin.shape[0]
    small = first_chunk(width)
    third = (width - small) // 3

    def copies_of(n):
        if isinstance(n, int) and n == 0:
            lanes = pl.ds(0, small)
        elif isinstance(n, int) and n == 1:
            return [pltpu.make_async_copy(proj_out, pout, sems.at[0, 1]), pltpu.make_async_copy(out_grad, og, sems.at[1, 1])]
        else:
            lanes = pl.ds(small + (n - 2) * third, third)
        return [
            pltpu.make_async_copy(proj_in.at[:, lanes], pin.at[:, lanes], sems.at[0, n]),
            pltpu.make_async_copy(hidden.at[:, lanes], hid.at[:, lanes], sems.at[1, n]),
        ]

    def partial(weights, data, at, size):
        depth = next(depth for depth in DEPTHS if size % depth == 0)
        terms = []
        for k in range(0, size, depth):
            lanes = pl.ds(at + k if isinstance(at, int) else pl.multiple_of(at + k, 128), depth)
            terms.append(lax.dot_general(weights[:, lanes], data[:, lanes], CONTRACT_LAST,
                                         preferred_element_type=jnp.float32))
        return tree_sum(terms)

    steps = range(0 if small else 1, 5)
    for n in steps:
        for copy in copies_of(n):
            copy.start()
    bounds = pltpu.make_async_copy(lengths, limits, sems.at[0, 5])
    bounds.start()
    fetch = pltpu.make_async_copy(tests, near_tests, sems.at[1, 5])
    fetch.start()
    total = jnp.zeros((k_in, rows), jnp.float32)
    if small:
        for copy in copies_of(0):
            copy.wait()
        total = partial(pin, hid, 0, small)
    for copy in copies_of(1):
        copy.wait()
    out[k_in:] = partial(pout, og, 0, og.shape[1]) * scales[1]

    def step(n, total):
        for copy in copies_of(n):
            copy.wait()
        return total + partial(pin, hid, small + (n - 2) * third, third)

    total = lax.fori_loop(2, 5, step, total)
    bounds.wait()
    slot = lax.broadcasted_iota(jnp.int32, (1, rows), 1)
    limit = jnp.zeros((1, rows), jnp.int32)
    for e in range(lengths.shape[0]):
        limit = jnp.where(slot >= e * SEQ, e * SEQ + limits[e], limit)
    out[:k_in] = jnp.where(slot < limit, total * scales[0], 0.0)
    fetch.wait()


def project(hidden, out_grad, lengths, proj_in, proj_out, test_proj, scales):
    rows, width = hidden.shape
    narrow = out_grad.shape[1]
    k_in, k_out = proj_in.shape[1], proj_out.shape[1]
    operands = (hidden, out_grad, lengths, proj_in.T, proj_out.T, test_proj)
    return pl.pallas_call(
        functools.partial(project_kernel, scales),
        out_shape=(
            jax.ShapeDtypeStruct((k_in + k_out, rows), jnp.float32),
            jax.ShapeDtypeStruct(test_proj.shape, test_proj.dtype),
        ),
        in_specs=[pl.BlockSpec(memory_space=pltpu.HBM)] * 6,
        out_specs=(pl.BlockSpec(memory_space=pltpu.VMEM),) * 2,
        scratch_shapes=[
            pltpu.VMEM((rows, width), jnp.bfloat16),
            pltpu.VMEM((rows, narrow), jnp.bfloat16),
            pltpu.VMEM((k_in, width), jnp.bfloat16),
            pltpu.VMEM((k_out, narrow), jnp.bfloat16),
            pltpu.SMEM(lengths.shape, jnp.int32),
            pltpu.SemaphoreType.DMA((2, 6)),
        ],
        compiler_params=pltpu.CompilerParams(vmem_limit_bytes=24 << 20),
        cost_estimate=pl.CostEstimate(
            flops=2 * rows * (width * k_in + narrow * k_out),
            bytes_accessed=2 * rows * (width + narrow) + 2 * (width * k_in + narrow * k_out),
            transcendentals=0,
        ),
    )(*(pltpu.with_memory_space_constraint(x, pltpu.HBM) for x in operands))


def halves(x):
    high = x.astype(jnp.bfloat16)
    return high, (x - high.astype(jnp.float32)).astype(jnp.bfloat16)


def grads_kernel(k_in, scales, *refs):
    *pieces, out, summed, placed = refs
    both = pieces[0][...]
    for piece in pieces[1:]:
        both = both + piece[...]
    k_out, slots = both.shape[0] - k_in, both.shape[1]
    for n in range(slots // 128):
        summed[n] = both[:k_in, n * 128:(n + 1) * 128]
    count = slots // SEQ
    across = 128 // k_out
    groups = k_in // across
    slot = lax.broadcasted_iota(jnp.int32, (1, slots), 1)
    left = []
    for first in range(across):
        act = jnp.concatenate([summed[n, pl.ds(first, groups, stride=across), :] for n in range(slots // 128)], axis=1)
        left += [jnp.where((slot >= e * SEQ) & (slot < (e + 1) * SEQ), act, 0.0) for e in range(count)]
    high, low = halves(jnp.concatenate(left, axis=0))
    left = jnp.concatenate([high, high, low], axis=1)
    high, low = (jnp.concatenate([part] * across, axis=0) for part in halves(both[k_in:]))
    right = jnp.concatenate([high, low, high], axis=1)
    product = lax.dot_general(left, right, CONTRACT_LAST, preferred_element_type=jnp.float32)
    size = count * groups
    lane = lax.broadcasted_iota(jnp.int32, (size, 128), 1)
    kept = product[:size]
    for first in range(1, across):
        kept = jnp.where(lane // k_out == first, product[first * size:(first + 1) * size], kept)
    placed[...] = kept * (1.0 / (scales[0] * scales[1]))
    for group in range(groups):
        out[:, group * 128:(group + 1) * 128] = placed[pl.ds(group, count, stride=groups), :].astype(jnp.bfloat16)


def example_grads(pieces, k_in, k_out, scales):
    vmem = pl.BlockSpec(memory_space=pltpu.VMEM)
    return pl.pallas_call(
        functools.partial(grads_kernel, k_in, scales),
        out_shape=jax.ShapeDtypeStruct((pieces[0].shape[1] // SEQ, k_in * k_out), jnp.bfloat16),
        in_specs=[vmem] * len(pieces),
        out_specs=vmem,
        scratch_shapes=[
            pltpu.VMEM((pieces[0].shape[1] // 128, k_in, 128), jnp.float32),
            pltpu.VMEM((pieces[0].shape[1] // SEQ * k_in * k_out // 128, 128), jnp.float32),
        ],
        compiler_params=pltpu.CompilerParams(vmem_limit_bytes=6 << 20),
        cost_estimate=pl.CostEstimate(flops=1 << 33, bytes_accessed=0, transcendentals=0),
    )(*pieces)


def finish_kernel(examples, n_pieces, n_raw, *refs):
    pieces, raw = refs[:n_pieces], refs[n_pieces:n_pieces + n_raw]
    cov, scores, block, row, sems = refs[n_pieces + n_raw:]
    own_rows, flat = cov.shape
    place = lax.axis_index(("dp", "sub"))
    every = jnp.concatenate([p[...] for p in pieces], axis=0)
    if own_rows % 128 == 0:
        at = pl.multiple_of(place * own_rows, own_rows)
        own = jnp.concatenate([p[:, pl.ds(at, own_rows)] for p in pieces], axis=0)
    else:
        at = pl.multiple_of((place * own_rows) // 128 * 128, 128)
        wider = jnp.concatenate([p[:, pl.ds(at, 128)] for p in pieces], axis=0)
        own = pltpu.roll(wider.astype(jnp.float32), (at - place * own_rows + 128) % 128, 1)[:, :own_rows].astype(jnp.bfloat16)
    wide = every.astype(jnp.float32)
    total = jnp.sum(jnp.sum(wide * wide, axis=0, keepdims=True), axis=1, keepdims=True)
    factor = lax.rsqrt(total * (1.0 / examples) + 1e-06)
    if n_raw == 2:
        near, far = raw[0][...] * factor, raw[1][...] * factor
        first = lax.axis_index("sub") == 0
        half = near.shape[1]
        row[:, :half] = jnp.where(first, near, far)
        row[:, half:] = jnp.where(first, far, near)
    else:
        row[...] = raw[0][...] * factor
    copies = [pltpu.make_async_copy(row, scores, sems.at[4])]
    copies[0].start()
    step = max(own_rows // 4, 8)
    for n, at in enumerate(range(0, own_rows, step)):
        part = pl.ds(at, step)
        block[part] = lax.dot_general(own[:, at:at + step], every, CONTRACT_FIRST,
                                      preferred_element_type=jnp.float32) * (1.0 / examples)
        copies.append(pltpu.make_async_copy(block.at[part], cov.at[part], sems.at[n]))
        copies[-1].start()
    for copy in copies:
        copy.wait()


def finish(examples, own_rows, pieces, raw):
    flat = pieces[0].shape[1]
    vmem = pl.BlockSpec(memory_space=pltpu.VMEM)
    hbm = pl.BlockSpec(memory_space=pltpu.HBM)
    cov = (own_rows, flat)
    scores = (raw[0].shape[0], sum(r.shape[1] for r in raw))
    return pl.pallas_call(
        functools.partial(finish_kernel, examples, len(pieces), len(raw)),
        out_shape=(jax.ShapeDtypeStruct(cov, jnp.float32), jax.ShapeDtypeStruct(scores, jnp.float32)),
        in_specs=[vmem] * (len(pieces) + len(raw)),
        out_specs=(hbm, hbm),
        scratch_shapes=[pltpu.VMEM(cov, jnp.float32), pltpu.VMEM(scores, jnp.float32), pltpu.SemaphoreType.DMA((5,))],
        compiler_params=pltpu.CompilerParams(vmem_limit_bytes=8 << 20),
    )(*pieces, *raw)


def per_device(hidden, out_grad, lengths, proj_in, proj_out, test_proj):
    k_in, k_out = proj_in.shape[1], proj_out.shape[1]
    flat = k_in * k_out
    group = ("dp", "sub")
    sharers = lax.axis_size(group)
    examples = lengths.shape[0] * sharers
    crossed = lax.axis_size("mp") == 2 and lax.axis_size("sub") == 2
    scales = (128.0, 4.0) if crossed else (1.0, 1.0)
    both, test_proj = project(hidden, out_grad, lengths, proj_in, proj_out, test_proj, scales)
    if crossed:
        sent = lax.optimization_barrier(both.astype(jnp.float16))
        far = lax.ppermute(sent, ("mp", "sub"), [(0, 3), (1, 2), (2, 1), (3, 0)])
        near = lax.ppermute(sent, "sub", [(0, 1), (1, 0)])
        made = example_grads([near.astype(jnp.float32), far.astype(jnp.float32)], k_in, k_out, scales)
        grads = lax.ppermute(made, "sub", [(0, 1), (1, 0)])
    else:
        grads = example_grads([lax.psum(both, "mp")], k_in, k_out, scales)

    if crossed and lax.axis_size("dp") == 4:
        swap = [(i, i ^ 1) for i in range(sharers)]
        for_other = jnp.einsum("ep,qp->eq", made, test_proj, preferred_element_type=jnp.float32)
        grads, for_other = lax.optimization_barrier((grads, for_other))
        held = jnp.concatenate([made, grads], axis=0)
        fetched = lax.ppermute(held, group, list(enumerate(SWAPPED_SEND)))
        direct = lax.ppermute(held, group, list(enumerate(DIRECT_SEND)))
        gathered = [held, direct, fetched, lax.ppermute(fetched, group, swap)]
        own = jnp.einsum("ep,qp->eq", grads, test_proj, preferred_element_type=jnp.float32)
        raw = [own, lax.ppermute(for_other, group, swap)]
    else:
        tests = lax.all_gather(test_proj, "sub", axis=0, tiled=True)
        raw = [jnp.einsum("ep,qp->eq", grads, tests, preferred_element_type=jnp.float32)]
        gathered = [lax.all_gather(grads, group, axis=0, tiled=True)]
    return finish(examples, flat // sharers, gathered, raw)


def solution(mesh):
    in_specs = (
        P(("groups", "dp", "sub"), "mp"),
        P(("groups", "dp", "sub"), "mp"),
        P(("groups", "dp", "sub")),
        P("mp", None),
        P("mp", None),
        P(("mp", "sub"), None),
    )
    out_specs = (P(("groups", "dp", "sub"), None), P(("groups", "dp", "sub"), "mp"))
    return jax.shard_map(
        per_device, mesh=mesh, in_specs=in_specs, out_specs=out_specs, check_vma=False
    )
```

```python
import functools

import jax
import jax.numpy as jnp
from jax import lax
from jax.experimental import pallas as pl
from jax.experimental.pallas import tpu as pltpu
from jax.sharding import PartitionSpec as P

SEQ = 64
DEPTHS = (3072, 2048, 1536, 1024, 512, 256, 128)
SWAPPED_SEND = (3, 5, 4, 7, 6, 0, 2, 1)
DIRECT_SEND = (7, 6, 0, 1, 2, 3, 5, 4)
CONTRACT_LAST = (((1,), (1,)), ((), ()))
CONTRACT_FIRST = (((0,), (0,)), ((), ()))


def first_chunk(width):
    small = width // 7
    return small if width % 7 == 0 and small % 128 == 0 else 0


def tree_sum(terms):
    while len(terms) > 1:
        terms = [a + b for a, b in zip(terms[::2], terms[1::2])] + terms[len(terms) // 2 * 2:]
    return terms[0]


def project_kernel(scales, hidden, out_grad, lengths, proj_in, proj_out, tests, out, near_tests, hid, og, pin, pout, limits, sems):
    rows, width = hidden.shape
    k_in = pin.shape[0]
    small = first_chunk(width)
    half = (width - small) // 2

    def copies_of(n):
        if isinstance(n, int) and n == 0:
            lanes = pl.ds(0, small)
        elif isinstance(n, int) and n == 1:
            return [pltpu.make_async_copy(proj_out, pout, sems.at[0, 1]), pltpu.make_async_copy(out_grad, og, sems.at[1, 1])]
        else:
            lanes = pl.ds(small + (n - 2) * half, half)
        return [
            pltpu.make_async_copy(proj_in.at[:, lanes], pin.at[:, lanes], sems.at[0, n]),
            pltpu.make_async_copy(hidden.at[:, lanes], hid.at[:, lanes], sems.at[1, n]),
        ]

    def partial(weights, data, at, size):
        depth = next(depth for depth in DEPTHS if size % depth == 0)
        terms = []
        for k in range(0, size, depth):
            lanes = pl.ds(at + k if isinstance(at, int) else pl.multiple_of(at + k, 128), depth)
            terms.append(lax.dot_general(weights[:, lanes], data[:, lanes], CONTRACT_LAST,
                                         preferred_element_type=jnp.float32))
        return tree_sum(terms)

    steps = range(0 if small else 1, 4)
    for n in steps:
        for copy in copies_of(n):
            copy.start()
    bounds = pltpu.make_async_copy(lengths, limits, sems.at[0, 4])
    bounds.start()
    fetch = pltpu.make_async_copy(tests, near_tests, sems.at[1, 4])
    fetch.start()
    total = jnp.zeros((k_in, rows), jnp.float32)
    if small:
        for copy in copies_of(0):
            copy.wait()
        total = partial(pin, hid, 0, small)
    for copy in copies_of(1):
        copy.wait()
    out[k_in:] = partial(pout, og, 0, og.shape[1]) * scales[1]

    def step(n, total):
        for copy in copies_of(n):
            copy.wait()
        return total + partial(pin, hid, small + (n - 2) * half, half)

    total = lax.fori_loop(2, 4, step, total)
    bounds.wait()
    slot = lax.broadcasted_iota(jnp.int32, (1, rows), 1)
    limit = jnp.zeros((1, rows), jnp.int32)
    for e in range(lengths.shape[0]):
        limit = jnp.where(slot >= e * SEQ, e * SEQ + limits[e], limit)
    out[:k_in] = jnp.where(slot < limit, total * scales[0], 0.0)
    fetch.wait()


def project(hidden, out_grad, lengths, proj_in, proj_out, test_proj, scales):
    rows, width = hidden.shape
    narrow = out_grad.shape[1]
    k_in, k_out = proj_in.shape[1], proj_out.shape[1]
    operands = (hidden, out_grad, lengths, proj_in.T, proj_out.T, test_proj)
    return pl.pallas_call(
        functools.partial(project_kernel, scales),
        out_shape=(
            jax.ShapeDtypeStruct((k_in + k_out, rows), jnp.float32),
            jax.ShapeDtypeStruct(test_proj.shape, test_proj.dtype),
        ),
        in_specs=[pl.BlockSpec(memory_space=pltpu.HBM)] * 6,
        out_specs=(pl.BlockSpec(memory_space=pltpu.VMEM),) * 2,
        scratch_shapes=[
            pltpu.VMEM((rows, width), jnp.bfloat16),
            pltpu.VMEM((rows, narrow), jnp.bfloat16),
            pltpu.VMEM((k_in, width), jnp.bfloat16),
            pltpu.VMEM((k_out, narrow), jnp.bfloat16),
            pltpu.SMEM(lengths.shape, jnp.int32),
            pltpu.SemaphoreType.DMA((2, 5)),
        ],
        compiler_params=pltpu.CompilerParams(vmem_limit_bytes=24 << 20),
        cost_estimate=pl.CostEstimate(
            flops=2 * rows * (width * k_in + narrow * k_out),
            bytes_accessed=2 * rows * (width + narrow) + 2 * (width * k_in + narrow * k_out),
            transcendentals=0,
        ),
    )(*(pltpu.with_memory_space_constraint(x, pltpu.HBM) for x in operands))


def halves(x):
    high = x.astype(jnp.bfloat16)
    return high, (x - high.astype(jnp.float32)).astype(jnp.bfloat16)


def grads_kernel(k_in, scales, *refs):
    *pieces, out, summed, placed = refs
    both = pieces[0][...]
    for piece in pieces[1:]:
        both = both + piece[...]
    k_out, slots = both.shape[0] - k_in, both.shape[1]
    for n in range(slots // 128):
        summed[n] = both[:k_in, n * 128:(n + 1) * 128]
    count = slots // SEQ
    across = 128 // k_out
    groups = k_in // across
    slot = lax.broadcasted_iota(jnp.int32, (1, slots), 1)
    left = []
    for first in range(across):
        act = jnp.concatenate([summed[n, pl.ds(first, groups, stride=across), :] for n in range(slots // 128)], axis=1)
        left += [jnp.where((slot >= e * SEQ) & (slot < (e + 1) * SEQ), act, 0.0) for e in range(count)]
    high, low = halves(jnp.concatenate(left, axis=0))
    left = jnp.concatenate([high, high, low], axis=1)
    high, low = (jnp.concatenate([part] * across, axis=0) for part in halves(both[k_in:]))
    right = jnp.concatenate([high, low, high], axis=1)
    product = lax.dot_general(left, right, CONTRACT_LAST, preferred_element_type=jnp.float32)
    size = count * groups
    lane = lax.broadcasted_iota(jnp.int32, (size, 128), 1)
    kept = product[:size]
    for first in range(1, across):
        kept = jnp.where(lane // k_out == first, product[first * size:(first + 1) * size], kept)
    placed[...] = kept * (1.0 / (scales[0] * scales[1]))
    for group in range(groups):
        out[:, group * 128:(group + 1) * 128] = placed[pl.ds(group, count, stride=groups), :].astype(jnp.bfloat16)


def example_grads(pieces, k_in, k_out, scales):
    vmem = pl.BlockSpec(memory_space=pltpu.VMEM)
    return pl.pallas_call(
        functools.partial(grads_kernel, k_in, scales),
        out_shape=jax.ShapeDtypeStruct((pieces[0].shape[1] // SEQ, k_in * k_out), jnp.bfloat16),
        in_specs=[vmem] * len(pieces),
        out_specs=vmem,
        scratch_shapes=[
            pltpu.VMEM((pieces[0].shape[1] // 128, k_in, 128), jnp.float32),
            pltpu.VMEM((pieces[0].shape[1] // SEQ * k_in * k_out // 128, 128), jnp.float32),
        ],
        compiler_params=pltpu.CompilerParams(vmem_limit_bytes=6 << 20),
        cost_estimate=pl.CostEstimate(flops=1 << 33, bytes_accessed=0, transcendentals=0),
    )(*pieces)


def finish_kernel(examples, n_pieces, n_raw, *refs):
    pieces, raw = refs[:n_pieces], refs[n_pieces:n_pieces + n_raw]
    cov, scores, block, row, sems = refs[n_pieces + n_raw:]
    own_rows, flat = cov.shape
    place = lax.axis_index(("dp", "sub"))
    every = jnp.concatenate([p[...] for p in pieces], axis=0)
    if own_rows % 128 == 0:
        at = pl.multiple_of(place * own_rows, own_rows)
        own = jnp.concatenate([p[:, pl.ds(at, own_rows)] for p in pieces], axis=0)
    else:
        at = pl.multiple_of((place * own_rows) // 128 * 128, 128)
        wider = jnp.concatenate([p[:, pl.ds(at, 128)] for p in pieces], axis=0)
        own = pltpu.roll(wider.astype(jnp.float32), (at - place * own_rows + 128) % 128, 1)[:, :own_rows].astype(jnp.bfloat16)
    wide = every.astype(jnp.float32)
    total = jnp.sum(jnp.sum(wide * wide, axis=0, keepdims=True), axis=1, keepdims=True)
    factor = lax.rsqrt(total * (1.0 / examples) + 1e-06)
    if n_raw == 2:
        near, far = raw[0][...] * factor, raw[1][...] * factor
        first = lax.axis_index("sub") == 0
        half = near.shape[1]
        row[:, :half] = jnp.where(first, near, far)
        row[:, half:] = jnp.where(first, far, near)
    else:
        row[...] = raw[0][...] * factor
    copies = [pltpu.make_async_copy(row, scores, sems.at[4])]
    copies[0].start()
    step = max(own_rows // 4, 8)
    for n, at in enumerate(range(0, own_rows, step)):
        part = pl.ds(at, step)
        block[part] = lax.dot_general(own[:, at:at + step], every, CONTRACT_FIRST,
                                      preferred_element_type=jnp.float32) * (1.0 / examples)
        copies.append(pltpu.make_async_copy(block.at[part], cov.at[part], sems.at[n]))
        copies[-1].start()
    for copy in copies:
        copy.wait()


def finish(examples, own_rows, pieces, raw):
    flat = pieces[0].shape[1]
    vmem = pl.BlockSpec(memory_space=pltpu.VMEM)
    hbm = pl.BlockSpec(memory_space=pltpu.HBM)
    cov = (own_rows, flat)
    scores = (raw[0].shape[0], sum(r.shape[1] for r in raw))
    return pl.pallas_call(
        functools.partial(finish_kernel, examples, len(pieces), len(raw)),
        out_shape=(jax.ShapeDtypeStruct(cov, jnp.float32), jax.ShapeDtypeStruct(scores, jnp.float32)),
        in_specs=[vmem] * (len(pieces) + len(raw)),
        out_specs=(hbm, hbm),
        scratch_shapes=[pltpu.VMEM(cov, jnp.float32), pltpu.VMEM(scores, jnp.float32), pltpu.SemaphoreType.DMA((5,))],
        compiler_params=pltpu.CompilerParams(vmem_limit_bytes=8 << 20),
    )(*pieces, *raw)


def per_device(hidden, out_grad, lengths, proj_in, proj_out, test_proj):
    k_in, k_out = proj_in.shape[1], proj_out.shape[1]
    flat = k_in * k_out
    group = ("dp", "sub")
    sharers = lax.axis_size(group)
    examples = lengths.shape[0] * sharers
    crossed = lax.axis_size("mp") == 2 and lax.axis_size("sub") == 2
    scales = (128.0, 4.0) if crossed else (1.0, 1.0)
    both, test_proj = project(hidden, out_grad, lengths, proj_in, proj_out, test_proj, scales)
    if crossed:
        sent = lax.optimization_barrier(both.astype(jnp.float16))
        far = lax.ppermute(sent, ("mp", "sub"), [(0, 3), (1, 2), (2, 1), (3, 0)])
        near = lax.ppermute(sent, "sub", [(0, 1), (1, 0)])
        made = example_grads([near.astype(jnp.float32), far.astype(jnp.float32)], k_in, k_out, scales)
        grads = lax.ppermute(made, "sub", [(0, 1), (1, 0)])
    else:
        grads = example_grads([lax.psum(both, "mp")], k_in, k_out, scales)

    if crossed and lax.axis_size("dp") == 4:
        swap = [(i, i ^ 1) for i in range(sharers)]
        for_other = jnp.einsum("ep,qp->eq", made, test_proj, preferred_element_type=jnp.float32)
        grads, for_other = lax.optimization_barrier((grads, for_other))
        held = jnp.concatenate([made, grads], axis=0)
        fetched = lax.ppermute(held, group, list(enumerate(SWAPPED_SEND)))
        direct = lax.ppermute(held, group, list(enumerate(DIRECT_SEND)))
        gathered = [held, direct, fetched, lax.ppermute(fetched, group, swap)]
        own = jnp.einsum("ep,qp->eq", grads, test_proj, preferred_element_type=jnp.float32)
        raw = [own, lax.ppermute(for_other, group, swap)]
    else:
        tests = lax.all_gather(test_proj, "sub", axis=0, tiled=True)
        raw = [jnp.einsum("ep,qp->eq", grads, tests, preferred_element_type=jnp.float32)]
        gathered = [lax.all_gather(grads, group, axis=0, tiled=True)]
    return finish(examples, flat // sharers, gathered, raw)


def solution(mesh):
    in_specs = (
        P(("groups", "dp", "sub"), "mp"),
        P(("groups", "dp", "sub"), "mp"),
        P(("groups", "dp", "sub")),
        P("mp", None),
        P("mp", None),
        P(("mp", "sub"), None),
    )
    out_specs = (P(("groups", "dp", "sub"), None), P(("groups", "dp", "sub"), "mp"))
    return jax.shard_map(
        per_device, mesh=mesh, in_specs=in_specs, out_specs=out_specs, check_vma=False
    )
```

```python
import functools

import jax
import jax.numpy as jnp
from jax import lax
from jax.experimental import pallas as pl
from jax.experimental.pallas import tpu as pltpu
from jax.sharding import PartitionSpec as P

SEQ = 64
DEPTHS = (3072, 2048, 1536, 1024, 512, 256, 128)
SWAPPED_SEND = (3, 5, 4, 7, 6, 0, 2, 1)
DIRECT_SEND = (7, 6, 0, 1, 2, 3, 5, 4)
CONTRACT_LAST = (((1,), (1,)), ((), ()))
CONTRACT_FIRST = (((0,), (0,)), ((), ()))


def first_chunk(width):
    small = width // 7
    return small if width % 7 == 0 and small % 128 == 0 else 0


def tree_sum(terms):
    while len(terms) > 1:
        terms = [a + b for a, b in zip(terms[::2], terms[1::2])] + terms[len(terms) // 2 * 2:]
    return terms[0]


def project_kernel(scales, hidden, out_grad, lengths, proj_in, proj_out, tests, out, near_tests, hid, og, pin, pout, limits, sems):
    rows, width = hidden.shape
    k_in = pin.shape[0]
    small = first_chunk(width)
    half = (width - small) // 2

    def copies_of(n):
        if isinstance(n, int) and n == 0:
            lanes = pl.ds(0, small)
        elif isinstance(n, int) and n == 1:
            return [pltpu.make_async_copy(proj_out, pout, sems.at[0, 1]), pltpu.make_async_copy(out_grad, og, sems.at[1, 1])]
        else:
            lanes = pl.ds(small + (n - 2) * half, half)
        return [
            pltpu.make_async_copy(proj_in.at[:, lanes], pin.at[:, lanes], sems.at[0, n]),
            pltpu.make_async_copy(hidden.at[:, lanes], hid.at[:, lanes], sems.at[1, n]),
        ]

    def partial(weights, data, at, size):
        depth = next(depth for depth in DEPTHS if size % depth == 0)
        terms = []
        for k in range(0, size, depth):
            lanes = pl.ds(at + k if isinstance(at, int) else pl.multiple_of(at + k, 128), depth)
            terms.append(lax.dot_general(weights[:, lanes], data[:, lanes], CONTRACT_LAST,
                                         preferred_element_type=jnp.float32))
        return tree_sum(terms)

    steps = range(0 if small else 1, 4)
    for n in steps:
        for copy in copies_of(n):
            copy.start()
    bounds = pltpu.make_async_copy(lengths, limits, sems.at[0, 4])
    bounds.start()
    fetch = pltpu.make_async_copy(tests, near_tests, sems.at[1, 4])
    fetch.start()
    total = jnp.zeros((k_in, rows), jnp.float32)
    if small:
        for copy in copies_of(0):
            copy.wait()
        total = partial(pin, hid, 0, small)
    for copy in copies_of(1):
        copy.wait()
    out[k_in:] = partial(pout, og, 0, og.shape[1]) * scales[1]

    def step(n, total):
        for copy in copies_of(n):
            copy.wait()
        return total + partial(pin, hid, small + (n - 2) * half, half)

    total = lax.fori_loop(2, 4, step, total)
    bounds.wait()
    slot = lax.broadcasted_iota(jnp.int32, (1, rows), 1)
    limit = jnp.zeros((1, rows), jnp.int32)
    for e in range(lengths.shape[0]):
        limit = jnp.where(slot >= e * SEQ, e * SEQ + limits[e], limit)
    out[:k_in] = jnp.where(slot < limit, total * scales[0], 0.0)
    fetch.wait()


def project(hidden, out_grad, lengths, proj_in, proj_out, test_proj, scales):
    rows, width = hidden.shape
    narrow = out_grad.shape[1]
    k_in, k_out = proj_in.shape[1], proj_out.shape[1]
    operands = (hidden, out_grad, lengths, proj_in.T, proj_out.T, test_proj)
    return pl.pallas_call(
        functools.partial(project_kernel, scales),
        out_shape=(
            jax.ShapeDtypeStruct((k_in + k_out, rows), jnp.float32),
            jax.ShapeDtypeStruct(test_proj.shape, test_proj.dtype),
        ),
        in_specs=[pl.BlockSpec(memory_space=pltpu.HBM)] * 6,
        out_specs=(pl.BlockSpec(memory_space=pltpu.VMEM),) * 2,
        scratch_shapes=[
            pltpu.VMEM((rows, width), jnp.bfloat16),
            pltpu.VMEM((rows, narrow), jnp.bfloat16),
            pltpu.VMEM((k_in, width), jnp.bfloat16),
            pltpu.VMEM((k_out, narrow), jnp.bfloat16),
            pltpu.SMEM(lengths.shape, jnp.int32),
            pltpu.SemaphoreType.DMA((2, 5)),
        ],
        compiler_params=pltpu.CompilerParams(vmem_limit_bytes=24 << 20),
        cost_estimate=pl.CostEstimate(
            flops=2 * rows * (width * k_in + narrow * k_out),
            bytes_accessed=2 * rows * (width + narrow) + 2 * (width * k_in + narrow * k_out),
            transcendentals=0,
        ),
    )(*(pltpu.with_memory_space_constraint(x, pltpu.HBM) for x in operands))


def halves(x):
    high = x.astype(jnp.bfloat16)
    return high, (x - high.astype(jnp.float32)).astype(jnp.bfloat16)


def grads_kernel(k_in, scales, *refs):
    *pieces, out, summed, placed = refs
    both = pieces[0][...]
    for piece in pieces[1:]:
        both = both + piece[...]
    k_out, slots = both.shape[0] - k_in, both.shape[1]
    for n in range(slots // 128):
        summed[n] = both[:k_in, n * 128:(n + 1) * 128]
    count = slots // SEQ
    across = 128 // k_out
    groups = k_in // across
    slot = lax.broadcasted_iota(jnp.int32, (1, slots), 1)
    left = []
    for first in range(across):
        act = jnp.concatenate([summed[n, pl.ds(first, groups, stride=across), :] for n in range(slots // 128)], axis=1)
        left += [jnp.where((slot >= e * SEQ) & (slot < (e + 1) * SEQ), act, 0.0) for e in range(count)]
    high, low = halves(jnp.concatenate(left, axis=0))
    left = jnp.concatenate([high, high, low], axis=1)
    high, low = (jnp.concatenate([part] * across, axis=0) for part in halves(both[k_in:]))
    right = jnp.concatenate([high, low, high], axis=1)
    product = lax.dot_general(left, right, CONTRACT_LAST, preferred_element_type=jnp.float32)
    size = count * groups
    lane = lax.broadcasted_iota(jnp.int32, (size, 128), 1)
    kept = product[:size]
    for first in range(1, across):
        kept = jnp.where(lane // k_out == first, product[first * size:(first + 1) * size], kept)
    placed[...] = kept * (1.0 / (scales[0] * scales[1]))
    for group in range(groups):
        out[:, group * 128:(group + 1) * 128] = placed[pl.ds(group, count, stride=groups), :].astype(jnp.bfloat16)


def example_grads(pieces, k_in, k_out, scales):
    vmem = pl.BlockSpec(memory_space=pltpu.VMEM)
    return pl.pallas_call(
        functools.partial(grads_kernel, k_in, scales),
        out_shape=jax.ShapeDtypeStruct((pieces[0].shape[1] // SEQ, k_in * k_out), jnp.bfloat16),
        in_specs=[vmem] * len(pieces),
        out_specs=vmem,
        scratch_shapes=[
            pltpu.VMEM((pieces[0].shape[1] // 128, k_in, 128), jnp.float32),
            pltpu.VMEM((pieces[0].shape[1] // SEQ * k_in * k_out // 128, 128), jnp.float32),
        ],
        compiler_params=pltpu.CompilerParams(vmem_limit_bytes=6 << 20),
        cost_estimate=pl.CostEstimate(flops=1 << 33, bytes_accessed=0, transcendentals=0),
    )(*pieces)


def finish_kernel(examples, n_pieces, n_raw, *refs):
    pieces, raw = refs[:n_pieces], refs[n_pieces:n_pieces + n_raw]
    cov, scores, block, row, sems = refs[n_pieces + n_raw:]
    own_rows, flat = cov.shape
    place = lax.axis_index(("dp", "sub"))
    every = jnp.concatenate([p[...] for p in pieces], axis=0)
    if own_rows % 128 == 0:
        at = pl.multiple_of(place * own_rows, own_rows)
        own = jnp.concatenate([p[:, pl.ds(at, own_rows)] for p in pieces], axis=0)
    else:
        at = pl.multiple_of((place * own_rows) // 128 * 128, 128)
        wider = jnp.concatenate([p[:, pl.ds(at, 128)] for p in pieces], axis=0)
        own = pltpu.roll(wider.astype(jnp.float32), (at - place * own_rows + 128) % 128, 1)[:, :own_rows].astype(jnp.bfloat16)
    wide = every.astype(jnp.float32)
    total = jnp.sum(jnp.sum(wide * wide, axis=0, keepdims=True), axis=1, keepdims=True)
    factor = lax.rsqrt(total * (1.0 / examples) + 1e-06)
    if n_raw == 2:
        near, far = raw[0][...] * factor, raw[1][...] * factor
        first = lax.axis_index("sub") == 0
        half = near.shape[1]
        row[:, :half] = jnp.where(first, near, far)
        row[:, half:] = jnp.where(first, far, near)
    else:
        row[...] = raw[0][...] * factor
    copies = [pltpu.make_async_copy(row, scores, sems.at[4])]
    copies[0].start()
    step = max(own_rows // 4, 8)
    for n, at in enumerate(range(0, own_rows, step)):
        part = pl.ds(at, step)
        block[part] = lax.dot_general(own[:, at:at + step], every, CONTRACT_FIRST,
                                      preferred_element_type=jnp.float32) * (1.0 / examples)
        copies.append(pltpu.make_async_copy(block.at[part], cov.at[part], sems.at[n]))
        copies[-1].start()
    for copy in copies:
        copy.wait()


def finish(examples, own_rows, pieces, raw):
    flat = pieces[0].shape[1]
    vmem = pl.BlockSpec(memory_space=pltpu.VMEM)
    hbm = pl.BlockSpec(memory_space=pltpu.HBM)
    cov = (own_rows, flat)
    scores = (raw[0].shape[0], sum(r.shape[1] for r in raw))
    return pl.pallas_call(
        functools.partial(finish_kernel, examples, len(pieces), len(raw)),
        out_shape=(jax.ShapeDtypeStruct(cov, jnp.float32), jax.ShapeDtypeStruct(scores, jnp.float32)),
        in_specs=[vmem] * (len(pieces) + len(raw)),
        out_specs=(hbm, hbm),
        scratch_shapes=[pltpu.VMEM(cov, jnp.float32), pltpu.VMEM(scores, jnp.float32), pltpu.SemaphoreType.DMA((5,))],
        compiler_params=pltpu.CompilerParams(vmem_limit_bytes=8 << 20),
    )(*pieces, *raw)


def per_device(hidden, out_grad, lengths, proj_in, proj_out, test_proj):
    k_in, k_out = proj_in.shape[1], proj_out.shape[1]
    flat = k_in * k_out
    group = ("dp", "sub")
    sharers = lax.axis_size(group)
    examples = lengths.shape[0] * sharers
    crossed = lax.axis_size("mp") == 2 and lax.axis_size("sub") == 2
    scales = (128.0, 4.0) if crossed else (1.0, 1.0)
    both, test_proj = project(hidden, out_grad, lengths, proj_in, proj_out, test_proj, scales)
    if crossed:
        sent = lax.optimization_barrier(both.astype(jnp.float16))
        far = lax.ppermute(sent, ("mp", "sub"), [(0, 3), (1, 2), (2, 1), (3, 0)])
        near = lax.ppermute(sent, "sub", [(0, 1), (1, 0)])
        made = example_grads([far.astype(jnp.float32), near.astype(jnp.float32)], k_in, k_out, scales)
        grads = lax.ppermute(made, "sub", [(0, 1), (1, 0)])
    else:
        grads = example_grads([lax.psum(both, "mp")], k_in, k_out, scales)

    if crossed and lax.axis_size("dp") == 4:
        swap = [(i, i ^ 1) for i in range(sharers)]
        for_other = jnp.einsum("ep,qp->eq", made, test_proj, preferred_element_type=jnp.float32)
        grads, for_other = lax.optimization_barrier((grads, for_other))
        held = jnp.concatenate([made, grads], axis=0)
        fetched = lax.ppermute(held, group, list(enumerate(SWAPPED_SEND)))
        direct = lax.ppermute(held, group, list(enumerate(DIRECT_SEND)))
        gathered = [held, direct, fetched, lax.ppermute(fetched, group, swap)]
        own = jnp.einsum("ep,qp->eq", grads, test_proj, preferred_element_type=jnp.float32)
        raw = [own, lax.ppermute(for_other, group, swap)]
    else:
        tests = lax.all_gather(test_proj, "sub", axis=0, tiled=True)
        raw = [jnp.einsum("ep,qp->eq", grads, tests, preferred_element_type=jnp.float32)]
        gathered = [lax.all_gather(grads, group, axis=0, tiled=True)]
    return finish(examples, flat // sharers, gathered, raw)


def solution(mesh):
    in_specs = (
        P(("groups", "dp", "sub"), "mp"),
        P(("groups", "dp", "sub"), "mp"),
        P(("groups", "dp", "sub")),
        P("mp", None),
        P("mp", None),
        P(("mp", "sub"), None),
    )
    out_specs = (P(("groups", "dp", "sub"), None), P(("groups", "dp", "sub"), "mp"))
    return jax.shard_map(
        per_device, mesh=mesh, in_specs=in_specs, out_specs=out_specs, check_vma=False
    )
```
